32 devices in a mesh: seq: 8 (over y, x, core), grp: 4 (over z).
Axes of the slice: x: 2, y: 2, z: 4, core: 2. Of those that a mesh axis runs over, the one named last changes fastest.
Arguments:
- tokens: bfloat16 [8192, 2048], P(('seq', 'grp')), may hold values from -6 to 6
- cotangent: bfloat16 [8192, 2048], P(('seq', 'grp')), may hold values from -6 to 6
- lengths: int32 [8], replicated, may hold values from 1 to 7936, as said below
- pad_mask: int32 [8192], P(('seq', 'grp')), may hold values 0 or 1
- mixer_gain: bfloat16 [2048], P(('seq', 'grp')), may hold values from 0.5 to 1.5
- query_weight: bfloat16 [2048, 2048], P(('seq', 'grp')), may hold values from -0.125 to 0.125
- key_weight: bfloat16 [2048, 2048], P(('seq', 'grp')), may hold values from -0.125 to 0.125
- value_weight: bfloat16 [2048, 2048], P(('seq', 'grp')), may hold values from -0.125 to 0.125
- conv_query: bfloat16 [2048, 4], P(('seq', 'grp')), may hold values from -3 to 3
- conv_key: bfloat16 [2048, 4], P(('seq', 'grp')), may hold values from -3 to 3
- conv_value: bfloat16 [2048, 4], P(('seq', 'grp')), may hold values from -3 to 3
- beta_weight: bfloat16 [2048, 16], P(('seq', 'grp')), may hold values from -0.125 to 0.125
- beta_bias: float32 [16], replicated, may hold values from -9 to 1
- head_gain: float32 [128], replicated, may hold values from 0.5 to 1.5
- out_weight: bfloat16 [2048, 2048], P(('seq', 'grp')), may hold values from -0.125 to 0.125
- feed_gain: bfloat16 [2048], P(('seq', 'grp')), may hold values from 0.5 to 1.5
- gate_weight: bfloat16 [2048, 5632], P(('seq', 'grp')), may hold values from -0.125 to 0.125
- up_weight: bfloat16 [2048, 5632], P(('seq', 'grp')), may hold values from -0.125 to 0.125
- down_weight: bfloat16 [2048, 5632], P(('seq', 'grp')), may hold values from -0.078125 to 0.078125
Outputs:
- block_out: bfloat16 [8192, 2048], P(('seq', 'grp'))
- input_grad: bfloat16 [8192, 2048], P(('seq', 'grp'))
- mixer_gain_grad: float32 [2048], P(('seq', 'grp'))
- query_grad: float32 [2048, 2048], P(('seq', 'grp'))
- key_grad: float32 [2048, 2048], P(('seq', 'grp'))
- value_grad: float32 [2048, 2048], P(('seq', 'grp'))
- conv_query_grad: float32 [2048, 4], P(('seq', 'grp'))
- conv_key_grad: float32 [2048, 4], P(('seq', 'grp'))
- conv_value_grad: float32 [2048, 4], P(('seq', 'grp'))
- beta_weight_grad: float32 [2048, 16], P(('seq', 'grp'))
- beta_bias_grad: float32 [16], replicated
- head_gain_grad: float32 [128], replicated
- out_weight_grad: float32 [2048, 2048], P(('seq', 'grp'))
- feed_gain_grad: float32 [2048], P(('seq', 'grp'))
- gate_grad: float32 [2048, 5632], P(('seq', 'grp'))
- up_grad: float32 [2048, 5632], P(('seq', 'grp'))
- down_grad: float32 [2048, 5632], P(('seq', 'grp'))
The draws below stay inside these ranges and needn't reach their ends.
Inputs may be any that keep to these rules, and one draw needn't show every extreme that they name: The 8 documents lie end to end from position 0 and their lengths sum to 8192; exactly one document, neither the first nor the last, holds the longest length, and the others together hold 256 positions.
All inputs are finite; a program needn't handle non-finite values. No bound on the sum of `pad_mask` on one device may be relied on, other than what follows from the above.
Results may differ from the reference program's by a relative error of at most 0.012.
The reference program's roundings to bfloat16 on the way count: a program that leaves them out, or rounds other values in their place, can miss the bound.
Values may be sent and summed in bfloat16 or wider, within the bound.
A program may use at most 704 MiB of HBM per device.

```python
import jax
import jax.numpy as jnp
from jax import lax

D = 2048
H = 16
DK = 128
FF = 5632
CONV = 4
BLOCK = 64
DOCS = 8
TOK_DEV = 256
TOKENS = 8192


def draw_lengths(key, part):
    key = jax.random.fold_in(key, 11)
    cut_key, place_key = jax.random.split(key, 2)
    rest_count = DOCS - 1
    shuffled = (jax.random.permutation(cut_key, TOK_DEV - 1) + 1).astype(jnp.int32)
    cuts = jnp.sort(shuffled[:rest_count - 1]).astype(jnp.int32)
    edges = jnp.concatenate([jnp.zeros((1,), jnp.int32), cuts, jnp.full((1,), TOK_DEV, jnp.int32)])
    others = (edges[1:] - edges[:-1]).astype(jnp.int32)
    chosen = jax.random.randint(place_key, (), 1, rest_count)
    places = jnp.arange(DOCS, dtype=jnp.int32)
    source = jnp.clip(places - (places > chosen).astype(jnp.int32), 0, rest_count - 1)
    return jnp.where(places == chosen, TOKENS - TOK_DEV, others[source]).astype(jnp.int32)


def touch_ends(array, rng, low, largest):
    longest = array.shape.index(max(array.shape))
    spots = []
    for shift in (0, 1):
        where = [jax.random.randint(jax.random.fold_in(rng, axis), (), 0, length) for axis, length in enumerate(array.shape)]
        where[longest] = (where[longest] + shift) % array.shape[longest]
        spots.append(tuple(where))
    return array.at[spots[0]].set(low).at[spots[1]].set(largest)


def levels(stream_key, extent, cuts, low, top_value):
    def one(position, parts):
        heights = jax.random.uniform(jax.random.fold_in(jax.random.fold_in(stream_key, 6), position), (parts,), jnp.float32, low / len(cuts), top_value / len(cuts))
        return jnp.repeat(jnp.exp(heights), extent[position] // parts).reshape((-1,) + (1,) * (len(extent) - position - 1))

    factor_of = one(*cuts[0])
    for cut in cuts[1:]:
        factor_of = factor_of * one(*cut)
    return factor_of


def gaussian(rng, extent, scale, bound, pieces=(), kind=jnp.bfloat16):
    drawn = scale * jax.random.normal(rng, extent, jnp.float32)
    if pieces:
        drawn = drawn * levels(rng, extent, pieces, -0.22, 0.18)
    return jnp.clip(drawn, -bound, bound).astype(kind)


def setup_inputs(seed: int = 0) -> dict:
    streams_of = jax.random.split(jax.random.key(seed), 20)
    return {
        "tokens": gaussian(streams_of[0], (TOKENS, D), 1.0, 6.0, ((0, 32),)),
        "cotangent": gaussian(streams_of[1], (TOKENS, D), 1.0, 6.0, ((0, 32),)),
        "lengths": draw_lengths(jax.random.fold_in(streams_of[19], 71), 0),
        "pad_mask": touch_ends((jax.random.randint(streams_of[3], (TOKENS,), 0, 16) < 15).astype(jnp.int32), jax.random.fold_in(streams_of[3], 1), 0, 1),
        "mixer_gain": jnp.clip(1.0 + 0.1 * jax.random.normal(streams_of[4], (D,), jnp.float32), 0.5, 1.5).astype(jnp.bfloat16),
        "query_weight": gaussian(streams_of[5], (D, D), D ** -0.5, 0.125, ((0, 32),)),
        "key_weight": gaussian(streams_of[6], (D, D), D ** -0.5, 0.125, ((0, 32),)),
        "value_weight": gaussian(streams_of[7], (D, D), D ** -0.5, 0.125, ((0, 32),)),
        "conv_query": gaussian(streams_of[8], (D, CONV), CONV ** -0.5, 3.0, ((0, 32),)),
        "conv_key": gaussian(streams_of[9], (D, CONV), CONV ** -0.5, 3.0, ((0, 32),)),
        "conv_value": gaussian(streams_of[10], (D, CONV), CONV ** -0.5, 3.0, ((0, 32),)),
        "beta_weight": gaussian(streams_of[11], (D, H), D ** -0.5, 0.125, ((0, 32),)),
        "beta_bias": jnp.clip(jax.random.uniform(streams_of[12], (H,), jnp.float32, -9.0, 1.0), -9.0, 1.0),
        "head_gain": jnp.clip(1.0 + 0.1 * jax.random.normal(streams_of[13], (DK,), jnp.float32), 0.5, 1.5),
        "out_weight": gaussian(streams_of[14], (D, D), D ** -0.5, 0.125, ((0, 32),)),
        "feed_gain": jnp.clip(1.0 + 0.1 * jax.random.normal(streams_of[15], (D,), jnp.float32), 0.5, 1.5).astype(jnp.bfloat16),
        "gate_weight": gaussian(streams_of[16], (D, FF), D ** -0.5, 0.125, ((0, 32),)),
        "up_weight": gaussian(streams_of[17], (D, FF), D ** -0.5, 0.125, ((0, 32),)),
        "down_weight": gaussian(streams_of[18], (D, FF), FF ** -0.5, 0.078125, ((0, 32),)),
    }


HIGH = lax.Precision.HIGHEST
EPSILON = 1e-06

@jax.custom_vjp
def low(v):
    return lax.optimization_barrier(v.astype(jnp.bfloat16)).astype(jnp.float32)

@jax.custom_vjp
def low_back(v):
    return v

def low_keep(v):
    return (low(v), None)

def low_pass(kept, grad):
    return (grad,)

def back_keep(v):
    return (v, None)

def back_low(kept, grad):
    return (low(grad),)
low.defvjp(low_keep, low_pass)
low_back.defvjp(back_keep, back_low)

def product(left, right):
    return jnp.dot(left, right, precision=HIGH, preferred_element_type=jnp.float32)

def rms_scale(values, gain):
    return values * lax.rsqrt(lax.optimization_barrier(jnp.mean(values * values, axis=-1, keepdims=True)) + EPSILON) * gain

def unit_rows(values):
    return values * lax.rsqrt(lax.optimization_barrier(jnp.sum(values * values, axis=-1, keepdims=True)) + EPSILON)

def causal_conv(hidden, kernel, valid):
    tap_count = kernel.shape[1]
    summed = hidden * kernel[:, tap_count - 1]
    for offset in range(1, tap_count):
        moved = jnp.concatenate([jnp.zeros((offset, hidden.shape[1]), jnp.float32), hidden[:-offset]], axis=0)
        summed = summed + moved * valid[offset - 1][:, None] * kernel[:, tap_count - 1 - offset]
    return jax.nn.silu(summed)

def delta_rule(queries, key_rows, value_rows, beta_rows, carry_on):
    head_count = queries.shape[1]
    head_width = queries.shape[2]

    def block_fn(memory, inputs):

        def token_fn(current, element):
            query_now, key_now, value_now, beta_now, keep_now = element
            current = current * keep_now
            recall = jnp.einsum('hd,hde->he', key_now, current, precision=HIGH)
            current = current + beta_now[:, None, None] * key_now[:, :, None] * (value_now - recall)[:, None, :]
            return (current, jnp.einsum('hd,hde->he', query_now, current, precision=HIGH))
        return lax.scan(token_fn, memory, inputs)
    inputs = tuple((stacked.reshape((stacked.shape[0] // BLOCK, BLOCK) + stacked.shape[1:]) for stacked in (queries, key_rows, value_rows, beta_rows, carry_on)))
    initial = jnp.zeros((head_count, head_width, head_width), jnp.float32)
    _, outputs = lax.scan(jax.checkpoint(block_fn), initial, inputs)
    return outputs.reshape(queries.shape)

def reference(tokens, cotangent, lengths, pad_mask, mixer_gain, query_weight, key_weight, value_weight, conv_query, conv_key, conv_value, beta_weight, beta_bias, head_gain, out_weight, feed_gain, gate_weight, up_weight, down_weight):
    token_count = tokens.shape[0]
    model_width = tokens.shape[1]
    head_count = beta_bias.shape[0]
    head_width = head_gain.shape[0]
    tap_count = conv_query.shape[1]
    places = jnp.arange(token_count, dtype=jnp.int32)
    starts = (jnp.cumsum(lengths) - lengths).astype(jnp.int32)
    row_start = lax.optimization_barrier(jnp.max(jnp.where(starts[None, :] <= places[:, None], starts[None, :], 0), axis=1)).astype(jnp.int32)
    valid = jnp.stack([(places - offset >= row_start).astype(jnp.float32) for offset in range(1, tap_count)])
    carry_on = (row_start < places).astype(jnp.float32)
    live_rows = pad_mask.astype(jnp.float32)

    def forward(inputs32, gain_mixer, w_query, w_key, w_value, c_query, c_key, c_value, w_beta, b_beta, g_head, w_out, gain_feed, w_gate, w_up, w_down):
        normed = low(rms_scale(inputs32, gain_mixer))
        query_pre = low(low_back(product(normed, w_query)))
        key_pre = low(low_back(product(normed, w_key)))
        value_pre = low(low_back(product(normed, w_value)))
        queries = unit_rows(causal_conv(query_pre, c_query, valid).reshape(token_count, head_count, head_width))
        key_rows = unit_rows(causal_conv(key_pre, c_key, valid).reshape(token_count, head_count, head_width))
        value_rows = causal_conv(value_pre, c_value, valid).reshape(token_count, head_count, head_width)
        logits = low_back(product(normed, w_beta)) + b_beta
        beta_rows = jax.nn.sigmoid(logits) * live_rows[:, None]
        mixed = delta_rule(queries, key_rows, value_rows, beta_rows, carry_on)
        head_out = low((rms_scale(mixed, g_head) * live_rows[:, None, None]).reshape(token_count, model_width))
        hidden_one = inputs32 + low_back(product(head_out, w_out))
        normed_f = low(rms_scale(hidden_one, gain_feed))
        gate = low_back(product(normed_f, w_gate))
        upper = low_back(product(normed_f, w_up))
        inner = low(jax.nn.silu(gate) * upper)
        return hidden_one + low_back(product(inner, jnp.transpose(w_down)))
    params = tuple((weight_in.astype(jnp.float32) for weight_in in (mixer_gain, query_weight, key_weight, value_weight, conv_query, conv_key, conv_value, beta_weight, beta_bias, head_gain, out_weight, feed_gain, gate_weight, up_weight, down_weight)))
    result, pullback = jax.vjp(forward, tokens.astype(jnp.float32), *params)
    grads = pullback(cotangent.astype(jnp.float32))
    return (result.astype(jnp.bfloat16), grads[0].astype(jnp.bfloat16), grads[1], grads[2], grads[3], grads[4], grads[5], grads[6], grads[7], grads[8], grads[9], grads[10], grads[11], grads[12], grads[13], grads[14], grads[15])
```

```python
import functools

import jax
import jax.numpy as jnp
from jax import lax
from jax.experimental import pallas as pl
from jax.experimental.pallas import tpu as pltpu
from jax.sharding import PartitionSpec as P

F32 = jnp.float32
LOW = jnp.bfloat16
EPSILON = 1e-06
VMEM_LIMIT = 56 * 1024 * 1024


def passed_along(value, axis, steps):
    count = lax.axis_size(axis)
    first, last = (max(0, -steps), min(count, count - steps))
    return lax.ppermute(value, axis, [(source, source + steps) for source in range(first, last)])


def rms_scale(values, gain):
    return values * lax.rsqrt(jnp.mean(values * values, axis=-1, keepdims=True) + EPSILON) * gain


def contract(left, right):
    return lax.dot_general(
        left, right, (((1,), (1,)), ((), ())), preferred_element_type=jnp.float32
    )


def split_low(value):
    upper = value.astype(LOW)
    return (upper, (value - upper.astype(F32)).astype(LOW))


def dot_one(left, right, dims=((1,), (0,))):
    return lax.dot_general(
        left.astype(LOW), right.astype(LOW), (dims, ((), ())), preferred_element_type=F32
    )


def dot_three(left, right, dims=((1,), (0,))):
    left_high, left_rest = split_low(left)
    right_high, right_rest = split_low(right)
    both = functools.partial(
        lax.dot_general, dimension_numbers=(dims, ((), ())), preferred_element_type=F32
    )
    return both(left_high, right_high) + (both(left_high, right_rest) + both(left_rest, right_high))


ROWS_ROWS = ((1,), (1,))
FIRST_FIRST = ((0,), (0,))


def inverse_unit_lower(lower, size):
    row = lax.broadcasted_iota(jnp.int32, (size, size), 0)
    column = lax.broadcasted_iota(jnp.int32, (size, size), 1)
    inverse = jnp.where(row == column, 1.0, 0.0).astype(F32)
    span = 1
    while span < size:
        joined = (row // (2 * span) == column // (2 * span)) & (row // span != column // span)
        part = jnp.where(joined, lower, 0.0)
        if span == 1:
            inverse = inverse - part
        else:
            inverse = inverse - dot_three(inverse, dot_three(part, inverse))
        span = span * 2
    return inverse


def unit(active):
    scale = lax.rsqrt(jnp.sum(active * active, axis=1, keepdims=True) + EPSILON)
    return (active * scale, scale)


def unit_back(grad, normal, scale):
    return scale * (grad - normal * jnp.sum(grad * normal, axis=1, keepdims=True))


def pick_lane(block, index):
    lane = lax.broadcasted_iota(jnp.int32, block.shape, 1)
    return jnp.sum(jnp.where(lane == index, block, 0.0), axis=1, keepdims=True)


def span_kernel(
    starts_col, starts_row, flags, betas, queries, keys, values,
    inverse_out, wy_out, scores_out, reach_out, local_out, pair_out,
):
    head = pl.program_id(0)
    count = queries.shape[0]
    width = queries.shape[1]
    row = lax.broadcasted_iota(jnp.int32, (count, count), 0)
    column = lax.broadcasted_iota(jnp.int32, (count, count), 1)
    same_doc = starts_col[...] == starts_row[...]
    first = flags[:, 0:1]
    last_part = flags[:, 1:2]
    beta = pick_lane(betas[...], head)
    query, _ = unit(queries[...])
    key, _ = unit(keys[...])
    value = values[...]
    products = dot_three(jnp.concatenate([key, query], axis=0), key, ROWS_ROWS)
    lower = jnp.where(same_doc & (row > column), beta * products[:count], 0.0)
    scores = jnp.where(same_doc & (row >= column), products[count:], 0.0)
    inverse = inverse_unit_lower(lower, count)
    wy = dot_three(inverse, jnp.concatenate([key * (beta * first), value * beta], axis=1))
    applied = dot_three(scores, wy)
    inverse_out[0] = inverse
    wy_out[0] = wy
    scores_out[0] = scores
    reach_out[...] = first * query - applied[:, :width]
    local_out[...] = applied[:, width:]
    pair = dot_three(key * last_part, wy, FIRST_FIRST)
    eye = jnp.where(
        lax.broadcasted_iota(jnp.int32, (width, width), 0)
        == lax.broadcasted_iota(jnp.int32, (width, width), 1),
        1.0,
        0.0,
    )
    change = (flags[count - 1 : count, 0:1] - 1.0) * eye - pair[:, :width]
    pair_out[0] = jnp.concatenate([change, pair[:, width:]], axis=1).astype(LOW)


def rows_specs(count, width, head_count):
    return [
        pl.BlockSpec((count, width), lambda head, part=part: (0, part * head_count + head))
        for part in range(3)
    ]


def span_call(starts, flags, betas, active, head_count):
    count, width = active.shape[0], active.shape[1] // (3 * head_count)
    rows = pl.BlockSpec((count, width), lambda head: (0, head))
    whole = lambda shape: pl.BlockSpec(shape, lambda head: (0, 0))
    square = pl.BlockSpec((1, count, count), lambda head: (head, 0, 0))
    return pl.pallas_call(
        span_kernel,
        grid=(head_count,),
        in_specs=[
            whole((count, 1)), whole((1, count)), whole(flags.shape), whole(betas.shape),
        ]
        + rows_specs(count, width, head_count),
        out_specs=[
            square,
            pl.BlockSpec((1, count, 2 * width), lambda head: (head, 0, 0)),
            square, rows, rows,
            pl.BlockSpec((1, width, 2 * width), lambda head: (head, 0, 0)),
        ],
        out_shape=[
            jax.ShapeDtypeStruct((head_count, count, count), F32),
            jax.ShapeDtypeStruct((head_count, count, 2 * width), F32),
            jax.ShapeDtypeStruct((head_count, count, count), F32),
            jax.ShapeDtypeStruct((count, head_count * width), F32),
            jax.ShapeDtypeStruct((count, head_count * width), F32),
            jax.ShapeDtypeStruct((head_count, width, 2 * width), LOW),
        ],
        compiler_params=pltpu.CompilerParams(vmem_limit_bytes=VMEM_LIMIT),
    )(starts[:, None], starts[None, :], flags, betas, active, active, active)


def mixed_kernel(reach, local, state, gain, flags, mixed_out, head_out):
    mixed = local[...] + dot_three(reach[...], state[0].astype(F32))
    mixed_out[...] = mixed
    scale = lax.rsqrt(jnp.mean(mixed * mixed, axis=1, keepdims=True) + EPSILON)
    head_out[...] = (mixed * scale * gain[...] * flags[:, 2:3]).astype(LOW)


def mixed_call(reach, local, states, gain, flags):
    head_count, width = states.shape[0], states.shape[1]
    count = reach.shape[0]
    rows = pl.BlockSpec((count, width), lambda head: (0, head))
    return pl.pallas_call(
        mixed_kernel,
        grid=(head_count,),
        in_specs=[
            rows, rows,
            pl.BlockSpec((1, width, width), lambda head: (head, 0, 0)),
            pl.BlockSpec((1, width), lambda head: (0, 0)),
            pl.BlockSpec(flags.shape, lambda head: (0, 0)),
        ],
        out_specs=[rows, rows],
        out_shape=[
            jax.ShapeDtypeStruct(reach.shape, F32),
            jax.ShapeDtypeStruct(reach.shape, LOW),
        ],
        compiler_params=pltpu.CompilerParams(vmem_limit_bytes=VMEM_LIMIT),
    )(reach, local, states, gain[None], flags)


def pull_kernel(reach, mixed_in, grads, gain, flags, change, d_mixed_out, gain_out, pair_out):
    mixed, d_head, live = mixed_in[...], grads[...], flags[:, 2:3]
    width = mixed.shape[1]
    scale = lax.rsqrt(jnp.mean(mixed * mixed, axis=1, keepdims=True) + EPSILON)
    lifted = d_head * gain[...]
    inner = jnp.mean(lifted * mixed, axis=1, keepdims=True)
    d_mixed = live * (scale * lifted - mixed * (scale * scale * scale * inner))
    d_mixed_out[...] = d_mixed
    part = jnp.sum(d_head * mixed * (scale * live), axis=0, keepdims=True)

    @pl.when(pl.program_id(0) == 0)
    def _():
        gain_out[...] = jnp.zeros_like(gain_out)

    gain_out[...] += part
    pulled = dot_three(reach[...], d_mixed, FIRST_FIRST)
    turned = jnp.transpose(change[0, :, :width].astype(F32))
    pair_out[0] = jnp.concatenate([turned, pulled], axis=1).astype(LOW)


def pull_call(reach, mixed, grads, gain, flags, pairs):
    head_count, width = pairs.shape[0], pairs.shape[1]
    count = reach.shape[0]
    rows = pl.BlockSpec((count, width), lambda head: (0, head))
    pair = pl.BlockSpec((1, width, 2 * width), lambda head: (head, 0, 0))
    return pl.pallas_call(
        pull_kernel,
        grid=(head_count,),
        in_specs=[
            rows, rows, rows,
            pl.BlockSpec((1, width), lambda head: (0, 0)),
            pl.BlockSpec(flags.shape, lambda head: (0, 0)),
            pair,
        ],
        out_specs=[rows, pl.BlockSpec((1, width), lambda head: (0, 0)), pair],
        out_shape=[
            jax.ShapeDtypeStruct(reach.shape, F32),
            jax.ShapeDtypeStruct((1, width), F32),
            jax.ShapeDtypeStruct(pairs.shape, LOW),
        ],
        compiler_params=pltpu.CompilerParams(vmem_limit_bytes=VMEM_LIMIT),
    )(reach, mixed, grads, gain[None], flags, pairs)


def back_kernel(
    starts_col, starts_row, flags, betas, queries, keys, values,
    inverse_in, wy_in, scores_in, state_in, end_in, grads,
    d_query_out, d_key_out, d_value_out, d_beta_out,
):
    head = pl.program_id(0)
    count = queries.shape[0]
    width = queries.shape[1]
    row = lax.broadcasted_iota(jnp.int32, (count, count), 0)
    column = lax.broadcasted_iota(jnp.int32, (count, count), 1)
    same_doc = starts_col[...] == starts_row[...]
    first = flags[:, 0:1]
    last_part = flags[:, 1:2]
    beta = pick_lane(betas[...], head)
    query, query_scale = unit(queries[...])
    key, key_scale = unit(keys[...])
    value, grad = values[...], grads[...]
    inverse, wy, scores = inverse_in[0], wy_in[0], scores_in[0]
    state, end = state_in[0].astype(F32), end_in[0].astype(F32)
    fresh = wy[:, width:] - dot_three(wy[:, :width], state)
    d_fresh = dot_three(scores, grad, FIRST_FIRST) + dot_three(key * last_part, end)
    pulled = dot_three(inverse, d_fresh, FIRST_FIRST)
    both = jnp.concatenate([grad, pulled], axis=0)
    through_state = dot_three(both, state, ROWS_ROWS)
    through_fresh = dot_three(both, fresh, ROWS_ROWS)
    d_scores = jnp.where(same_doc & (row >= column), through_fresh[:count], 0.0)
    d_lower = jnp.where(same_doc & (row > column), -through_fresh[count:], 0.0)
    by_keys = dot_three(jnp.concatenate([d_scores, d_lower], axis=0), key)
    d_query = first * through_state[:count] + by_keys[:count]
    d_query_out[...] = unit_back(d_query, query, query_scale)
    recalled = -through_state[count:]
    row_part = by_keys[count:]
    d_key = (
        dot_three(d_scores, query, FIRST_FIRST)
        + dot_three(d_lower, beta * key, FIRST_FIRST)
        + last_part * dot_three(fresh, end, ROWS_ROWS)
        + (beta * first) * recalled
        + beta * row_part
    )
    d_key_out[...] = unit_back(d_key, key, key_scale)
    d_value_out[...] = beta * pulled
    d_beta = jnp.sum(
        (row_part + first * recalled) * key + pulled * value, axis=1, keepdims=True
    )

    @pl.when(head == 0)
    def _():
        d_beta_out[...] = jnp.zeros_like(d_beta_out)

    lane = lax.broadcasted_iota(jnp.int32, d_beta_out.shape, 1)
    d_beta_out[...] += jnp.where(lane == head, d_beta, 0.0)


def back_call(starts, flags, betas, active, inverse, wy, scores, states, ends, grads):
    head_count, width = states.shape[0], states.shape[1]
    count = active.shape[0]
    rows = pl.BlockSpec((count, width), lambda head: (0, head))
    whole = lambda shape: pl.BlockSpec(shape, lambda head: (0, 0))
    per_head = lambda shape: pl.BlockSpec((1,) + shape, lambda head: (head, 0, 0))
    return pl.pallas_call(
        back_kernel,
        grid=(head_count,),
        in_specs=[
            whole((count, 1)), whole((1, count)), whole(flags.shape), whole(betas.shape),
            *rows_specs(count, width, head_count),
            per_head((count, count)), per_head((count, 2 * width)), per_head((count, count)),
            per_head((width, width)), per_head((width, width)),
            rows,
        ],
        out_specs=[rows, rows, rows, whole(betas.shape)],
        out_shape=[jax.ShapeDtypeStruct(grads.shape, F32)] * 3
        + [jax.ShapeDtypeStruct(betas.shape, F32)],
        compiler_params=pltpu.CompilerParams(vmem_limit_bytes=VMEM_LIMIT),
    )(
        starts[:, None], starts[None, :], flags, betas, active, active, active, inverse, wy, scores,
        states, ends, grads,
    )


def apply_pair(change, pair):
    upper, rest = split_low(pair)
    product = functools.partial(jnp.dot, preferred_element_type=F32)
    return pair + (product(change, upper) + product(change, rest))


def scan_kernel(
    backwards, group_size, seq_size, pairs, states_out,
    got, total_sent, total_got, state_sent, arrived, send_sem, recv_sem,
):
    head_count, width = pairs.shape[0], pairs.shape[1]
    share = head_count // group_size
    my_seq, my_group = lax.axis_index("seq"), lax.axis_index("grp")
    peers = [lax.rem(my_group + step, group_size) for step in range(1, group_size)]
    bits = []
    while 2 ** len(bits) < seq_size:
        bits.append(2 ** len(bits))
    upper_half = [lax.rem(my_seq // bit, 2) for bit in bits]
    partners = [my_seq + bit - 2 * bit * half for bit, half in zip(bits, upper_half)]
    barrier = pltpu.get_barrier_semaphore()
    for peer in peers:
        pl.semaphore_signal(
            barrier, inc=1, device_id=(my_seq, peer), device_id_type=pl.DeviceIdType.MESH
        )
    for partner in partners:
        pl.semaphore_signal(
            barrier, inc=1, device_id=(partner, my_group), device_id_type=pl.DeviceIdType.MESH
        )
    pl.semaphore_wait(barrier, len(peers) + len(partners))

    def send(source, target, place, device):
        copy = pltpu.make_async_remote_copy(
            src_ref=source,
            dst_ref=target,
            send_sem=send_sem.at[place],
            recv_sem=recv_sem.at[place],
            device_id=device,
            device_id_type=pl.DeviceIdType.MESH,
        )
        copy.start()
        return copy

    mine = pl.ds(my_group * share, share)
    copies = [
        send(pairs.at[pl.ds(peer * share, share)], got.at[my_group], place, (my_seq, peer))
        for place, peer in enumerate(peers)
    ]
    got[my_group] = pairs[mine]
    for copy in copies:
        copy.wait()
    members = list(range(group_size))
    if backwards:
        members = members[::-1]
    eye = jnp.where(
        lax.broadcasted_iota(jnp.int32, (width, width), 0)
        == lax.broadcasted_iota(jnp.int32, (width, width), 1),
        1.0,
        0.0,
    )
    nothing = jnp.zeros((width, width), F32)
    start = jnp.concatenate([eye, nothing], axis=1)

    def added(pair):
        return jnp.concatenate([nothing, pair[:, width:].astype(F32)], axis=1)

    totals = []
    for head in range(share):
        total = start + got[members[0], head].astype(F32)
        for member in members[1:]:
            pair = got[member, head]
            total = apply_pair(pair[:, :width], total) + added(pair)
        totals.append(total)
    before = [start for _ in range(share)]
    for level, partner in enumerate(partners):
        for head in range(share):
            total_sent[level, head] = (totals[head] - start).astype(LOW)
        copy = send(
            total_sent.at[level],
            total_got.at[level],
            group_size - 1 + level,
            (partner, my_group),
        )
        copy.wait()
        later = upper_half[level] == (0 if backwards else 1)
        for head in range(share):
            theirs = total_got[level, head].astype(F32) + start
            first_pair = jnp.where(later, theirs, totals[head])
            second_pair = jnp.where(later, totals[head], theirs)
            moved = dot_three(
                jnp.concatenate([second_pair[:, :width], before[head][:, :width]], axis=0),
                first_pair,
            )
            totals[head] = moved[:width] + added(second_pair)
            before[head] = jnp.where(later, moved[width:] + added(before[head]), before[head])
    for head in range(share):
        state = before[head][:, width:]
        for member in members:
            state_sent[member, head] = state.astype(LOW)
            if member != members[-1]:
                pair = got[member, head]
                state = apply_pair(pair[:, :width], state) + pair[:, width:].astype(F32)
    place_now = group_size - 1 + len(bits)
    copies = [
        send(state_sent.at[peer], arrived.at[mine], place_now + place, (my_seq, peer))
        for place, peer in enumerate(peers)
    ]
    arrived[mine] = state_sent[my_group]
    for copy in copies:
        copy.wait()
    states_out[...] = arrived[...]


def scan_call(pairs, backwards, collective_id):
    head_count, width = pairs.shape[0], pairs.shape[1]
    group_size, seq_size = lax.axis_size("grp"), lax.axis_size("seq")
    share = head_count // group_size
    levels = (seq_size - 1).bit_length()
    sems = 2 * (group_size - 1) + levels
    return pl.pallas_call(
        functools.partial(scan_kernel, backwards, group_size, seq_size),
        in_specs=[pl.BlockSpec(memory_space=pltpu.VMEM)],
        out_specs=pl.BlockSpec(memory_space=pltpu.VMEM),
        out_shape=jax.ShapeDtypeStruct((head_count, width, width), LOW),
        scratch_shapes=[
            pltpu.VMEM((group_size, share, width, 2 * width), LOW),
            pltpu.VMEM((levels, share, width, 2 * width), LOW),
            pltpu.VMEM((levels, share, width, 2 * width), LOW),
            pltpu.VMEM((group_size, share, width, width), LOW),
            pltpu.VMEM((head_count, width, width), LOW),
            pltpu.SemaphoreType.DMA((sems,)),
            pltpu.SemaphoreType.DMA((sems,)),
        ],
        compiler_params=pltpu.CompilerParams(
            collective_id=collective_id, has_side_effects=True, vmem_limit_bytes=VMEM_LIMIT
        ),
    )(pairs)


def seq_bits():
    count = lax.axis_size("seq")
    bits = []
    bit = 1
    while bit < count:
        bits.append(bit)
        bit = bit * 2
    return bits


def phase_orders():
    bits = seq_bits()
    return (list(reversed(bits[1:])) + bits[:1], bits[1:] + bits[:1])


def masks_of(order):
    masks = [0]
    for bit in order:
        masks = masks + [mask ^ bit for mask in masks]
    return masks


def swapped(value, bit):
    count = lax.axis_size("seq")
    return lax.ppermute(value, "seq", [(place, place ^ bit) for place in range(count)])


def gathered(rows, order):
    pieces = [rows]
    for bit in order:
        pieces = pieces + [swapped(piece, bit) for piece in pieces]
    return jnp.concatenate(pieces, axis=0)


def fetch(shard):
    block = lax.all_gather(shard, "grp", axis=0, tiled=True)
    half = block.shape[1] // 2
    first, second = phase_orders()
    return (gathered(block[:, :half], first), gathered(block[:, half:], second))


def relative(values, order):
    count = lax.axis_size("seq")
    width = values.shape[1] // count
    mine = lax.axis_index("seq")
    return jnp.concatenate(
        [
            lax.dynamic_slice_in_dim(values, (mine ^ mask) * width, width, 1)
            for mask in masks_of(order)
        ],
        axis=1,
    )


def absolute(values, order):
    count = lax.axis_size("seq")
    width = values.shape[1] // count
    mine = lax.axis_index("seq")
    masks = masks_of(order)
    where_mask = jnp.array([masks.index(mask) for mask in range(count)], jnp.int32)
    return jnp.concatenate(
        [
            lax.dynamic_slice_in_dim(values, where_mask[mine ^ place] * width, width, 1)
            for place in range(count)
        ],
        axis=1,
    )


def relative_pair(values):
    first, second = phase_orders()
    return (relative(values, first), relative(values, second))


def absolute_pair(pair):
    first, second = phase_orders()
    return absolute(pair[0], first) + absolute(pair[1], second)


def outer(matrix, grads):
    return lax.dot_general(
        matrix, grads, (((0,), (0,)), ((), ())), preferred_element_type=jnp.float32
    )


def scattered(rel_rows, grads, order):
    half = rel_rows.shape[1] // 2
    lower = outer(rel_rows[:, half:], grads).astype(jnp.bfloat16)
    arrived = swapped(lower, order[-1])
    kept = (outer(rel_rows[:, :half], grads) + arrived.astype(jnp.float32)).astype(jnp.bfloat16)
    for bit in reversed(order[:-1]):
        half = kept.shape[0] // 2
        arrived = swapped(kept[half:], bit)
        kept = (kept[:half].astype(jnp.float32) + arrived.astype(jnp.float32)).astype(jnp.bfloat16)
    return kept


def weight_grad(rel_pair, grads):
    first, second = phase_orders()
    half = grads.shape[1] // 2
    kept = jnp.concatenate(
        [
            scattered(rel_pair[0], grads[:, :half], first),
            scattered(rel_pair[1], grads[:, half:], second),
        ],
        axis=1,
    )
    return lax.psum_scatter(kept, "grp", scatter_dimension=0, tiled=True).astype(jnp.float32)


def product_pair(rel_pair, weight_pair):
    return jnp.concatenate(
        [
            jnp.dot(rows, weight, preferred_element_type=jnp.float32)
            for rows, weight in zip(rel_pair, weight_pair)
        ],
        axis=1,
    )


def contract_pair(grads, weight_pair):
    half = grads.shape[1] // 2
    return (contract(grads[:, :half], weight_pair[0]), contract(grads[:, half:], weight_pair[1]))


def local(
    tokens,
    cotangent,
    lengths,
    pad_mask,
    mixer_gain,
    query_weight,
    key_weight,
    value_weight,
    conv_query,
    conv_key,
    conv_value,
    beta_weight,
    beta_bias,
    head_gain,
    out_weight,
    feed_gain,
    gate_weight,
    up_weight,
    down_weight,
):
    row_count, model_width = tokens.shape
    head_count = beta_bias.shape[0]
    head_width = head_gain.shape[0]
    tap_count = conv_query.shape[1]
    small = lax.all_gather(
        jnp.concatenate(
            [mixer_gain[:, None], feed_gain[:, None], conv_query, conv_key, conv_value, beta_weight],
            axis=1,
        ),
        ("seq", "grp"),
        axis=0,
        tiled=True,
    )
    gain_mixer, gain_feed = small[:, 0], small[:, 1]
    c_query = small[:, 2 : 2 + tap_count]
    c_key = small[:, 2 + tap_count : 2 + 2 * tap_count]
    c_value = small[:, 2 + 2 * tap_count : 2 + 3 * tap_count]
    w_beta = small[:, 2 + 3 * tap_count :]
    w_qkv = fetch(jnp.concatenate([query_weight, key_weight, value_weight], axis=1))
    w_out = fetch(out_weight)
    w_gate = fetch(gate_weight)
    w_up = fetch(up_weight)
    w_down = fetch(down_weight)
    anchor = lax.axis_index(("seq", "grp")) * row_count
    places = anchor + jnp.arange(row_count, dtype=jnp.int32)
    starts = jnp.cumsum(lengths) - lengths
    row_start = jnp.max(jnp.where(starts[None, :] <= places[:, None], starts[None, :], 0), axis=1)
    valid = jnp.stack(
        [(places - offset >= row_start).astype(jnp.float32) for offset in range(1, tap_count)]
    )
    live_rows = pad_mask.astype(jnp.float32)
    inputs32 = tokens.astype(jnp.float32)
    normed_a, norm_a_back = jax.vjp(rms_scale, inputs32, gain_mixer.astype(jnp.float32))
    normed_low = normed_a.astype(jnp.bfloat16)
    normed_rel = relative_pair(normed_low)
    own_pre = product_pair(normed_rel, w_qkv).astype(jnp.bfloat16)
    logit_part = jnp.dot(normed_low, w_beta, preferred_element_type=jnp.float32)
    sigmoid_val = jax.nn.sigmoid(logit_part + beta_bias)
    beta_rows = sigmoid_val * live_rows[:, None]
    earlier_rows = passed_along(own_pre[row_count - (tap_count - 1) :], ("seq", "grp"), 1)
    extended = jnp.concatenate([earlier_rows, own_pre], axis=0).astype(jnp.float32)
    kernel = jnp.concatenate([c_query, c_key, c_value], axis=0).astype(jnp.float32)

    def conv_act(padded, kernel_all):
        summed = padded[tap_count - 1 :] * kernel_all[:, tap_count - 1]
        for offset in range(1, tap_count):
            moved = padded[tap_count - 1 - offset : tap_count - 1 - offset + row_count]
            summed = (
                summed + moved * valid[offset - 1][:, None] * kernel_all[:, tap_count - 1 - offset]
            )
        return jax.nn.silu(summed)

    active, conv_pull = jax.vjp(conv_act, extended, kernel)
    flags = jnp.stack(
        [
            (row_start < anchor).astype(jnp.float32),
            (row_start == row_start[-1]).astype(jnp.float32),
            live_rows,
        ],
        axis=1,
    )
    inverse, wy, scores, reach, local_out, pairs = span_call(
        row_start, flags, beta_rows, active, head_count
    )
    start_states = scan_call(pairs, False, 0)
    mixed, head_low = mixed_call(reach, local_out, start_states, head_gain, flags)
    head_rel = relative_pair(head_low)
    hidden_one = inputs32 + product_pair(head_rel, w_out)
    normed_f, norm_f_back = jax.vjp(rms_scale, hidden_one, gain_feed.astype(jnp.float32))
    feed_low = normed_f.astype(jnp.bfloat16)
    feed_rel = relative_pair(feed_low)
    gate = product_pair(feed_rel, w_gate)
    upper = product_pair(feed_rel, w_up)
    gate_sig = jax.nn.sigmoid(gate)
    gate_act = gate * gate_sig
    inner_low = (gate_act * upper).astype(jnp.bfloat16)
    block_out = (hidden_one + absolute_pair(contract_pair(inner_low, w_down))).astype(jnp.bfloat16)
    grad_out = cotangent.astype(jnp.float32)
    cotangent_rel = relative_pair(cotangent)
    d_inner = product_pair(cotangent_rel, w_down)
    d_gate = (d_inner * upper * gate_sig * (1.0 + gate * (1.0 - gate_sig))).astype(jnp.bfloat16)
    d_upper = (d_inner * gate_act).astype(jnp.bfloat16)
    d_feed = absolute_pair(
        tuple(
            one + two
            for one, two in zip(contract_pair(d_gate, w_gate), contract_pair(d_upper, w_up))
        )
    )
    down_grad = weight_grad(cotangent_rel, inner_low)
    gate_grad = weight_grad(feed_rel, d_gate)
    up_grad = weight_grad(feed_rel, d_upper)
    d_hidden_part, d_gain_feed = norm_f_back(d_feed)
    d_hidden = grad_out + d_hidden_part
    d_attn = d_hidden.astype(jnp.bfloat16)
    d_head = absolute_pair(contract_pair(d_attn, w_out))
    out_grad = weight_grad(head_rel, d_attn)
    d_mixed, d_head_gain, back_pairs = pull_call(reach, mixed, d_head, head_gain, flags, pairs)
    end_states = scan_call(back_pairs, True, 1)
    d_queries, d_keys, d_values, d_betas = back_call(
        row_start,
        flags,
        beta_rows,
        active,
        inverse,
        wy,
        scores,
        start_states,
        end_states,
        d_mixed,
    )
    d_logit32 = d_betas * live_rows[:, None] * sigmoid_val * (1.0 - sigmoid_val)
    d_logit = d_logit32.astype(jnp.bfloat16)
    d_extended, d_kernel = conv_pull(jnp.concatenate([d_queries, d_keys, d_values], axis=1))
    from_next = passed_along(
        d_extended[: tap_count - 1].astype(jnp.bfloat16), ("seq", "grp"), -1
    ).astype(jnp.float32)
    d_own = d_extended[tap_count - 1 :] + jnp.pad(
        from_next, ((row_count - (tap_count - 1), 0), (0, 0))
    )
    d_pre = d_own.astype(jnp.bfloat16)
    d_normed = absolute_pair(contract_pair(d_pre, w_qkv)) + contract(d_logit, w_beta)
    qkv_grad = weight_grad(normed_rel, d_pre)
    d_input_part, d_gain_mixer = norm_a_back(d_normed)
    input_grad = (d_hidden + d_input_part).astype(jnp.bfloat16)
    replicated = jnp.sum(
        lax.all_gather(
            jnp.concatenate([d_head_gain[0], jnp.sum(d_logit32, axis=0)])[None],
            ("seq", "grp"),
            axis=0,
            tiled=True,
        ),
        axis=0,
    )
    sharded = lax.psum_scatter(
        jnp.concatenate(
            [
                outer(normed_low, d_logit),
                d_kernel[:model_width],
                d_kernel[model_width : 2 * model_width],
                d_kernel[2 * model_width :],
                d_gain_mixer[:, None],
                d_gain_feed[:, None],
            ],
            axis=1,
        ),
        ("seq", "grp"),
        scatter_dimension=0,
        tiled=True,
    )
    taps_at = head_count + 3 * tap_count
    return (
        block_out,
        input_grad,
        sharded[:, taps_at],
        qkv_grad[:, :model_width],
        qkv_grad[:, model_width : 2 * model_width],
        qkv_grad[:, 2 * model_width :],
        sharded[:, head_count : head_count + tap_count],
        sharded[:, head_count + tap_count : head_count + 2 * tap_count],
        sharded[:, head_count + 2 * tap_count : taps_at],
        sharded[:, :head_count],
        replicated[head_width:],
        replicated[:head_width],
        out_grad,
        sharded[:, taps_at + 1],
        gate_grad,
        up_grad,
        down_grad,
    )


def solution(mesh):
    placed = (
        P(("seq", "grp"), None),
        P(("seq", "grp"), None),
        P(),
        P(("seq", "grp")),
        P(("seq", "grp")),
        P(("seq", "grp"), None),
        P(("seq", "grp"), None),
        P(("seq", "grp"), None),
        P(("seq", "grp"), None),
        P(("seq", "grp"), None),
        P(("seq", "grp"), None),
        P(("seq", "grp"), None),
        P(),
        P(),
        P(("seq", "grp"), None),
        P(("seq", "grp")),
        P(("seq", "grp"), None),
        P(("seq", "grp"), None),
        P(("seq", "grp"), None),
    )
    return jax.shard_map(
        local,
        mesh=mesh,
        in_specs=placed,
        out_specs=(
            P(("seq", "grp"), None),
            P(("seq", "grp"), None),
            P(("seq", "grp")),
            P(("seq", "grp"), None),
            P(("seq", "grp"), None),
            P(("seq", "grp"), None),
            P(("seq", "grp"), None),
            P(("seq", "grp"), None),
            P(("seq", "grp"), None),
            P(("seq", "grp"), None),
            P(),
            P(),
            P(("seq", "grp"), None),
            P(("seq", "grp")),
            P(("seq", "grp"), None),
            P(("seq", "grp"), None),
            P(("seq", "grp"), None),
        ),
        check_vma=False,
    )
```

```python
import functools

import jax
import jax.numpy as jnp
from jax import lax
from jax.experimental import pallas as pl
from jax.experimental.pallas import tpu as pltpu
from jax.sharding import PartitionSpec as P

F32 = jnp.float32
LOW = jnp.bfloat16
EPSILON = 1e-06
VMEM_LIMIT = 56 * 1024 * 1024


def passed_along(value, axis, steps):
    count = lax.axis_size(axis)
    first, last = (max(0, -steps), min(count, count - steps))
    return lax.ppermute(value, axis, [(source, source + steps) for source in range(first, last)])


def rms_scale(values, gain):
    return values * lax.rsqrt(jnp.mean(values * values, axis=-1, keepdims=True) + EPSILON) * gain


def contract(left, right):
    return lax.dot_general(
        left, right, (((1,), (1,)), ((), ())), preferred_element_type=jnp.float32
    )


def launch(kernel, after, in_specs, operands, **options):
    count = len(after)

    def body(*refs):
        kernel(*refs[count:])

    return pl.pallas_call(
        body,
        in_specs=[pl.BlockSpec(memory_space=pl.ANY)] * count + list(in_specs),
        compiler_params=pltpu.CompilerParams(vmem_limit_bytes=VMEM_LIMIT),
        **options,
    )(*after, *operands)


def estimate(flops, moved, steps=0):
    return pl.CostEstimate(flops=1, bytes_accessed=1, transcendentals=0)


def split_low(value):
    upper = value.astype(LOW)
    return (upper, (value - upper.astype(F32)).astype(LOW))


def dot_one(left, right, dims=((1,), (0,))):
    return lax.dot_general(
        left.astype(LOW), right.astype(LOW), (dims, ((), ())), preferred_element_type=F32
    )


def dot_three(left, right, dims=((1,), (0,))):
    left_high, left_rest = split_low(left)
    right_high, right_rest = split_low(right)
    both = functools.partial(
        lax.dot_general, dimension_numbers=(dims, ((), ())), preferred_element_type=F32
    )
    return both(left_high, right_high) + (both(left_high, right_rest) + both(left_rest, right_high))


ROWS_ROWS = ((1,), (1,))
FIRST_FIRST = ((0,), (0,))


def inverse_unit_lower(lower, size):
    row = lax.broadcasted_iota(jnp.int32, (size, size), 0)
    column = lax.broadcasted_iota(jnp.int32, (size, size), 1)
    inverse = jnp.where(row == column, 1.0, 0.0).astype(F32)
    span = 1
    while span < size:
        joined = (row // (2 * span) == column // (2 * span)) & (row // span != column // span)
        part = jnp.where(joined, lower, 0.0)
        if span == 1:
            inverse = inverse - part
        else:
            inverse = inverse - dot_three(inverse, dot_three(part, inverse))
        span = span * 2
    return inverse


def unit(active):
    scale = lax.rsqrt(jnp.sum(active * active, axis=1, keepdims=True) + EPSILON)
    return (active * scale, scale)


def unit_back(grad, normal, scale):
    return scale * (grad - normal * jnp.sum(grad * normal, axis=1, keepdims=True))


def pick_lane(block, index):
    lane = lax.broadcasted_iota(jnp.int32, block.shape, 1)
    return jnp.sum(jnp.where(lane == index, block, 0.0), axis=1, keepdims=True)


def span_kernel(
    starts_col, starts_row, flags, betas, queries, keys, values,
    inverse_out, wy_out, scores_out, reach_out, local_out, pair_out,
):
    head = pl.program_id(0)
    count = queries.shape[0]
    width = queries.shape[1]
    row = lax.broadcasted_iota(jnp.int32, (count, count), 0)
    column = lax.broadcasted_iota(jnp.int32, (count, count), 1)
    same_doc = starts_col[...] == starts_row[...]
    first = flags[:, 0:1]
    last_part = flags[:, 1:2]
    beta = pick_lane(betas[...], head)
    query, _ = unit(queries[...])
    key, _ = unit(keys[...])
    value = values[...]
    products = dot_three(jnp.concatenate([key, query], axis=0), key, ROWS_ROWS)
    lower = jnp.where(same_doc & (row > column), beta * products[:count], 0.0)
    scores = jnp.where(same_doc & (row >= column), products[count:], 0.0)
    inverse = inverse_unit_lower(lower, count)
    wy = dot_three(inverse, jnp.concatenate([key * (beta * first), value * beta], axis=1))
    applied = dot_three(scores, wy)
    inverse_out[0] = inverse
    wy_out[0] = wy
    scores_out[0] = scores
    reach_out[...] = first * query - applied[:, :width]
    local_out[...] = applied[:, width:]
    pair = dot_three(key * last_part, wy, FIRST_FIRST)
    eye = jnp.where(
        lax.broadcasted_iota(jnp.int32, (width, width), 0)
        == lax.broadcasted_iota(jnp.int32, (width, width), 1),
        1.0,
        0.0,
    )
    change = (flags[count - 1 : count, 0:1] - 1.0) * eye - pair[:, :width]
    pair_out[0] = jnp.concatenate([change, pair[:, width:]], axis=1).astype(LOW)


def rows_specs(count, width, head_count):
    return [
        pl.BlockSpec((count, width), lambda head, part=part: (0, part * head_count + head))
        for part in range(3)
    ]


def span_call(starts, flags, betas, active, head_count, after=()):
    count, width = active.shape[0], active.shape[1] // (3 * head_count)
    rows = pl.BlockSpec((count, width), lambda head: (0, head))
    whole = lambda shape: pl.BlockSpec(shape, lambda head: (0, 0))
    square = pl.BlockSpec((1, count, count), lambda head: (head, 0, 0))
    return launch(
        span_kernel,
        after,
        grid=(head_count,),
        in_specs=[
            whole((count, 1)), whole((1, count)), whole(flags.shape), whole(betas.shape),
        ]
        + rows_specs(count, width, head_count),
        out_specs=[
            square,
            pl.BlockSpec((1, count, 2 * width), lambda head: (head, 0, 0)),
            square, rows, rows,
            pl.BlockSpec((1, width, 2 * width), lambda head: (head, 0, 0)),
        ],
        out_shape=[
            jax.ShapeDtypeStruct((head_count, count, count), F32),
            jax.ShapeDtypeStruct((head_count, count, 2 * width), F32),
            jax.ShapeDtypeStruct((head_count, count, count), F32),
            jax.ShapeDtypeStruct((count, head_count * width), F32),
            jax.ShapeDtypeStruct((count, head_count * width), F32),
            jax.ShapeDtypeStruct((head_count, width, 2 * width), LOW),
        ],
        cost_estimate=estimate(100 * head_count * count**3, 24 * active.shape[0] * active.shape[1]),
        operands=(starts[:, None], starts[None, :], flags, betas, active, active, active,),
    )


def mixed_kernel(reach, local, state, gain, flags, mixed_out, head_out):
    mixed = local[...] + dot_three(reach[...], state[0].astype(F32))
    mixed_out[...] = mixed
    scale = lax.rsqrt(jnp.mean(mixed * mixed, axis=1, keepdims=True) + EPSILON)
    head_out[...] = (mixed * scale * gain[...] * flags[:, 2:3]).astype(LOW)


def mixed_call(reach, local, states, gain, flags, after=()):
    head_count, width = states.shape[0], states.shape[1]
    count = reach.shape[0]
    rows = pl.BlockSpec((count, width), lambda head: (0, head))
    return launch(
        mixed_kernel,
        after,
        grid=(head_count,),
        in_specs=[
            rows, rows,
            pl.BlockSpec((1, width, width), lambda head: (head, 0, 0)),
            pl.BlockSpec((1, width), lambda head: (0, 0)),
            pl.BlockSpec(flags.shape, lambda head: (0, 0)),
        ],
        out_specs=[rows, rows],
        out_shape=[
            jax.ShapeDtypeStruct(reach.shape, F32),
            jax.ShapeDtypeStruct(reach.shape, LOW),
        ],
        cost_estimate=estimate(6 * count * width * width * head_count, 14 * reach.shape[0] * reach.shape[1]),
        operands=(reach, local, states, gain[None], flags,),
    )


def pull_kernel(reach, mixed_in, grads, gain, flags, change, d_mixed_out, gain_out, pair_out):
    mixed, d_head, live = mixed_in[...], grads[...], flags[:, 2:3]
    width = mixed.shape[1]
    scale = lax.rsqrt(jnp.mean(mixed * mixed, axis=1, keepdims=True) + EPSILON)
    lifted = d_head * gain[...]
    inner = jnp.mean(lifted * mixed, axis=1, keepdims=True)
    d_mixed = live * (scale * lifted - mixed * (scale * scale * scale * inner))
    d_mixed_out[...] = d_mixed
    part = jnp.sum(d_head * mixed * (scale * live), axis=0, keepdims=True)

    @pl.when(pl.program_id(0) == 0)
    def _():
        gain_out[...] = jnp.zeros_like(gain_out)

    gain_out[...] += part
    pulled = dot_three(reach[...], d_mixed, FIRST_FIRST)
    turned = jnp.transpose(change[0, :, :width].astype(F32))
    pair_out[0] = jnp.concatenate([turned, pulled], axis=1).astype(LOW)


def pull_call(reach, mixed, grads, gain, flags, pairs, after=()):
    head_count, width = pairs.shape[0], pairs.shape[1]
    count = reach.shape[0]
    rows = pl.BlockSpec((count, width), lambda head: (0, head))
    pair = pl.BlockSpec((1, width, 2 * width), lambda head: (head, 0, 0))
    return launch(
        pull_kernel,
        after,
        grid=(head_count,),
        in_specs=[
            rows, rows, rows,
            pl.BlockSpec((1, width), lambda head: (0, 0)),
            pl.BlockSpec(flags.shape, lambda head: (0, 0)),
            pair,
        ],
        out_specs=[rows, pl.BlockSpec((1, width), lambda head: (0, 0)), pair],
        out_shape=[
            jax.ShapeDtypeStruct(reach.shape, F32),
            jax.ShapeDtypeStruct((1, width), F32),
            jax.ShapeDtypeStruct(pairs.shape, LOW),
        ],
        cost_estimate=estimate(6 * count * width * width * head_count, 20 * reach.shape[0] * reach.shape[1]),
        operands=(reach, mixed, grads, gain[None], flags, pairs,),
    )


def back_kernel(
    starts_col, starts_row, flags, betas, queries, keys, values,
    inverse_in, wy_in, scores_in, state_in, end_in, grads,
    d_query_out, d_key_out, d_value_out, d_beta_out,
):
    head = pl.program_id(0)
    count = queries.shape[0]
    width = queries.shape[1]
    row = lax.broadcasted_iota(jnp.int32, (count, count), 0)
    column = lax.broadcasted_iota(jnp.int32, (count, count), 1)
    same_doc = starts_col[...] == starts_row[...]
    first = flags[:, 0:1]
    last_part = flags[:, 1:2]
    beta = pick_lane(betas[...], head)
    query, query_scale = unit(queries[...])
    key, key_scale = unit(keys[...])
    value, grad = values[...], grads[...]
    inverse, wy, scores = inverse_in[0], wy_in[0], scores_in[0]
    state, end = state_in[0].astype(F32), end_in[0].astype(F32)
    fresh = wy[:, width:] - dot_three(wy[:, :width], state)
    d_fresh = dot_three(scores, grad, FIRST_FIRST) + dot_three(key * last_part, end)
    pulled = dot_three(inverse, d_fresh, FIRST_FIRST)
    both = jnp.concatenate([grad, pulled], axis=0)
    through_state = dot_three(both, state, ROWS_ROWS)
    through_fresh = dot_three(both, fresh, ROWS_ROWS)
    d_scores = jnp.where(same_doc & (row >= column), through_fresh[:count], 0.0)
    d_lower = jnp.where(same_doc & (row > column), -through_fresh[count:], 0.0)
    by_keys = dot_three(jnp.concatenate([d_scores, d_lower], axis=0), key)
    d_query = first * through_state[:count] + by_keys[:count]
    d_query_out[...] = unit_back(d_query, query, query_scale)
    recalled = -through_state[count:]
    row_part = by_keys[count:]
    d_key = (
        dot_three(d_scores, query, FIRST_FIRST)
        + dot_three(d_lower, beta * key, FIRST_FIRST)
        + last_part * dot_three(fresh, end, ROWS_ROWS)
        + (beta * first) * recalled
        + beta * row_part
    )
    d_key_out[...] = unit_back(d_key, key, key_scale)
    d_value_out[...] = beta * pulled
    d_beta = jnp.sum(
        (row_part + first * recalled) * key + pulled * value, axis=1, keepdims=True
    )

    @pl.when(head == 0)
    def _():
        d_beta_out[...] = jnp.zeros_like(d_beta_out)

    lane = lax.broadcasted_iota(jnp.int32, d_beta_out.shape, 1)
    d_beta_out[...] += jnp.where(lane == head, d_beta, 0.0)


def back_call(starts, flags, betas, active, inverse, wy, scores, states, ends, grads, after=()):
    head_count, width = states.shape[0], states.shape[1]
    count = active.shape[0]
    rows = pl.BlockSpec((count, width), lambda head: (0, head))
    whole = lambda shape: pl.BlockSpec(shape, lambda head: (0, 0))
    per_head = lambda shape: pl.BlockSpec((1,) + shape, lambda head: (head, 0, 0))
    return launch(
        back_kernel,
        after,
        grid=(head_count,),
        in_specs=[
            whole((count, 1)), whole((1, count)), whole(flags.shape), whole(betas.shape),
            *rows_specs(count, width, head_count),
            per_head((count, count)), per_head((count, 2 * width)), per_head((count, count)),
            per_head((width, width)), per_head((width, width)),
            rows,
        ],
        out_specs=[rows, rows, rows, whole(betas.shape)],
        out_shape=[jax.ShapeDtypeStruct(grads.shape, F32)] * 3
        + [jax.ShapeDtypeStruct(betas.shape, F32)],
        cost_estimate=estimate(36 * head_count * count**3, 40 * grads.shape[0] * grads.shape[1]),
        operands=(starts[:, None], starts[None, :], flags, betas, active, active, active, inverse, wy, scores,
        states, ends, grads,),
    )


def apply_pair(change, pair):
    upper, rest = split_low(pair)
    product = functools.partial(jnp.dot, preferred_element_type=F32)
    return pair + (product(change, upper) + product(change, rest))


def scan_kernel(
    waited, backwards, group_size, seq_size, *refs,
):
    scan_steps(backwards, group_size, seq_size, *refs[waited:])


def scan_steps(
    backwards, group_size, seq_size, pairs, states_out,
    got, total_sent, total_got, state_sent, arrived, send_sem, recv_sem,
):
    head_count, width = pairs.shape[0], pairs.shape[1]
    share = head_count // group_size
    my_seq, my_group = lax.axis_index("seq"), lax.axis_index("grp")
    peers = [lax.rem(my_group + step, group_size) for step in range(1, group_size)]
    bits = []
    while 2 ** len(bits) < seq_size:
        bits.append(2 ** len(bits))
    upper_half = [lax.rem(my_seq // bit, 2) for bit in bits]
    partners = [my_seq + bit - 2 * bit * half for bit, half in zip(bits, upper_half)]
    barrier = pltpu.get_barrier_semaphore()
    for peer in peers:
        pl.semaphore_signal(
            barrier, inc=1, device_id=(my_seq, peer), device_id_type=pl.DeviceIdType.MESH
        )
    for partner in partners:
        pl.semaphore_signal(
            barrier, inc=1, device_id=(partner, my_group), device_id_type=pl.DeviceIdType.MESH
        )
    pl.semaphore_wait(barrier, len(peers) + len(partners))

    def send(source, target, place, device):
        copy = pltpu.make_async_remote_copy(
            src_ref=source,
            dst_ref=target,
            send_sem=send_sem.at[place],
            recv_sem=recv_sem.at[place],
            device_id=device,
            device_id_type=pl.DeviceIdType.MESH,
        )
        copy.start()
        return copy

    mine = pl.ds(my_group * share, share)
    copies = [
        send(pairs.at[pl.ds(peer * share, share)], got.at[my_group], place, (my_seq, peer))
        for place, peer in enumerate(peers)
    ]
    got[my_group] = pairs[mine]
    for copy in copies:
        copy.wait()
    members = list(range(group_size))
    if backwards:
        members = members[::-1]
    eye = jnp.where(
        lax.broadcasted_iota(jnp.int32, (width, width), 0)
        == lax.broadcasted_iota(jnp.int32, (width, width), 1),
        1.0,
        0.0,
    )
    nothing = jnp.zeros((width, width), F32)
    start = jnp.concatenate([eye, nothing], axis=1)

    def added(pair):
        return jnp.concatenate([nothing, pair[:, width:].astype(F32)], axis=1)

    totals = []
    for head in range(share):
        total = start + got[members[0], head].astype(F32)
        for member in members[1:]:
            pair = got[member, head]
            total = apply_pair(pair[:, :width], total) + added(pair)
        totals.append(total)
    before = [start for _ in range(share)]
    for level, partner in enumerate(partners):
        for head in range(share):
            total_sent[level, head] = (totals[head] - start).astype(LOW)
        copy = send(
            total_sent.at[level],
            total_got.at[level],
            group_size - 1 + level,
            (partner, my_group),
        )
        copy.wait()
        later = upper_half[level] == (0 if backwards else 1)
        for head in range(share):
            theirs = total_got[level, head].astype(F32) + start
            first_pair = jnp.where(later, theirs, totals[head])
            second_pair = jnp.where(later, totals[head], theirs)
            moved = dot_three(
                jnp.concatenate([second_pair[:, :width], before[head][:, :width]], axis=0),
                first_pair,
            )
            totals[head] = moved[:width] + added(second_pair)
            before[head] = jnp.where(later, moved[width:] + added(before[head]), before[head])
    for head in range(share):
        state = before[head][:, width:]
        for member in members:
            state_sent[member, head] = state.astype(LOW)
            if member != members[-1]:
                pair = got[member, head]
                state = apply_pair(pair[:, :width], state) + pair[:, width:].astype(F32)
    place_now = group_size - 1 + len(bits)
    copies = [
        send(state_sent.at[peer], arrived.at[mine], place_now + place, (my_seq, peer))
        for place, peer in enumerate(peers)
    ]
    arrived[mine] = state_sent[my_group]
    for copy in copies:
        copy.wait()
    states_out[...] = arrived[...]


def scan_call(pairs, backwards, collective_id, after=()):
    head_count, width = pairs.shape[0], pairs.shape[1]
    group_size, seq_size = lax.axis_size("grp"), lax.axis_size("seq")
    share = head_count // group_size
    levels = (seq_size - 1).bit_length()
    sems = 2 * (group_size - 1) + levels
    return pl.pallas_call(
        functools.partial(scan_kernel, len(after), backwards, group_size, seq_size),
        in_specs=[pl.BlockSpec(memory_space=pl.ANY)] * len(after)
        + [pl.BlockSpec(memory_space=pltpu.VMEM)],
        out_specs=pl.BlockSpec(memory_space=pltpu.VMEM),
        out_shape=jax.ShapeDtypeStruct((head_count, width, width), LOW),
        cost_estimate=estimate(400 * share * width**3 * levels, 64 * pairs.size),
        scratch_shapes=[
            pltpu.VMEM((group_size, share, width, 2 * width), LOW),
            pltpu.VMEM((levels, share, width, 2 * width), LOW),
            pltpu.VMEM((levels, share, width, 2 * width), LOW),
            pltpu.VMEM((group_size, share, width, width), LOW),
            pltpu.VMEM((head_count, width, width), LOW),
            pltpu.SemaphoreType.DMA((sems,)),
            pltpu.SemaphoreType.DMA((sems,)),
        ],
        compiler_params=pltpu.CompilerParams(
            collective_id=collective_id, has_side_effects=True, vmem_limit_bytes=VMEM_LIMIT
        ),
    )(*after, pairs)


def swapped(value, bit):
    count = lax.axis_size("seq")
    return lax.ppermute(value, "seq", [(place, place ^ bit) for place in range(count)])


def chip_bits():
    count = lax.axis_size("seq")
    bits = []
    bit = 2
    while bit < count:
        bits.append(bit)
        bit = bit * 2
    return bits


def masks_of(order):
    masks = [0]
    for bit in order:
        masks = masks + [mask ^ bit for mask in masks]
    return masks


def tied(value, *others):
    return lax.optimization_barrier((value,) + others)[0]


def relative(values, masks):
    count = lax.axis_size("seq")
    width = values.shape[1] // count
    mine = lax.axis_index("seq")
    return jnp.concatenate(
        [lax.dynamic_slice_in_dim(values, (mine ^ mask) * width, width, 1) for mask in masks],
        axis=1,
    )


def absolute(values, masks):
    count = lax.axis_size("seq")
    width = values.shape[1] // count
    mine = lax.axis_index("seq")
    where_mask = jnp.array([masks.index(mask) for mask in range(count)], jnp.int32)
    return jnp.concatenate(
        [
            lax.dynamic_slice_in_dim(values, where_mask[mine ^ place] * width, width, 1)
            for place in range(count)
        ],
        axis=1,
    )


def spread_views(block, order, joined):
    views = [(block, 0)]
    for bit in order:
        if joined:
            if len(views) > 1:
                rows = block.shape[0]
                held = jnp.concatenate(
                    [array[at * rows : (at + 1) * rows] for array, at in views], axis=0
                )
            else:
                held = block
            arrived = swapped(held, bit)
            views = views + [(arrived, at) for at in range(len(views))]
        else:
            views = views + [(swapped(array, bit), at) for array, at in views]
    return views


def halved_sum(kept, bit):
    half = kept.shape[0] // 2
    arrived = swapped(kept[half:], bit)
    return (kept[:half].astype(F32) + arrived.astype(F32)).astype(LOW)


def over_groups(rows):
    return lax.psum_scatter(rows, "grp", scatter_dimension=0, tiled=True).astype(F32)


def tile_of(width, largest):
    tile = largest
    while width % tile:
        tile = tile // 2
    return tile


def join_kernel(first, second, target):
    rows = first.shape[0]
    target[:rows] = first[...]
    target[rows:] = second[...]


def join_columns(first, second, start, width, after=()):
    tile = tile_of(width, 1024)
    while start % tile:
        tile = tile // 2
    rows = first.shape[0]
    return launch(
        join_kernel,
        after,
        grid=(width // tile,),
        in_specs=[pl.BlockSpec((rows, tile), lambda step: (0, start // tile + step))] * 2,
        out_specs=pl.BlockSpec((2 * rows, tile), lambda step: (0, step)),
        out_shape=jax.ShapeDtypeStruct((2 * rows, width), first.dtype),
        cost_estimate=estimate(0, 4 * rows * width),
        operands=(first, second),
    )


def contract_kernel(grads, weights, total):
    @pl.when(pl.program_id(0) == 0)
    def _():
        total[...] = jnp.zeros_like(total)

    total[...] += lax.dot_general(
        grads[...], weights[...], (((1,), (1,)), ((), ())), preferred_element_type=F32
    )


def contract_rows(grads, weights, start, after=()):
    tokens, width = grads.shape
    tile = tile_of(width, 512)
    depth = weights.shape[0]
    first = start // tile
    return launch(
        contract_kernel,
        after,
        grid=(width // tile,),
        in_specs=[
            pl.BlockSpec((tokens, tile), lambda step: (0, step)),
            pl.BlockSpec((depth, tile), lambda step: (0, first + step)),
        ],
        out_specs=pl.BlockSpec((tokens, depth), lambda step: (0, 0)),
        out_shape=jax.ShapeDtypeStruct((tokens, depth), F32),
        cost_estimate=estimate(2 * tokens * depth * width, 2 * depth * width),
        operands=(grads, weights),
    )


def feed_kernel(count, cuts, resumed, feed, slopes, *refs):
    weights, refs = refs[: 6 * count], refs[6 * count :]
    if resumed:
        before, refs = refs[:2], refs[2:]
    grads_first, grads_second, out_total, d_total = refs
    step = pl.program_id(0)

    @pl.when(step == 0)
    def _():
        out_total[...] = before[0][...] if resumed else jnp.zeros_like(out_total)
        d_total[...] = before[1][...] if resumed else jnp.zeros_like(d_total)

    back = functools.partial(
        lax.dot_general, dimension_numbers=(((1,), (1,)), ((), ())), preferred_element_type=F32
    )

    def tile_step(pieces, grads_out):
        gate_part, up_part, down_part = [
            jnp.concatenate(
                [piece[...] for piece in pieces[kind * count : (kind + 1) * count]], axis=0
            )
            for kind in range(3)
        ]
        gate = jnp.dot(feed[...], gate_part, preferred_element_type=F32)
        upper = jnp.dot(feed[...], up_part, preferred_element_type=F32)
        d_inner = jnp.dot(slopes[...], down_part, preferred_element_type=F32)
        gate_sig = 1.0 / (1.0 + jnp.exp(-gate))
        gate_act = gate * gate_sig
        inner = (gate_act * upper).astype(LOW)
        d_gate = (d_inner * upper * gate_sig * (1.0 + gate * (1.0 - gate_sig))).astype(LOW)
        d_upper = (d_inner * gate_act).astype(LOW)
        grads_out[0] = d_gate
        grads_out[1] = d_upper
        grads_out[2] = inner
        out_total[...] += back(inner, down_part)
        d_total[...] += back(d_gate, gate_part) + back(d_upper, up_part)

    @pl.when(step < cuts[0])
    def _():
        tile_step(weights[: 3 * count], grads_first)

    @pl.when(step >= cuts[0])
    def _():
        tile_step(weights[3 * count :], grads_second)


def feed_call(feed, slopes, piece_lists, before, tile, after=()):
    tokens, depth = feed.shape
    cuts = [pieces[0][0].shape[1] // (3 * tile) for pieces in piece_lists]
    block_rows = depth // len(piece_lists[0])
    count = len(piece_lists[0])
    first = lambda step: jnp.minimum(step, cuts[0] - 1)
    second = lambda step: jnp.maximum(step - cuts[0], 0)
    whole = pl.BlockSpec((tokens, depth), lambda step: (0, 0))
    weights = [
        pl.BlockSpec(
            (block_rows, tile),
            lambda step, at=at, kind=kind, where=where, cut=cut: (at, kind * cut + where(step)),
        )
        for pieces, where, cut in zip(piece_lists, (first, second), cuts)
        for kind in range(3)
        for _, at in pieces
    ]
    width = (cuts[0] + cuts[1]) * tile
    return launch(
        functools.partial(feed_kernel, count, cuts, before is not None),
        after,
        grid=(cuts[0] + cuts[1],),
        in_specs=[whole, whole] + weights + ([whole, whole] if before is not None else []),
        out_specs=[
            pl.BlockSpec((3, tokens, tile), lambda step: (0, 0, first(step))),
            pl.BlockSpec((3, tokens, tile), lambda step: (0, 0, second(step))),
            whole,
            whole,
        ],
        out_shape=[
            jax.ShapeDtypeStruct((3, tokens, cuts[0] * tile), LOW),
            jax.ShapeDtypeStruct((3, tokens, cuts[1] * tile), LOW),
            jax.ShapeDtypeStruct((tokens, depth), F32),
            jax.ShapeDtypeStruct((tokens, depth), F32),
        ],
        cost_estimate=estimate(
            12 * tokens * depth * width, 6 * depth * width, 3 * tokens * width
        ),
        operands=(
            feed, slopes,
            *([array for array, _ in piece_lists[0]] * 3),
            *([array for array, _ in piece_lists[1]] * 3),
            *(before if before is not None else ()),
        ),
    )


def outer_kernel(count, kinds, starts, first_kind, *refs):
    sources = (refs[:count], refs[count : 2 * count])
    grads, arrived, out = refs[2 * count], refs[2 * count + 1 : -1], refs[-1]
    kind = pl.program_id(0) + first_kind
    depth = out.shape[0] // count

    def fill(source, added):
        for place in range(count):
            rows = slice(place * depth, (place + 1) * depth)
            total = lax.dot_general(
                source[place][...], grads[0], (((0,), (0,)), ((), ())),
                preferred_element_type=F32,
            )
            if added is not None:
                total = total + added[rows].astype(F32)
            out[rows] = total.astype(LOW)

    for which in range(2):
        wanted = (kind == kinds - 1) if which else (kind < kinds - 1)
        if not arrived:
            pl.when(wanted)(functools.partial(fill, sources[which], None))
        for place, added in enumerate(arrived):
            inside = kind >= starts[place]
            if place + 1 < len(arrived):
                inside = inside & (kind < starts[place + 1])
            pl.when(wanted & inside)(functools.partial(fill, sources[which], added))


def outer_call(sources, grads, places, span=None, arrived=(), starts=(0,), after=()):
    tokens, model = sources[0].shape
    kinds, _, width = grads.shape
    blocks = 2 * len(places)
    depth = model // blocks
    half = model // 2
    first_kind, stop = span or (0, kinds)
    last = stop - first_kind

    def own(place):
        return pl.BlockSpec((tokens, depth), lambda kind: (0, place))

    def added(array, start):
        most = array.shape[1] // width - 1
        return pl.BlockSpec(
            (half, width), lambda kind: (0, jnp.clip(kind + first_kind - start, 0, most))
        )

    return launch(
        functools.partial(outer_kernel, len(places), kinds, starts, first_kind),
        after,
        grid=(last,),
        in_specs=[own(place) for place in places] * 2
        + [pl.BlockSpec((1, tokens, width), lambda kind: (first_kind + kind, 0, 0))]
        + [added(array, start) for array, start in zip(arrived, starts)],
        out_specs=pl.BlockSpec((half, width), lambda kind: (0, kind)),
        out_shape=jax.ShapeDtypeStruct((half, last * width), LOW),
        cost_estimate=estimate(1, 1),
        operands=(
            *([sources[0]] * len(places)), *([sources[1]] * len(places)), grads, *arrived,
        ),
    )


def gather_kernel(
    group_size, bits, orders, cuts, feed_cuts, shard, feed, full, pair_first, pair_second, rest,
    own_sem, line_send, line_recv, tree_send, tree_recv, feed_send, feed_recv, core_send, core_recv,
):
    my_seq, my_group = lax.axis_index("seq"), lax.axis_index("grp")
    rows = shard.shape[0]
    levels = len(orders[0])

    def flipped(mask):
        place = my_seq
        for bit in bits:
            if mask & bit:
                place = place + bit - 2 * bit * lax.rem(my_seq // bit, 2)
        return place

    def remote(source, target, send_sem, recv_sem, device):
        return pltpu.make_async_remote_copy(
            src_ref=source, dst_ref=target, send_sem=send_sem, recv_sem=recv_sem,
            device_id=device, device_id_type=pl.DeviceIdType.MESH,
        )

    def greet(device):
        pl.semaphore_signal(
            barrier, inc=1, device_id=device, device_id_type=pl.DeviceIdType.MESH
        )

    def has(direction, steps):
        return my_group >= steps if direction == 0 else my_group + steps < group_size

    def beside(direction, steps):
        return my_group - steps if direction == 0 else my_group + steps

    barrier = pltpu.get_barrier_semaphore()
    for bit in bits:
        greet((flipped(bit), my_group))
    for direction in range(2):

        @pl.when(has(direction, 1))
        def _():
            greet((my_seq, beside(direction, 1)))

    pl.semaphore_wait(
        barrier,
        len(bits) + jnp.minimum(my_group, 1) + jnp.minimum(group_size - 1 - my_group, 1),
    )

    def place_of(mask, group):
        return pl.ds(pl.multiple_of((flipped(mask) * group_size + group) * rows, rows), rows)

    def line_copies(kind, direction, hop):
        origin = beside(direction, hop - 1)
        device = (my_seq, beside(1 - direction, 1))
        if kind == 0:
            views = [(shard if hop == 1 else full.at[place_of(0, origin)], full.at[place_of(0, origin)])]
            sems = (line_send, line_recv)
        else:
            spot = pl.ds(pl.multiple_of(origin * rows, rows), rows)
            parts = (pair_first, pair_second, rest)
            views = [
                (
                    feed.at[:, cut] if hop == 1 else part.at[spot],
                    part.at[spot],
                )
                for part, cut in zip(parts, feed_cuts)
            ]
            sems = (feed_send, feed_recv)
        return [
            remote(source, target, sems[0].at[direction, hop - 1, at], sems[1].at[direction, hop - 1, at], device)
            for at, (source, target) in enumerate(views)
        ]

    def line_send_now(kind, direction, hop):
        @pl.when(has(1 - direction, 1))
        def _():
            for copy in line_copies(kind, direction, hop):
                copy.start()

    def line_wait(kind, direction, hop):
        for copy in line_copies(kind, direction, hop):
            copy.wait_recv()

    def line_drain(kind):
        for direction in range(2):
            for hop in range(1, group_size):

                @pl.when(has(direction, hop - 1) & has(1 - direction, 1))
                def _():
                    for copy in line_copies(kind, direction, hop):
                        copy.wait_send()

    slots = [(0, 0)] + [(direction, hop) for hop in range(1, group_size) for direction in range(2)]

    def node_copy(slot, part, level, mask):
        direction, hop = slots[slot]
        origin = beside(direction, hop) if hop else my_group
        view = full.at[place_of(mask, origin), cuts[part]]
        source = shard.at[:, cuts[part]] if hop == 0 and mask == 0 else view
        node = 2**level - 1 + masks_of(orders[part][:level]).index(mask)
        return remote(
            source, view, tree_send.at[slot, part, node], tree_recv.at[slot, part, node],
            (flipped(orders[part][level]), my_group),
        )

    def stage(slot, lag):
        direction, hop = slots[slot]
        if lag == 0:
            if hop:
                line_wait(0, direction, hop)
                if hop + 1 < group_size:
                    line_send_now(0, direction, hop + 1)
            for part in range(2):
                for level in range(levels):
                    node_copy(slot, part, level, 0).start()
        else:
            level = lag - 1
            for part in range(2):
                for mask in masks_of(orders[part][:level]):
                    node_copy(slot, part, level, mask).wait_recv()
                    for later in range(level + 1, levels):
                        node_copy(slot, part, later, mask ^ orders[part][level]).start()

    def when_held(slot, work):
        direction, hop = slots[slot]
        if hop == 0:
            work()
        else:
            pl.when(has(direction, hop))(work)

    own = pltpu.make_async_copy(shard, full.at[place_of(0, my_group)], own_sem.at[0])
    own.start()
    spot = pl.ds(pl.multiple_of(my_group * rows, rows), rows)
    own_feed = [
        pltpu.make_async_copy(feed.at[:, cut], part.at[spot], own_sem.at[1 + at])
        for at, (part, cut) in enumerate(zip((pair_first, pair_second, rest), feed_cuts))
    ]
    for copy in own_feed:
        copy.start()
    for direction in range(2):
        line_send_now(0, direction, 1)
    def feed_hop(hop):
        for direction in range(2):

            @pl.when(has(direction, hop))
            def _():
                line_wait(1, direction, hop)
                if hop + 1 < group_size:
                    line_send_now(1, direction, hop + 1)

    def at_lag(slot, lag):
        when_held(slot, functools.partial(stage, slot, lag))

    at_lag(0, 0)
    for hop in range(1, group_size):
        at_lag(2 * hop - 1, 0)
        at_lag(2 * hop, 0)
        if hop == group_size - 2:
            for direction in range(2):
                line_send_now(1, direction, 1)
        for slot in [0] if hop == 1 else [2 * hop - 3, 2 * hop - 2]:
            at_lag(slot, 1)
    for slot in range(max(2 * group_size - 3, 0), len(slots)):
        at_lag(slot, 1)
    hop_now = 1
    for lag in range(2, levels):
        for slot in range(len(slots)):
            if slot % 3 == 0 and hop_now < group_size:
                feed_hop(hop_now)
                hop_now = hop_now + 1
            at_lag(slot, lag)
    for hop in range(hop_now, group_size):
        feed_hop(hop)
    line_drain(1)
    for copy in own_feed:
        copy.wait()
    half = rest.shape[0]
    first_width = pair_first.shape[1]
    swaps = [
        remote(
            rest.at[:, cut], part.at[pl.ds(half, half)], core_send.at[at], core_recv.at[at],
            (flipped(1), my_group),
        )
        for at, (part, cut) in enumerate(
            (
                (pair_first, pl.ds(0, first_width)),
                (pair_second, pl.ds(first_width, pair_second.shape[1])),
            )
        )
    ]
    for copy in swaps:
        copy.start()
    for slot in range(len(slots)):
        when_held(slot, functools.partial(stage, slot, levels))
    for copy in swaps:
        copy.wait()
    own.wait()
    line_drain(0)

    def drain(slot):
        for part in range(2):
            for level in range(levels):
                for mask in masks_of(orders[part][:level]):
                    node_copy(slot, part, level, mask).wait_send()

    for slot in range(len(slots)):
        when_held(slot, functools.partial(drain, slot))


def gather_call(shard, feed, cuts, feed_cuts, orders, collective_id):
    group_size, seq_size = lax.axis_size("grp"), lax.axis_size("seq")
    rows, width = shard.shape
    bits = [1] + chip_bits()
    nodes = 2 ** len(bits) - 1
    slots = 2 * group_size - 1
    first_width, second_width = feed_cuts[0].size, feed_cuts[1].size
    any_space = pl.BlockSpec(memory_space=pl.ANY)
    dma = pltpu.SemaphoreType.DMA
    return pl.pallas_call(
        functools.partial(gather_kernel, group_size, bits, orders, cuts, feed_cuts),
        in_specs=[any_space] * 2,
        out_specs=[any_space] * 4,
        out_shape=[
            jax.ShapeDtypeStruct((rows * group_size * seq_size, width), LOW),
            jax.ShapeDtypeStruct((2 * rows * group_size, first_width), LOW),
            jax.ShapeDtypeStruct((2 * rows * group_size, second_width), LOW),
            jax.ShapeDtypeStruct((rows * group_size, first_width + second_width), LOW),
        ],
        scratch_shapes=[
            dma((4,)),
            dma((2, group_size - 1, 1)), dma((2, group_size - 1, 1)),
            dma((slots, 2, nodes)), dma((slots, 2, nodes)),
            dma((2, group_size - 1, 3)), dma((2, group_size - 1, 3)),
            dma((2,)), dma((2,)),
        ],
        cost_estimate=estimate(1.5e11, 1e8),
        compiler_params=pltpu.CompilerParams(collective_id=collective_id, has_side_effects=True),
    )(shard, feed)


def reduce_kernel(waited, group_size, orders, groups, *refs):
    refs = refs[waited:]
    sets = len(groups)
    inputs, refs = refs[: 4 * sets + 1], refs[4 * sets + 1 :]
    totals, everywhere, refs = refs[:sets], refs[sets], refs[sets + 1 :]
    buffers, refs = refs[: 5 * sets], refs[5 * sets :]
    vector_out, vector_in = refs[:2]
    send_sem, recv_sem, core_send, core_recv, line_send, line_recv, v_send, v_recv = refs[2:]
    my_seq, my_group = lax.axis_index("seq"), lax.axis_index("grp")
    levels = len(orders[0])
    peers = [lax.rem(my_group + step, group_size) for step in range(1, group_size)]
    bits = [1] + list(orders[1])
    units = [(place, group) for place in range(sets) for group in range(groups[place])]
    lower_rows = inputs[0].shape[0]
    final = lower_rows // 2 ** (levels - 1)
    half = final // 2
    rows = half // group_size

    def partner(bit):
        return my_seq + bit - 2 * bit * lax.rem(my_seq // bit, 2)

    def greet(device):
        pl.semaphore_signal(
            barrier, inc=1, device_id=device, device_id_type=pl.DeviceIdType.MESH
        )

    barrier = pltpu.get_barrier_semaphore()
    for bit in bits:
        greet((partner(bit), my_group))
    for peer in peers:
        greet((my_seq, peer))
    pl.semaphore_wait(barrier, len(bits) + len(peers))

    def remote(source, target, send, recv, device):
        return pltpu.make_async_remote_copy(
            src_ref=source, dst_ref=target, send_sem=send, recv_sem=recv,
            device_id=device, device_id_type=pl.DeviceIdType.MESH,
        )

    def held(level):
        return lower_rows // 2**level

    def begins(level):
        return sum(held(before) for before in range(level))

    def parts_of(unit):
        place, group = units[unit]
        return inputs[4 * place : 4 * place + 4], buffers[5 * place : 5 * place + 5], group

    def chip_copy(unit, part, level):
        given, (arrived, leaving, _, _, _), group = parts_of(unit)
        width = arrived.shape[-1]
        count = held(level)
        if level == 0:
            source = given[part].at[:, pl.ds(group * width, width)]
        else:
            source = leaving.at[part, group, pl.ds(begins(level) - held(0), count)]
        return remote(
            source,
            arrived.at[part, group, pl.ds(begins(level), count)],
            send_sem.at[unit, part, level],
            recv_sem.at[unit, part, level],
            (partner(orders[part][levels - 1 - level]), my_group),
        )

    def core_copy(unit):
        _, (_, _, chip_total, core_in, _), group = parts_of(unit)
        return remote(
            chip_total.at[group, pl.ds(half, half)],
            core_in.at[group],
            core_send.at[unit],
            core_recv.at[unit],
            (partner(1), my_group),
        )

    def line_copies(unit):
        _, (_, _, chip_total, core_in, line_in), group = parts_of(unit)
        copies = []
        for at, peer in enumerate(peers):
            spot = pl.ds(pl.multiple_of(peer * rows, rows), rows)
            for side, source in enumerate((chip_total.at[group, spot], core_in.at[group, spot])):
                copies.append(
                    remote(
                        source,
                        line_in.at[group, at, side],
                        line_send.at[unit, at, side],
                        line_recv.at[unit, at, side],
                        (my_seq, peer),
                    )
                )
        return copies

    def stage(unit, lag):
        given, (arrived, leaving, chip_total, core_in, line_in), group = parts_of(unit)
        width = arrived.shape[-1]
        if lag == 0:
            for part in range(2):
                chip_copy(unit, part, 0).start()
        elif lag <= levels:
            level = lag - 1
            for part in range(2):
                chip_copy(unit, part, level).wait_recv()
                count = held(level)

                def added(low, high):
                    base = begins(level)
                    value = arrived[part, group, base + low : base + high].astype(F32)
                    if level == 0:
                        kept = given[2 + part][low:high, group * width : (group + 1) * width]
                    else:
                        before = begins(level - 1)
                        kept = arrived[part, group, before + low : before + high]
                    return value + kept.astype(F32)

                if lag < levels:
                    middle = count // 2
                    spot = begins(level + 1) - held(0)
                    leaving[part, group, spot : spot + middle] = added(middle, count).astype(LOW)
                    chip_copy(unit, part, level + 1).start()
                    base = begins(level)
                    arrived[part, group, base : base + middle] = added(0, middle).astype(LOW)
                else:
                    chip_total[group, :, part * width : (part + 1) * width] = added(
                        0, count
                    ).astype(LOW)
            if lag == levels:
                core_copy(unit).start()
        elif lag == levels + 1:
            core_copy(unit).wait_recv()
            for copy in line_copies(unit):
                copy.start()
        else:
            own = pl.ds(pl.multiple_of(my_group * rows, rows), rows)
            for copy in line_copies(unit):
                copy.wait_recv()
            total = totals[units[unit][0]]
            for side, source in enumerate((chip_total, core_in)):
                value = source[group, own].astype(F32)
                for at in range(len(peers)):
                    value = value + line_in[group, at, side].astype(F32)
                spot = (group * 2 + side) * 2 * width
                total[:, spot : spot + 2 * width] = value

    def vector_copies(step):
        if step < len(bits):
            return [
                remote(
                    vector_out.at[step], vector_in.at[step], v_send.at[step], v_recv.at[step],
                    (partner(bits[step]), my_group),
                )
            ]
        return [
            remote(
                vector_out.at[step], vector_in.at[step + at], v_send.at[step + at],
                v_recv.at[step + at], (my_seq, peer),
            )
            for at, peer in enumerate(peers)
        ]

    def vector_step(step):
        if step:
            for copy in vector_copies(step - 1):
                copy.wait_recv()
        if step == 0:
            vector_out[0] = inputs[-1][...]
        elif step <= len(bits):
            vector_out[step] = vector_out[step - 1] + vector_in[step - 1]
        else:
            value = vector_out[len(bits)]
            for at in range(len(peers)):
                value = value + vector_in[len(bits) + at]
            everywhere[...] = value
        if step <= len(bits):
            for copy in vector_copies(step):
                copy.start()

    last_step = len(units) + levels + 2
    for step in range(last_step):
        for lag in range(levels + 3):
            if 0 <= step - lag < len(units):
                stage(step - lag, lag)
        if step <= len(bits) + 1:
            vector_step(step)
    for step in range(last_step, len(bits) + 2):
        vector_step(step)
    for step in range(len(bits) + 1):
        for copy in vector_copies(step):
            copy.wait_send()
    for unit in range(len(units)):
        for part in range(2):
            for level in range(levels):
                chip_copy(unit, part, level).wait_send()
        core_copy(unit).wait_send()
        for copy in line_copies(unit):
            copy.wait_send()


def reduce_call(sets, vector, orders, collective_id, after=()):
    group_size = lax.axis_size("grp")
    depth = sets[0][0][0].shape[0]
    levels = len(orders[0])
    final = depth // 2 ** (levels - 1)
    half = final // 2
    rows = half // group_size
    held_all = sum(depth // 2**level for level in range(levels))
    groups = [group for _, _, group in sets]
    units = sum(groups)
    bits = levels + 1
    in_vmem = pl.BlockSpec(memory_space=pltpu.VMEM)
    in_any = pl.BlockSpec(memory_space=pl.ANY)
    dma = pltpu.SemaphoreType.DMA
    widths = [lowers[0].shape[1] // group for lowers, _, group in sets]
    scratch = []
    for group, width in zip(groups, widths):
        scratch += [
            pltpu.VMEM((2, group, held_all, width), LOW),
            pltpu.VMEM((2, group, max(held_all - depth, 16), width), LOW),
            pltpu.VMEM((group, final, 2 * width), LOW),
            pltpu.VMEM((group, half, 2 * width), LOW),
            pltpu.VMEM((group, max(group_size - 1, 1), 2, rows, 2 * width), LOW),
        ]
    operands = []
    for lowers, uppers, _ in sets:
        operands += [*lowers, *uppers]
    return pl.pallas_call(
        functools.partial(reduce_kernel, len(after), group_size, orders, groups),
        in_specs=[in_any] * len(after) + [in_any, in_any, in_vmem, in_vmem] * len(sets) + [in_vmem],
        out_specs=[in_vmem] * (len(sets) + 1),
        out_shape=[
            jax.ShapeDtypeStruct((rows, group * 4 * width), F32)
            for group, width in zip(groups, widths)
        ]
        + [jax.ShapeDtypeStruct(vector.shape, F32)],
        scratch_shapes=scratch
        + [
            pltpu.VMEM((bits + 1,) + vector.shape, F32),
            pltpu.VMEM((bits + group_size,) + vector.shape, F32),
            dma((units, 2, levels)), dma((units, 2, levels)),
            dma((units,)), dma((units,)),
            dma((units, group_size, 2)), dma((units, group_size, 2)),
            dma((bits + group_size,)), dma((bits + group_size,)),
        ],
        cost_estimate=estimate(1, 1),
        compiler_params=pltpu.CompilerParams(
            collective_id=collective_id, has_side_effects=True, vmem_limit_bytes=VMEM_LIMIT
        ),
    )(*after, *operands, vector)


def local(
    tokens,
    cotangent,
    lengths,
    pad_mask,
    mixer_gain,
    query_weight,
    key_weight,
    value_weight,
    conv_query,
    conv_key,
    conv_value,
    beta_weight,
    beta_bias,
    head_gain,
    out_weight,
    feed_gain,
    gate_weight,
    up_weight,
    down_weight,
):
    row_count, model_width = tokens.shape
    head_count = beta_bias.shape[0]
    head_width = head_gain.shape[0]
    tap_count = conv_query.shape[1]
    hidden_units = gate_weight.shape[1]
    my_core = lax.rem(lax.axis_index("seq"), 2)
    chip = chip_bits()
    chip_orders = (list(reversed(chip)), list(chip))
    plain_orders = [order + [1] for order in chip_orders]
    plain_masks = [masks_of(order) for order in plain_orders]
    pair_masks = [masks_of([1] + order) for order in chip_orders]

    def along_groups(shard):
        return lax.all_gather(shard, "grp", axis=0, tiled=True)

    small_shard = jnp.concatenate(
        [mixer_gain[:, None], feed_gain[:, None], conv_query, conv_key, conv_value, beta_weight],
        axis=1,
    )
    small_width = small_shard.shape[1]
    padded_small = jnp.pad(small_shard, ((0, 0), (0, -small_width % 128)))
    plain_shard = jnp.concatenate(
        [query_weight, key_weight, value_weight, out_weight, padded_small], axis=1
    )
    plain_cut = 2 * model_width
    plain_cuts = (pl.ds(0, plain_cut), pl.ds(plain_cut, plain_shard.shape[1] - plain_cut))
    unit_width = hidden_units // 2
    tile = tile_of(unit_width, 256)
    tiles = unit_width // tile
    half_tiles = -(-tiles // 2)
    rest = tiles - half_tiles
    counts = [-(-half_tiles // 2), half_tiles // 2, -(-rest // 2), rest // 2]
    edges = [sum(counts[:place]) * tile for place in range(5)]
    spans = list(zip(edges[:-1], edges[1:]))
    feed_shards = (gate_weight, up_weight, down_weight)

    def units_of(core, start, stop):
        return [
            lax.dynamic_slice_in_dim(shard, core * unit_width + start, stop - start, 1)
            for shard in feed_shards
        ]

    feed_shard = jnp.concatenate(
        [
            part
            for core in (my_core, 1 - my_core)
            for start, stop in spans[:2]
            for part in units_of(core, start, stop)
        ],
        axis=1,
    )
    widths = [3 * (stop - start) for start, stop in spans]
    feed_cuts = (
        pl.ds(0, widths[0]),
        pl.ds(widths[0], widths[1]),
        pl.ds(widths[0] + widths[1], widths[0] + widths[1]),
    )
    full, pair_first, pair_second, _ = gather_call(
        plain_shard, feed_shard, plain_cuts, feed_cuts, plain_orders, 2
    )
    w_qkv, w_out = full[:, : 3 * model_width], full[:, 3 * model_width : 4 * model_width]
    small = full[:, 4 * model_width : 4 * model_width + small_width]
    gain_mixer, gain_feed = small[:, 0], small[:, 1]
    c_query = small[:, 2 : 2 + tap_count]
    c_key = small[:, 2 + tap_count : 2 + 2 * tap_count]
    c_value = small[:, 2 + 2 * tap_count : 2 + 3 * tap_count]
    w_beta = small[:, 2 + 3 * tap_count :]

    feed_blocks = [
        along_groups(
            tied(
                jnp.concatenate(
                    [part for start, stop in spans[2:] for part in units_of(core, start, stop)],
                    axis=1,
                ),
                full,
            )
        )
        for core in (1 - my_core, my_core)
    ]
    theirs_block = swapped(feed_blocks[0], 1)
    feed_pieces = [
        spread_views(pair_first, chip_orders[0], True),
        spread_views(pair_second, chip_orders[1], True),
    ]
    out_half = model_width // 2
    qkv_half = 3 * model_width // 2

    anchor = lax.axis_index(("seq", "grp")) * row_count
    places = anchor + jnp.arange(row_count, dtype=jnp.int32)
    starts = jnp.cumsum(lengths) - lengths
    row_start = jnp.max(jnp.where(starts[None, :] <= places[:, None], starts[None, :], 0), axis=1)
    valid = jnp.stack(
        [(places - offset >= row_start).astype(jnp.float32) for offset in range(1, tap_count)]
    )
    live_rows = pad_mask.astype(jnp.float32)
    inputs32 = tokens.astype(jnp.float32)
    normed_a, norm_a_back = jax.vjp(rms_scale, inputs32, gain_mixer.astype(jnp.float32))
    normed_low = normed_a.astype(jnp.bfloat16)
    own_pre = jnp.dot(normed_low, w_qkv, preferred_element_type=F32).astype(LOW)
    logit_part = jnp.dot(normed_low, w_beta, preferred_element_type=jnp.float32)
    sigmoid_val = jax.nn.sigmoid(logit_part + beta_bias)
    beta_rows = sigmoid_val * live_rows[:, None]
    earlier_rows = passed_along(own_pre[row_count - (tap_count - 1) :], ("seq", "grp"), 1)
    extended = jnp.concatenate([earlier_rows, own_pre], axis=0).astype(jnp.float32)
    kernel = jnp.concatenate([c_query, c_key, c_value], axis=0).astype(jnp.float32)

    def conv_act(padded, kernel_all):
        summed = padded[tap_count - 1 :] * kernel_all[:, tap_count - 1]
        for offset in range(1, tap_count):
            moved = padded[tap_count - 1 - offset : tap_count - 1 - offset + row_count]
            summed = (
                summed + moved * valid[offset - 1][:, None] * kernel_all[:, tap_count - 1 - offset]
            )
        return jax.nn.silu(summed)

    active, conv_pull = jax.vjp(conv_act, extended, kernel)
    flags = jnp.stack(
        [
            (row_start < anchor).astype(jnp.float32),
            (row_start == row_start[-1]).astype(jnp.float32),
            live_rows,
        ],
        axis=1,
    )
    inverse, wy, scores, reach, local_out, pairs = span_call(
        row_start,
        flags,
        beta_rows,
        active,
        head_count,
        after=(feed_pieces[0][1][0], feed_pieces[1][1][0]),
    )
    ready = (pairs, feed_pieces[0][-1][0], feed_pieces[1][-1][0])
    edge = 0
    for place, width in enumerate(widths[2:]):
        paired = join_columns(feed_blocks[1], theirs_block, edge, width, ready)
        feed_pieces.append(spread_views(paired, chip_orders[place], False))
        edge = edge + width
    start_states = scan_call(pairs, False, 0)
    mixed, head_low = mixed_call(
        reach,
        local_out,
        start_states,
        head_gain,
        flags,
        after=tuple(feed_pieces[place][at][0] for place in (2, 3) for at in (1, 2)),
    )
    hidden_one = inputs32 + jnp.dot(head_low, w_out, preferred_element_type=F32)
    normed_f, norm_f_back = jax.vjp(rms_scale, hidden_one, gain_feed.astype(jnp.float32))
    feed_low = normed_f.astype(jnp.bfloat16)
    both_feed = jnp.concatenate([feed_low, swapped(feed_low, 1)], axis=0)
    both_slopes = jnp.concatenate([cotangent, swapped(cotangent, 1)], axis=0)
    feed_rel = relative(both_feed, pair_masks[0])
    slopes_rel = relative(both_slopes, pair_masks[0])
    depth = model_width // len(feed_pieces[0])
    second_places = [pair_masks[1][::2].index(mask) for mask in pair_masks[0][::2]]
    first_places = [pair_masks[0][::2].index(mask) for mask in pair_masks[1][::2]]
    chip_count = len(feed_pieces[0])
    half_places = [
        [list(range(chip_count // 2)), list(range(chip_count // 2, chip_count))],
        [first_places[: chip_count // 2], first_places[chip_count // 2 :]],
    ]
    sources = (feed_rel, slopes_rel)
    totals = None
    feed_grads, lower_halves, sent = [], [], []
    for chunk in range(2):
        grads_first, grads_second, *totals = feed_call(
            feed_rel,
            slopes_rel,
            [
                feed_pieces[2 * chunk],
                [feed_pieces[2 * chunk + 1][place] for place in second_places],
            ],
            totals,
            tile,
            after=lower_halves,
        )
        feed_grads += [grads_first, grads_second]
        for part, grads in enumerate((grads_first, grads_second)):
            places = half_places[part][1]
            pieces = [outer_call(sources, grads, places)]
            lower_halves += pieces
            sent.append([swapped(piece, chip_orders[part][-1]) for piece in pieces])
    out_total, d_total = totals
    their_masks = [mask ^ 1 for mask in pair_masks[0]]
    d_feed = absolute(d_total[:row_count], pair_masks[0]) + absolute(
        swapped(d_total[row_count:], 1), their_masks
    )
    block_out = (
        hidden_one
        + absolute(out_total[:row_count], pair_masks[0])
        + absolute(swapped(out_total[row_count:], 1), their_masks)
    ).astype(jnp.bfloat16)
    grad_out = cotangent.astype(jnp.float32)
    d_hidden_part, d_gain_feed = norm_f_back(d_feed)
    d_hidden = grad_out + d_hidden_part
    d_attn = d_hidden.astype(jnp.bfloat16)
    d_head = contract_rows(d_attn, full, 3 * model_width, after=lower_halves)

    def feed_upper(place, after):
        starts = (0, 1)[: len(sent[place])]
        return outer_call(
            sources, feed_grads[place], half_places[place % 2][0], None, sent[place], starts, after
        )

    def chip_sum(total, part):
        for bit in reversed(chip_orders[part][:-1]):
            total = halved_sum(total, bit)
        return total

    def device_sum(totals):
        half = totals[0].shape[0] // 2
        mine = [total[:half] for total in totals]
        theirs = [swapped(total[half:], 1) for total in totals]
        return over_groups(jnp.concatenate(mine + theirs, axis=1))

    def both_halves(grads):
        width = grads.shape[1] // 2
        mine = lax.dynamic_slice_in_dim(grads, my_core * width, width, 1)
        theirs = lax.dynamic_slice_in_dim(grads, (1 - my_core) * width, width, 1)
        return jnp.concatenate([mine, swapped(theirs, 1)], axis=0)

    d_mixed, d_head_gain, back_pairs = pull_call(
        reach, mixed, d_head, head_gain, flags, pairs, after=(sent[0][0], sent[1][0])
    )
    upper_first = [feed_upper(place, ()) for place in range(2)]
    end_states = scan_call(back_pairs, True, 1, after=upper_first)
    chip_first = [chip_sum(total, part) for part, total in enumerate(upper_first)]
    upper_second = [feed_upper(place, (end_states,)) for place in range(2, 4)]
    chip_second = [chip_sum(total, part) for part, total in enumerate(upper_second)]
    both_attn = both_halves(d_attn)
    plain_sources = [
        relative(jnp.concatenate([rows, swapped(rows, 1)], axis=0), pair_masks[0])
        for rows in (normed_low, head_low)
    ]
    d_queries, d_keys, d_values, d_betas = back_call(
        row_start,
        flags,
        beta_rows,
        active,
        inverse,
        wy,
        scores,
        start_states,
        end_states,
        d_mixed,
        after=upper_second,
    )
    d_logit32 = d_betas * live_rows[:, None] * sigmoid_val * (1.0 - sigmoid_val)
    d_logit = d_logit32.astype(jnp.bfloat16)
    d_extended, d_kernel = conv_pull(jnp.concatenate([d_queries, d_keys, d_values], axis=1))
    from_next = passed_along(
        d_extended[: tap_count - 1].astype(jnp.bfloat16), ("seq", "grp"), -1
    ).astype(jnp.float32)
    d_own = d_extended[tap_count - 1 :] + jnp.pad(
        from_next, ((row_count - (tap_count - 1), 0), (0, 0))
    )
    d_pre = d_own.astype(jnp.bfloat16)
    both_pre = both_halves(d_pre)
    fine = model_width // 4

    def plain_grads(part):
        kinds = [
            both_pre[:, (3 * part + kind) * fine : (3 * part + kind + 1) * fine]
            for kind in range(3)
        ]
        return jnp.stack(kinds + [both_attn[:, part * fine : (part + 1) * fine]])

    plain_slopes = [plain_grads(part) for part in range(2)]
    plain_lower = [
        outer_call(
            plain_sources, plain_slopes[part], half_places[part][1], after=(*chip_first, *chip_second)
        )
        for part in range(2)
    ]
    plain_upper = [
        outer_call(plain_sources, plain_slopes[part], half_places[part][0]) for part in range(2)
    ]
    d_normed = contract(d_logit, w_beta) + contract_rows(d_pre, full, 0)
    feed_kept = [device_sum(chip_first), device_sum(chip_second)]
    d_input_part, d_gain_mixer = norm_a_back(d_normed)
    input_grad = (d_hidden + d_input_part).astype(jnp.bfloat16)
    small_grads = jnp.concatenate(
        [
            lax.dot_general(
                normed_low, d_logit, (((0,), (0,)), ((), ())), preferred_element_type=F32
            ),
            d_kernel[:model_width],
            d_kernel[model_width : 2 * model_width],
            d_kernel[2 * model_width :],
            d_gain_mixer[:, None],
            d_gain_feed[:, None],
        ],
        axis=1,
    )
    small_both = jnp.pad(
        jnp.where(my_core == 0, small_grads + swapped(small_grads, 1), 0.0).astype(LOW),
        ((0, 0), (0, 128 - small_grads.shape[1])),
    )
    block_rows = model_width // lax.axis_size("seq")
    small_blocks = [
        lax.dynamic_slice_in_dim(
            small_both, (lax.axis_index("seq") ^ mask) * block_rows, block_rows, 0
        )
        for mask in pair_masks[0]
    ]
    half_blocks = len(small_blocks) // 2
    small_upper = jnp.concatenate(small_blocks[:half_blocks], axis=0)
    small_lower = jnp.concatenate(small_blocks[half_blocks:], axis=0)
    vector = jnp.concatenate([d_head_gain[0], jnp.sum(d_logit32, axis=0)])
    padded = jnp.zeros((8, 256), F32).at[0, : vector.shape[0]].set(vector)
    plain_sum, small_sum, everywhere = reduce_call(
        [
            (plain_lower, plain_upper, 8),
            ((small_lower, small_lower), (small_upper, small_upper), 1),
        ],
        padded,
        chip_orders,
        3,
    )
    replicated = everywhere[0, : vector.shape[0]]

    def in_order(mine, other):
        return jnp.concatenate(
            [jnp.where(my_core == 0, mine, other), jnp.where(my_core == 0, other, mine)], axis=1
        )

    fine = fine // 2
    groups = [plain_sum[:, at * fine : (at + 1) * fine] for at in range(32)]
    qkv_grad, out_grad = [
        in_order(
            *[
                jnp.concatenate(
                    [
                        groups[4 * kind + 2 * owner + part]
                        for part in range(2)
                        for kind in range(*span)
                    ],
                    axis=1,
                )
                for owner in range(2)
            ]
        )
        for span in ((0, 6), (6, 8))
    ]
    feed_sums = []
    for kind in range(3):
        halves = []
        for owner in range(2):
            for chunk in range(2):
                at = owner * feed_kept[chunk].shape[1] // 2
                for start, stop in spans[2 * chunk : 2 * chunk + 2]:
                    width = stop - start
                    halves.append(
                        feed_kept[chunk][:, at + kind * width : at + (kind + 1) * width]
                    )
                    at = at + 3 * width
        feed_sums.append(
            in_order(jnp.concatenate(halves[:4], axis=1), jnp.concatenate(halves[4:], axis=1))
        )
    gate_grad, up_grad, down_grad = feed_sums
    sharded = jnp.where(my_core == 0, small_sum[:, :128], small_sum[:, 256:384])
    taps_at = head_count + 3 * tap_count
    return (
        block_out,
        input_grad,
        sharded[:, taps_at],
        qkv_grad[:, :model_width],
        qkv_grad[:, model_width : 2 * model_width],
        qkv_grad[:, 2 * model_width :],
        sharded[:, head_count : head_count + tap_count],
        sharded[:, head_count + tap_count : head_count + 2 * tap_count],
        sharded[:, head_count + 2 * tap_count : taps_at],
        sharded[:, :head_count],
        replicated[head_width:],
        replicated[:head_width],
        out_grad,
        sharded[:, taps_at + 1],
        gate_grad,
        up_grad,
        down_grad,
    )


def solution(mesh):
    placed = (
        P(("seq", "grp"), None),
        P(("seq", "grp"), None),
        P(),
        P(("seq", "grp")),
        P(("seq", "grp")),
        P(("seq", "grp"), None),
        P(("seq", "grp"), None),
        P(("seq", "grp"), None),
        P(("seq", "grp"), None),
        P(("seq", "grp"), None),
        P(("seq", "grp"), None),
        P(("seq", "grp"), None),
        P(),
        P(),
        P(("seq", "grp"), None),
        P(("seq", "grp")),
        P(("seq", "grp"), None),
        P(("seq", "grp"), None),
        P(("seq", "grp"), None),
    )
    return jax.shard_map(
        local,
        mesh=mesh,
        in_specs=placed,
        out_specs=(
            P(("seq", "grp"), None),
            P(("seq", "grp"), None),
            P(("seq", "grp")),
            P(("seq", "grp"), None),
            P(("seq", "grp"), None),
            P(("seq", "grp"), None),
            P(("seq", "grp"), None),
            P(("seq", "grp"), None),
            P(("seq", "grp"), None),
            P(("seq", "grp"), None),
            P(),
            P(),
            P(("seq", "grp"), None),
            P(("seq", "grp")),
            P(("seq", "grp"), None),
            P(("seq", "grp"), None),
            P(("seq", "grp"), None),
        ),
        check_vma=False,
    )
```

```python
import functools

import jax
import jax.numpy as jnp
from jax import lax
from jax.experimental import pallas as pl
from jax.experimental.pallas import tpu as pltpu
from jax.sharding import PartitionSpec as P

F32 = jnp.float32
LOW = jnp.bfloat16
EPSILON = 1e-06
VMEM_LIMIT = 56 * 1024 * 1024
SPAN_HEADS = 4
BACK_HEADS = 2
HALO = 16
AHEAD = 1


def passed_along(value, axis, steps):
    count = lax.axis_size(axis)
    first, last = (max(0, -steps), min(count, count - steps))
    return lax.ppermute(value, axis, [(source, source + steps) for source in range(first, last)])


def rms_scale(values, gain):
    return values * lax.rsqrt(jnp.mean(values * values, axis=-1, keepdims=True) + EPSILON) * gain


def contract(left, right):
    return lax.dot_general(
        left, right, (((1,), (1,)), ((), ())), preferred_element_type=jnp.float32
    )


def launch(kernel, after, in_specs, operands, **options):
    count = len(after)

    def body(*refs):
        kernel(*refs[count:])

    return pl.pallas_call(
        body,
        in_specs=[pl.BlockSpec(memory_space=pl.ANY)] * count + list(in_specs),
        compiler_params=pltpu.CompilerParams(vmem_limit_bytes=VMEM_LIMIT),
        **options,
    )(*after, *operands)


def estimate(flops, moved, steps=0):
    return pl.CostEstimate(flops=1, bytes_accessed=1, transcendentals=0)


def split_low(value):
    upper = value.astype(LOW)
    return (upper, (value - upper.astype(F32)).astype(LOW))


def dot_one(left, right, dims=((1,), (0,))):
    return lax.dot_general(
        left.astype(LOW), right.astype(LOW), (dims, ((), ())), preferred_element_type=F32
    )


def dot_three(left, right, dims=((1,), (0,))):
    left_high, left_rest = split_low(left)
    right_high, right_rest = split_low(right)
    both = functools.partial(
        lax.dot_general, dimension_numbers=(dims, ((), ())), preferred_element_type=F32
    )
    return both(left_high, right_high) + (both(left_high, right_rest) + both(left_rest, right_high))


ROWS_ROWS = ((1,), (1,))
FIRST_FIRST = ((0,), (0,))


def inverse_unit_lower(lowers, size):
    row = lax.broadcasted_iota(jnp.int32, (size, size), 0)
    column = lax.broadcasted_iota(jnp.int32, (size, size), 1)
    eye = jnp.where(row == column, 1.0, 0.0).astype(F32)
    inverses = [eye for _ in lowers]
    span = 1
    while span < size:
        joined = (row // (2 * span) == column // (2 * span)) & (row // span != column // span)
        parts = [jnp.where(joined, lower, 0.0) for lower in lowers]
        if span > 1:
            parts = [dot_three(part, inverse) for part, inverse in zip(parts, inverses)]
            parts = [dot_three(inverse, part) for part, inverse in zip(parts, inverses)]
        inverses = [inverse - part for part, inverse in zip(parts, inverses)]
        span = span * 2
    return inverses


def unit(active):
    scale = lax.rsqrt(jnp.sum(active * active, axis=1, keepdims=True) + EPSILON)
    return (active * scale, scale)


def unit_back(grad, normal, scale):
    return scale * (grad - normal * jnp.sum(grad * normal, axis=1, keepdims=True))


def pick_lane(block, index):
    lane = lax.broadcasted_iota(jnp.int32, block.shape, 1)
    return jnp.sum(jnp.where(lane == index, block, 0.0), axis=1, keepdims=True)


def convolved(rows, taps, flags, tap_count):
    extended = rows[HALO - 8 :].astype(F32)
    total = extended[8:] * taps[tap_count - 1 : tap_count]
    for offset in range(1, tap_count):
        moved = pltpu.roll(extended, offset, 0)[8:] * flags[:, 2 + offset : 3 + offset]
        total = total + moved * taps[tap_count - 1 - offset : tap_count - offset]
    return (total, extended)


def convolved_back(d_total, extended, taps, flags, tap_count):
    rows = extended.shape[0]
    before = jnp.zeros((8, d_total.shape[1]), F32)
    d_rows = jnp.concatenate([before, d_total * taps[tap_count - 1 : tap_count]], axis=0)
    d_taps = [jnp.sum(d_total * extended[8:], axis=0, keepdims=True)]
    for offset in range(1, tap_count):
        kept = d_total * flags[:, 2 + offset : 3 + offset]
        moved = pltpu.roll(extended, offset, 0)[8:]
        d_taps = [jnp.sum(kept * moved, axis=0, keepdims=True)] + d_taps
        scaled = jnp.concatenate(
            [before, kept * taps[tap_count - 1 - offset : tap_count - offset]], axis=0
        )
        d_rows = d_rows + pltpu.roll(scaled, rows - offset, 0)
    d_taps = d_taps + [jnp.zeros((8 - tap_count, d_total.shape[1]), F32)]
    return (d_rows[8:], d_rows[:8], jnp.concatenate(d_taps, axis=0))


def silu_of(total):
    gate = 1.0 / (1.0 + jnp.exp(-total))
    return (total * gate, gate)


def span_kernel(
    many, tap_count, starts_col, starts_row, flags, betas, rows_q, rows_k, rows_v,
    taps_q, taps_k, taps_v,
    inverse_out, wy_out, scores_out, reach_out, local_out, pair_out,
):
    count = flags.shape[0]
    width = rows_q.shape[1] // many
    queries, keys, values = [
        silu_of(convolved(rows[...], taps[...], flags, tap_count)[0])[0]
        for rows, taps in ((rows_q, taps_q), (rows_k, taps_k), (rows_v, taps_v))
    ]
    row = lax.broadcasted_iota(jnp.int32, (count, count), 0)
    column = lax.broadcasted_iota(jnp.int32, (count, count), 1)
    same_doc = starts_col[...] == starts_row[...]
    first = flags[:, 0:1]
    last_part = flags[:, 1:2]
    eye = jnp.where(
        lax.broadcasted_iota(jnp.int32, (width, width), 0)
        == lax.broadcasted_iota(jnp.int32, (width, width), 1),
        1.0,
        0.0,
    )
    spots = [slice(at * width, (at + 1) * width) for at in range(many)]
    beta = [pick_lane(betas[...], pl.program_id(0) * many + at) for at in range(many)]
    query = [unit(queries[:, spot])[0] for spot in spots]
    key = [unit(keys[:, spot])[0] for spot in spots]
    products = [
        dot_three(jnp.concatenate([k, q], axis=0), k, ROWS_ROWS) for q, k in zip(query, key)
    ]
    lower = [
        jnp.where(same_doc & (row > column), b * p[:count], 0.0) for b, p in zip(beta, products)
    ]
    scores = [jnp.where(same_doc & (row >= column), p[count:], 0.0) for p in products]
    inverse = inverse_unit_lower(lower, count)
    for at, spot in enumerate(spots):
        scaled = jnp.concatenate(
            [key[at] * (beta[at] * first), values[:, spot] * beta[at]], axis=1
        )
        wy = dot_three(inverse[at], scaled)
        applied = dot_three(scores[at], wy)
        inverse_out[at] = inverse[at]
        wy_out[at] = wy
        scores_out[at] = scores[at]
        reach_out[:, spot] = first * query[at] - applied[:, :width]
        local_out[:, spot] = applied[:, width:]
        pair = dot_three(key[at] * last_part, wy, FIRST_FIRST)
        change = (flags[count - 1 : count, 0:1] - 1.0) * eye - pair[:, :width]
        pair_out[at] = jnp.concatenate([change, pair[:, width:]], axis=1).astype(LOW)


def rows_specs(count, width, head_count):
    steps = head_count
    return [
        pl.BlockSpec((count, width), lambda step, part=part: (0, part * steps + step))
        for part in range(3)
    ]


def span_call(starts, flags, betas, extended, taps, tap_count, head_count, after=()):
    many = SPAN_HEADS
    count, width = flags.shape[0], extended.shape[1] // (3 * head_count)
    rows = pl.BlockSpec((count, many * width), lambda step: (0, step))
    whole = lambda shape: pl.BlockSpec(shape, lambda step: (0, 0))
    square = pl.BlockSpec((many, count, count), lambda step: (step, 0, 0))
    return launch(
        functools.partial(span_kernel, many, tap_count),
        after,
        grid=(head_count // many,),
        in_specs=[
            whole((count, 1)), whole((1, count)), whole(flags.shape), whole(betas.shape),
        ]
        + rows_specs(extended.shape[0], many * width, head_count // many)
        + rows_specs(8, many * width, head_count // many),
        out_specs=[
            square,
            pl.BlockSpec((many, count, 2 * width), lambda step: (step, 0, 0)),
            square, rows, rows,
            pl.BlockSpec((many, width, 2 * width), lambda step: (step, 0, 0)),
        ],
        out_shape=[
            jax.ShapeDtypeStruct((head_count, count, count), F32),
            jax.ShapeDtypeStruct((head_count, count, 2 * width), F32),
            jax.ShapeDtypeStruct((head_count, count, count), F32),
            jax.ShapeDtypeStruct((count, head_count * width), F32),
            jax.ShapeDtypeStruct((count, head_count * width), F32),
            jax.ShapeDtypeStruct((head_count, width, 2 * width), LOW),
        ],
        cost_estimate=estimate(1, 1),
        operands=(
            starts[:, None], starts[None, :], flags, betas, extended, extended, extended,
            taps, taps, taps,
        ),
    )


def mixed_kernel(reach, local, state, gain, flags, mixed_out, head_out):
    mixed = local[...] + dot_three(reach[...], state[0].astype(F32))
    mixed_out[...] = mixed
    scale = lax.rsqrt(jnp.mean(mixed * mixed, axis=1, keepdims=True) + EPSILON)
    head_out[...] = (mixed * scale * gain[...] * flags[:, 2:3]).astype(LOW)


def mixed_call(reach, local, states, gain, flags, after=()):
    head_count, width = states.shape[0], states.shape[1]
    count = reach.shape[0]
    rows = pl.BlockSpec((count, width), lambda head: (0, head))
    return launch(
        mixed_kernel,
        after,
        grid=(head_count,),
        in_specs=[
            rows, rows,
            pl.BlockSpec((1, width, width), lambda head: (head, 0, 0)),
            pl.BlockSpec((1, width), lambda head: (0, 0)),
            pl.BlockSpec(flags.shape, lambda head: (0, 0)),
        ],
        out_specs=[rows, rows],
        out_shape=[
            jax.ShapeDtypeStruct(reach.shape, F32),
            jax.ShapeDtypeStruct(reach.shape, LOW),
        ],
        cost_estimate=estimate(6 * count * width * width * head_count, 14 * reach.shape[0] * reach.shape[1]),
        operands=(reach, local, states, gain[None], flags,),
    )


def pull_kernel(reach, mixed_in, grads, gain, flags, change, d_mixed_out, gain_out, pair_out):
    mixed, d_head, live = mixed_in[...], grads[...], flags[:, 2:3]
    width = mixed.shape[1]
    scale = lax.rsqrt(jnp.mean(mixed * mixed, axis=1, keepdims=True) + EPSILON)
    lifted = d_head * gain[...]
    inner = jnp.mean(lifted * mixed, axis=1, keepdims=True)
    d_mixed = live * (scale * lifted - mixed * (scale * scale * scale * inner))
    d_mixed_out[...] = d_mixed
    part = jnp.sum(d_head * mixed * (scale * live), axis=0, keepdims=True)

    @pl.when(pl.program_id(0) == 0)
    def _():
        gain_out[...] = jnp.zeros_like(gain_out)

    gain_out[...] += part
    pulled = dot_three(reach[...], d_mixed, FIRST_FIRST)
    turned = jnp.transpose(change[0, :, :width].astype(F32))
    pair_out[0] = jnp.concatenate([turned, pulled], axis=1).astype(LOW)


def pull_call(reach, mixed, grads, gain, flags, pairs, after=()):
    head_count, width = pairs.shape[0], pairs.shape[1]
    count = reach.shape[0]
    rows = pl.BlockSpec((count, width), lambda head: (0, head))
    pair = pl.BlockSpec((1, width, 2 * width), lambda head: (head, 0, 0))
    return launch(
        pull_kernel,
        after,
        grid=(head_count,),
        in_specs=[
            rows, rows, rows,
            pl.BlockSpec((1, width), lambda head: (0, 0)),
            pl.BlockSpec(flags.shape, lambda head: (0, 0)),
            pair,
        ],
        out_specs=[rows, pl.BlockSpec((1, width), lambda head: (0, 0)), pair],
        out_shape=[
            jax.ShapeDtypeStruct(reach.shape, F32),
            jax.ShapeDtypeStruct((1, width), F32),
            jax.ShapeDtypeStruct(pairs.shape, LOW),
        ],
        cost_estimate=estimate(6 * count * width * width * head_count, 20 * reach.shape[0] * reach.shape[1]),
        operands=(reach, mixed, grads, gain[None], flags, pairs,),
    )


def back_kernel(
    many, tap_count, starts_col, starts_row, flags, betas, rows_q, rows_k, rows_v,
    taps_q, taps_k, taps_v, inverse_in, wy_in, scores_in, state_in, end_in, grads,
    d_rows_out, d_tail_out, d_before_out, d_taps_out, d_beta_out,
):
    count = flags.shape[0]
    width = rows_q.shape[1] // many
    all_rows, all_taps = (rows_q, rows_k, rows_v), (taps_q, taps_k, taps_v)
    row = lax.broadcasted_iota(jnp.int32, (count, count), 0)
    column = lax.broadcasted_iota(jnp.int32, (count, count), 1)
    same_doc = starts_col[...] == starts_row[...]
    first = flags[:, 0:1]
    last_part = flags[:, 1:2]
    lane = lax.broadcasted_iota(jnp.int32, d_beta_out.shape, 1)
    d_betas = jnp.zeros(d_beta_out.shape, F32)
    for at in range(many):
        spot = slice(at * width, (at + 1) * width)
        head = pl.program_id(0) * many + at
        beta = pick_lane(betas[...], head)
        summed = [
            convolved(rows[:, spot], taps[:, spot], flags, tap_count)
            for rows, taps in zip(all_rows, all_taps)
        ]
        active = [silu_of(total) for total, _ in summed]
        query, query_scale = unit(active[0][0])
        key, key_scale = unit(active[1][0])
        value, grad = active[2][0], grads[:, spot]
        inverse, wy, scores = inverse_in[at], wy_in[at], scores_in[at]
        state, end = state_in[at].astype(F32), end_in[at].astype(F32)
        fresh = wy[:, width:] - dot_three(wy[:, :width], state)
        d_fresh = dot_three(scores, grad, FIRST_FIRST) + dot_three(key * last_part, end)
        pulled = dot_three(inverse, d_fresh, FIRST_FIRST)
        both = jnp.concatenate([grad, pulled], axis=0)
        through_state = dot_three(both, state, ROWS_ROWS)
        through_fresh = dot_three(both, fresh, ROWS_ROWS)
        d_scores = jnp.where(same_doc & (row >= column), through_fresh[:count], 0.0)
        d_lower = jnp.where(same_doc & (row > column), -through_fresh[count:], 0.0)
        by_keys = dot_three(jnp.concatenate([d_scores, d_lower], axis=0), key)
        d_query = first * through_state[:count] + by_keys[:count]
        recalled = -through_state[count:]
        row_part = by_keys[count:]
        d_key = (
            dot_three(d_scores, query, FIRST_FIRST)
            + dot_three(d_lower, beta * key, FIRST_FIRST)
            + last_part * dot_three(fresh, end, ROWS_ROWS)
            + (beta * first) * recalled
            + beta * row_part
        )
        d_active = (
            unit_back(d_query, query, query_scale),
            unit_back(d_key, key, key_scale),
            beta * pulled,
        )
        for kind in range(3):
            total, gate = summed[kind][0], active[kind][1]
            d_total = d_active[kind] * gate * (1.0 + total * (1.0 - gate))
            d_rows, d_before, d_taps = convolved_back(
                d_total, summed[kind][1], all_taps[kind][:, spot], flags, tap_count
            )
            d_rows_out[kind, :, spot] = d_rows.astype(LOW)
            d_tail_out[kind, :, spot] = d_rows[count - 8 :]
            d_before_out[kind, :, spot] = d_before
            d_taps_out[kind, :, spot] = d_taps
        d_beta = jnp.sum(
            (row_part + first * recalled) * key + pulled * value, axis=1, keepdims=True
        )
        d_betas = d_betas + jnp.where(lane == head, d_beta, 0.0)

    @pl.when(pl.program_id(0) == 0)
    def _():
        d_beta_out[...] = d_betas

    @pl.when(pl.program_id(0) > 0)
    def _():
        d_beta_out[...] += d_betas


def back_call(
    starts, flags, betas, extended, taps, tap_count, inverse, wy, scores, states, ends, grads,
    after=(),
):
    many = BACK_HEADS
    head_count, width = states.shape[0], states.shape[1]
    count = flags.shape[0]
    steps = head_count // many
    kinds = lambda height: pl.BlockSpec((3, height, many * width), lambda step: (0, 0, step))
    rows = pl.BlockSpec((count, many * width), lambda step: (0, step))
    whole = lambda shape: pl.BlockSpec(shape, lambda step: (0, 0))
    per_head = lambda shape: pl.BlockSpec((many,) + shape, lambda step: (step, 0, 0))
    return launch(
        functools.partial(back_kernel, many, tap_count),
        after,
        grid=(head_count // many,),
        in_specs=[
            whole((count, 1)), whole((1, count)), whole(flags.shape), whole(betas.shape),
            *rows_specs(extended.shape[0], many * width, steps),
            *rows_specs(8, many * width, steps),
            per_head((count, count)), per_head((count, 2 * width)), per_head((count, count)),
            per_head((width, width)), per_head((width, width)),
            rows,
        ],
        out_specs=[kinds(count), kinds(8), kinds(8), kinds(8), whole(betas.shape)],
        out_shape=[
            jax.ShapeDtypeStruct((3,) + grads.shape, LOW),
            jax.ShapeDtypeStruct((3, 8, grads.shape[1]), F32),
            jax.ShapeDtypeStruct((3, 8, grads.shape[1]), F32),
            jax.ShapeDtypeStruct((3, 8, grads.shape[1]), F32),
            jax.ShapeDtypeStruct(betas.shape, F32),
        ],
        cost_estimate=estimate(36 * head_count * count**3, 40 * grads.shape[0] * grads.shape[1]),
        operands=(
            starts[:, None], starts[None, :], flags, betas, extended, extended, extended,
            taps, taps, taps, inverse, wy, scores, states, ends, grads,
        ),
    )


def apply_pair(change, pair):
    upper, rest = split_low(pair)
    product = functools.partial(jnp.dot, preferred_element_type=F32)
    return pair + (product(change, upper) + product(change, rest))


def scan_kernel(
    waited, backwards, group_size, seq_size, *refs,
):
    scan_steps(backwards, group_size, seq_size, *refs[waited:])


def scan_steps(
    backwards, group_size, seq_size, pairs, states_out,
    got, total_sent, total_got, state_sent, arrived, send_sem, recv_sem,
):
    head_count, width = pairs.shape[0], pairs.shape[1]
    share = head_count // group_size
    my_seq, my_group = lax.axis_index("seq"), lax.axis_index("grp")
    peers = [lax.rem(my_group + step, group_size) for step in range(1, group_size)]
    bits = []
    while 2 ** len(bits) < seq_size:
        bits.append(2 ** len(bits))
    upper_half = [lax.rem(my_seq // bit, 2) for bit in bits]
    partners = [my_seq + bit - 2 * bit * half for bit, half in zip(bits, upper_half)]
    barrier = pltpu.get_barrier_semaphore()
    for peer in peers:
        pl.semaphore_signal(
            barrier, inc=1, device_id=(my_seq, peer), device_id_type=pl.DeviceIdType.MESH
        )
    for partner in partners:
        pl.semaphore_signal(
            barrier, inc=1, device_id=(partner, my_group), device_id_type=pl.DeviceIdType.MESH
        )
    pl.semaphore_wait(barrier, len(peers) + len(partners))

    def send(source, target, place, device):
        copy = pltpu.make_async_remote_copy(
            src_ref=source,
            dst_ref=target,
            send_sem=send_sem.at[place],
            recv_sem=recv_sem.at[place],
            device_id=device,
            device_id_type=pl.DeviceIdType.MESH,
        )
        copy.start()
        return copy

    mine = pl.ds(my_group * share, share)
    copies = [
        send(pairs.at[pl.ds(peer * share, share)], got.at[my_group], place, (my_seq, peer))
        for place, peer in enumerate(peers)
    ]
    got[my_group] = pairs[mine]
    for copy in copies:
        copy.wait()
    members = list(range(group_size))
    if backwards:
        members = members[::-1]
    eye = jnp.where(
        lax.broadcasted_iota(jnp.int32, (width, width), 0)
        == lax.broadcasted_iota(jnp.int32, (width, width), 1),
        1.0,
        0.0,
    )
    nothing = jnp.zeros((width, width), F32)
    start = jnp.concatenate([eye, nothing], axis=1)

    def added(pair):
        return jnp.concatenate([nothing, pair[:, width:].astype(F32)], axis=1)

    totals = []
    for head in range(share):
        total = start + got[members[0], head].astype(F32)
        for member in members[1:]:
            pair = got[member, head]
            total = apply_pair(pair[:, :width], total) + added(pair)
        totals.append(total)
    before = [start for _ in range(share)]
    for level, partner in enumerate(partners):
        for head in range(share):
            total_sent[level, head] = (totals[head] - start).astype(LOW)
        copy = send(
            total_sent.at[level],
            total_got.at[level],
            group_size - 1 + level,
            (partner, my_group),
        )
        copy.wait()
        later = upper_half[level] == (0 if backwards else 1)
        for head in range(share):
            theirs = total_got[level, head].astype(F32) + start
            first_pair = jnp.where(later, theirs, totals[head])
            second_pair = jnp.where(later, totals[head], theirs)
            moved = dot_three(
                jnp.concatenate([second_pair[:, :width], before[head][:, :width]], axis=0),
                first_pair,
            )
            totals[head] = moved[:width] + added(second_pair)
            before[head] = jnp.where(later, moved[width:] + added(before[head]), before[head])
    for head in range(share):
        state = before[head][:, width:]
        for member in members:
            state_sent[member, head] = state.astype(LOW)
            if member != members[-1]:
                pair = got[member, head]
                state = apply_pair(pair[:, :width], state) + pair[:, width:].astype(F32)
    place_now = group_size - 1 + len(bits)
    copies = [
        send(state_sent.at[peer], arrived.at[mine], place_now + place, (my_seq, peer))
        for place, peer in enumerate(peers)
    ]
    arrived[mine] = state_sent[my_group]
    for copy in copies:
        copy.wait()
    states_out[...] = arrived[...]


def scan_call(pairs, backwards, collective_id, after=()):
    head_count, width = pairs.shape[0], pairs.shape[1]
    group_size, seq_size = lax.axis_size("grp"), lax.axis_size("seq")
    share = head_count // group_size
    levels = (seq_size - 1).bit_length()
    sems = 2 * (group_size - 1) + levels
    return pl.pallas_call(
        functools.partial(scan_kernel, len(after), backwards, group_size, seq_size),
        in_specs=[pl.BlockSpec(memory_space=pl.ANY)] * len(after)
        + [pl.BlockSpec(memory_space=pltpu.VMEM)],
        out_specs=pl.BlockSpec(memory_space=pltpu.VMEM),
        out_shape=jax.ShapeDtypeStruct((head_count, width, width), LOW),
        cost_estimate=estimate(400 * share * width**3 * levels, 64 * pairs.size),
        scratch_shapes=[
            pltpu.VMEM((group_size, share, width, 2 * width), LOW),
            pltpu.VMEM((levels, share, width, 2 * width), LOW),
            pltpu.VMEM((levels, share, width, 2 * width), LOW),
            pltpu.VMEM((group_size, share, width, width), LOW),
            pltpu.VMEM((head_count, width, width), LOW),
            pltpu.SemaphoreType.DMA((sems,)),
            pltpu.SemaphoreType.DMA((sems,)),
        ],
        compiler_params=pltpu.CompilerParams(
            collective_id=collective_id, has_side_effects=True, vmem_limit_bytes=VMEM_LIMIT
        ),
    )(*after, pairs)


def swapped(value, bit):
    count = lax.axis_size("seq")
    return lax.ppermute(value, "seq", [(place, place ^ bit) for place in range(count)])


def chip_bits():
    count = lax.axis_size("seq")
    bits = []
    bit = 2
    while bit < count:
        bits.append(bit)
        bit = bit * 2
    return bits


def masks_of(order):
    masks = [0]
    for bit in order:
        masks = masks + [mask ^ bit for mask in masks]
    return masks


def tied(value, *others):
    return lax.optimization_barrier((value,) + others)[0]


def relative(values, masks):
    count = lax.axis_size("seq")
    width = values.shape[1] // count
    mine = lax.axis_index("seq")
    return jnp.concatenate(
        [lax.dynamic_slice_in_dim(values, (mine ^ mask) * width, width, 1) for mask in masks],
        axis=1,
    )


def spread_views(block, order, joined):
    views = [(block, 0)]
    for bit in order:
        if joined:
            if len(views) > 1:
                rows = block.shape[0]
                held = jnp.concatenate(
                    [array[at * rows : (at + 1) * rows] for array, at in views], axis=0
                )
            else:
                held = block
            arrived = swapped(held, bit)
            views = views + [(arrived, at) for at in range(len(views))]
        else:
            views = views + [(swapped(array, bit), at) for array, at in views]
    return views


def add_kernel(kept, arrived, total):
    total[...] = (kept[...].astype(F32) + arrived[...].astype(F32)).astype(LOW)


def halved_sum(kept, bit, after=()):
    rows, width = kept.shape
    half = rows // 2
    arrived = swapped(kept[half:], bit)
    tile = tile_of(width, 512)
    spot = pl.BlockSpec((half, tile), lambda step: (0, step))
    return launch(
        add_kernel,
        after,
        grid=(width // tile,),
        in_specs=[spot, spot],
        out_specs=spot,
        out_shape=jax.ShapeDtypeStruct((half, width), LOW),
        cost_estimate=estimate(1, 1),
        operands=(kept, arrived),
    )


def over_groups(rows):
    return lax.psum_scatter(rows, "grp", scatter_dimension=0, tiled=True).astype(F32)


def tile_of(width, largest):
    tile = largest
    while width % tile:
        tile = tile // 2
    return tile


def copy_kernel(source, target):
    target[...] = source[...]


def columns(block, start, width):
    rows = block.shape[0]
    return launch(
        copy_kernel,
        (),
        grid=(1,),
        in_specs=[pl.BlockSpec((rows, width), lambda step: (0, start // width))],
        out_specs=pl.BlockSpec((rows, width), lambda step: (0, 0)),
        out_shape=jax.ShapeDtypeStruct((rows, width), block.dtype),
        cost_estimate=estimate(1, 1),
        operands=(block,),
    )


def join_kernel(first, second, target):
    rows = first.shape[0]
    target[:rows] = first[...]
    target[rows:] = second[...]


def join_columns(first, second, start, width, after=()):
    tile = tile_of(width, 1024)
    while start % tile:
        tile = tile // 2
    rows = first.shape[0]
    return launch(
        join_kernel,
        after,
        grid=(width // tile,),
        in_specs=[pl.BlockSpec((rows, tile), lambda step: (0, start // tile + step))] * 2,
        out_specs=pl.BlockSpec((2 * rows, tile), lambda step: (0, step)),
        out_shape=jax.ShapeDtypeStruct((2 * rows, width), first.dtype),
        cost_estimate=estimate(0, 4 * rows * width),
        operands=(first, second),
    )


def contract_kernel(grads, weights, total):
    @pl.when(pl.program_id(0) == 0)
    def _():
        total[...] = jnp.zeros_like(total)

    total[...] += lax.dot_general(
        grads[...], weights[...], (((1,), (1,)), ((), ())), preferred_element_type=F32
    )


def contract_rows(grads, weights, start, after=()):
    tokens, width = grads.shape
    tile = tile_of(width, 512)
    depth = weights.shape[0]
    first = start // tile
    return launch(
        contract_kernel,
        after,
        grid=(width // tile,),
        in_specs=[
            pl.BlockSpec((tokens, tile), lambda step: (0, step)),
            pl.BlockSpec((depth, tile), lambda step: (0, first + step)),
        ],
        out_specs=pl.BlockSpec((tokens, depth), lambda step: (0, 0)),
        out_shape=jax.ShapeDtypeStruct((tokens, depth), F32),
        cost_estimate=estimate(2 * tokens * depth * width, 2 * depth * width),
        operands=(grads, weights),
    )


def chip_spots(orders, depth):
    chip = lax.axis_index("seq") // 2
    spots = []
    for mask in orders:
        place = chip
        bit = 1
        while bit <= mask:
            if mask & bit:
                place = place + bit - 2 * bit * lax.rem(chip // bit, 2)
            bit = bit * 2
        spots.append(pl.ds(pl.multiple_of(place * depth, depth), depth))
    return spots


def cores_turned(block):
    half = block.shape[1] // 2
    turned = jnp.concatenate([block[:, half:], block[:, :half]], axis=1)
    return jnp.where(lax.rem(lax.axis_index("seq"), 2) == 0, block, turned)


def feed_kernel(count, cuts, masks, stage, *refs):
    if stage == 0:
        given, refs = refs[:4], refs[4:]
    else:
        (feed, slopes), refs = refs[:2], refs[2:]
    weights, refs = refs[: 6 * count], refs[6 * count :]
    if stage == 0:
        grads_first, grads_second, feed, slopes, out_total, d_total = refs
    else:
        out_before, d_before, grads_first, grads_second, out_own, out_other, d_own, d_other = refs[:8]
        out_total, d_total = refs[8:]
    step = pl.program_id(0)
    tokens, model = feed.shape
    depth = model // count
    spans = [slice(place * depth, (place + 1) * depth) for place in range(count)]

    @pl.when(step == 0)
    def _():
        if stage == 0:
            spots = chip_spots(masks, depth)
            half = tokens // 2
            for target, (own, other) in ((feed, given[:2]), (slopes, given[2:])):
                for span, spot in zip(spans, spots):
                    target[:half, span] = cores_turned(own[:, spot].astype(F32)).astype(LOW)
                    target[half:, span] = cores_turned(other[:, spot].astype(F32)).astype(LOW)
            out_total[...] = jnp.zeros_like(out_total)
            d_total[...] = jnp.zeros_like(d_total)
        else:
            out_total[...] = out_before[...]
            d_total[...] = d_before[...]

    back = functools.partial(
        lax.dot_general, dimension_numbers=(((1,), (1,)), ((), ())), preferred_element_type=F32
    )

    def tile_step(pieces, grads_out):
        gate_part, up_part, down_part = [
            jnp.concatenate(
                [piece[...] for piece in pieces[kind * count : (kind + 1) * count]], axis=0
            )
            for kind in range(3)
        ]
        gate = jnp.dot(feed[...], gate_part, preferred_element_type=F32)
        upper = jnp.dot(feed[...], up_part, preferred_element_type=F32)
        d_inner = jnp.dot(slopes[...], down_part, preferred_element_type=F32)
        gate_sig = 1.0 / (1.0 + jnp.exp(-gate))
        gate_act = gate * gate_sig
        inner = (gate_act * upper).astype(LOW)
        d_gate = (d_inner * upper * gate_sig * (1.0 + gate * (1.0 - gate_sig))).astype(LOW)
        d_upper = (d_inner * gate_act).astype(LOW)
        grads_out[0] = d_gate
        grads_out[1] = d_upper
        grads_out[2] = inner
        out_total[...] += back(inner, down_part)
        d_total[...] += back(d_gate, gate_part) + back(d_upper, up_part)

    @pl.when(step < cuts[0])
    def _():
        tile_step(weights[: 3 * count], grads_first)

    @pl.when(step >= cuts[0])
    def _():
        tile_step(weights[3 * count :], grads_second)

    if stage:

        @pl.when(step == cuts[0] + cuts[1] - 1)
        def _():
            spots = chip_spots(masks, depth)
            half = tokens // 2
            for source, own, other in ((out_total, out_own, out_other), (d_total, d_own, d_other)):
                for span, spot in zip(spans, spots):
                    own[:, spot] = cores_turned(source[:half, span])
                    other[:, spot] = cores_turned(source[half:, span])


def feed_call(rows, piece_lists, before, masks, tile, after=()):
    tokens, depth = (2 * rows[0].shape[0] if before is None else rows[0].shape[0]), rows[0].shape[1]
    cuts = [pieces[0][0].shape[1] // (3 * tile) for pieces in piece_lists]
    block_rows = depth // len(piece_lists[0])
    count = len(piece_lists[0])
    first = lambda step: jnp.minimum(step, cuts[0] - 1)
    second = lambda step: jnp.maximum(step - cuts[0], 0)
    whole = pl.BlockSpec((tokens, depth), lambda step: (0, 0))
    single = pl.BlockSpec((tokens // 2, depth), lambda step: (0, 0))
    weights = [
        pl.BlockSpec(
            (block_rows, tile),
            lambda step, at=at, kind=kind, where=where, cut=cut: (at, kind * cut + where(step)),
        )
        for pieces, where, cut in zip(piece_lists, (first, second), cuts)
        for kind in range(3)
        for _, at in pieces
    ]
    both = jax.ShapeDtypeStruct((tokens, depth), F32)
    one = jax.ShapeDtypeStruct((tokens // 2, depth), F32)
    kept = jax.ShapeDtypeStruct((tokens, depth), LOW)
    return launch(
        functools.partial(feed_kernel, count, cuts, masks, 0 if before is None else 1),
        after,
        grid=(cuts[0] + cuts[1],),
        in_specs=([single] * 4 if before is None else [whole] * 2)
        + weights
        + ([] if before is None else [whole] * 2),
        out_specs=[
            pl.BlockSpec((3, tokens, tile), lambda step: (0, 0, first(step))),
            pl.BlockSpec((3, tokens, tile), lambda step: (0, 0, second(step))),
        ]
        + ([whole] * 4 if before is None else [single] * 4),
        out_shape=[
            jax.ShapeDtypeStruct((3, tokens, cuts[0] * tile), LOW),
            jax.ShapeDtypeStruct((3, tokens, cuts[1] * tile), LOW),
        ]
        + ([kept, kept, both, both] if before is None else [one] * 4),
        scratch_shapes=[]
        if before is None
        else [pltpu.VMEM((tokens, depth), F32), pltpu.VMEM((tokens, depth), F32)],
        cost_estimate=estimate(1, 1),
        operands=(
            *rows,
            *([array for array, _ in piece_lists[0]] * 3),
            *([array for array, _ in piece_lists[1]] * 3),
            *(before if before is not None else ()),
        ),
    )


def outer_kernel(count, kinds, starts, first_kind, *refs):
    sources = (refs[:count], refs[count : 2 * count])
    grads, arrived, out = refs[2 * count], refs[2 * count + 1 : -1], refs[-1]
    kind = pl.program_id(0) + first_kind
    depth = out.shape[0] // count

    def fill(source, added):
        for place in range(count):
            rows = slice(place * depth, (place + 1) * depth)
            total = lax.dot_general(
                source[place][...], grads[0], (((0,), (0,)), ((), ())),
                preferred_element_type=F32,
            )
            if added is not None:
                total = total + added[rows].astype(F32)
            out[rows] = total.astype(LOW)

    for which in range(2):
        wanted = (kind == kinds - 1) if which else (kind < kinds - 1)
        if not arrived:
            pl.when(wanted)(functools.partial(fill, sources[which], None))
        for place, added in enumerate(arrived):
            inside = kind >= starts[place]
            if place + 1 < len(arrived):
                inside = inside & (kind < starts[place + 1])
            pl.when(wanted & inside)(functools.partial(fill, sources[which], added))


def outer_call(sources, grads, places, span=None, arrived=(), starts=(0,), after=()):
    tokens, model = sources[0].shape
    kinds, _, width = grads.shape
    blocks = 2 * len(places)
    depth = model // blocks
    half = model // 2
    first_kind, stop = span or (0, kinds)
    last = stop - first_kind

    def own(place):
        return pl.BlockSpec((tokens, depth), lambda kind: (0, place))

    def added(array, start):
        most = array.shape[1] // width - 1
        return pl.BlockSpec(
            (half, width), lambda kind: (0, jnp.clip(kind + first_kind - start, 0, most))
        )

    return launch(
        functools.partial(outer_kernel, len(places), kinds, starts, first_kind),
        after,
        grid=(last,),
        in_specs=[own(place) for place in places] * 2
        + [pl.BlockSpec((1, tokens, width), lambda kind: (first_kind + kind, 0, 0))]
        + [added(array, start) for array, start in zip(arrived, starts)],
        out_specs=pl.BlockSpec((half, width), lambda kind: (0, kind)),
        out_shape=jax.ShapeDtypeStruct((half, last * width), LOW),
        cost_estimate=estimate(1, 1),
        operands=(
            *([sources[0]] * len(places)), *([sources[1]] * len(places)), grads, *arrived,
        ),
    )


def gather_kernel(
    group_size, bits, orders, cuts, feed_cuts, shard, feed, full, pair_first, pair_second, rest,
    own_sem, line_send, line_recv, tree_send, tree_recv, feed_send, feed_recv, core_send, core_recv,
):
    my_seq, my_group = lax.axis_index("seq"), lax.axis_index("grp")
    rows = shard.shape[0]
    levels = len(orders[0])

    def flipped(mask):
        place = my_seq
        for bit in bits:
            if mask & bit:
                place = place + bit - 2 * bit * lax.rem(my_seq // bit, 2)
        return place

    def remote(source, target, send_sem, recv_sem, device):
        return pltpu.make_async_remote_copy(
            src_ref=source, dst_ref=target, send_sem=send_sem, recv_sem=recv_sem,
            device_id=device, device_id_type=pl.DeviceIdType.MESH,
        )

    def greet(device):
        pl.semaphore_signal(
            barrier, inc=1, device_id=device, device_id_type=pl.DeviceIdType.MESH
        )

    def has(direction, steps):
        return my_group >= steps if direction == 0 else my_group + steps < group_size

    def beside(direction, steps):
        return my_group - steps if direction == 0 else my_group + steps

    barrier = pltpu.get_barrier_semaphore()
    for bit in bits:
        greet((flipped(bit), my_group))
    for direction in range(2):

        @pl.when(has(direction, 1))
        def _():
            greet((my_seq, beside(direction, 1)))

    pl.semaphore_wait(
        barrier,
        len(bits) + jnp.minimum(my_group, 1) + jnp.minimum(group_size - 1 - my_group, 1),
    )

    def place_of(mask, group):
        return pl.ds(pl.multiple_of((flipped(mask) * group_size + group) * rows, rows), rows)

    def line_copies(kind, direction, hop):
        origin = beside(direction, hop - 1)
        device = (my_seq, beside(1 - direction, 1))
        if kind == 0:
            views = [(shard if hop == 1 else full.at[place_of(0, origin)], full.at[place_of(0, origin)])]
            sems = (line_send, line_recv)
        else:
            spot = pl.ds(pl.multiple_of(origin * rows, rows), rows)
            parts = (pair_first, pair_second, rest)
            views = [
                (
                    feed.at[:, cut] if hop == 1 else part.at[spot],
                    part.at[spot],
                )
                for part, cut in zip(parts, feed_cuts)
            ]
            sems = (feed_send, feed_recv)
        return [
            remote(source, target, sems[0].at[direction, hop - 1, at], sems[1].at[direction, hop - 1, at], device)
            for at, (source, target) in enumerate(views)
        ]

    def line_send_now(kind, direction, hop):
        @pl.when(has(1 - direction, 1))
        def _():
            for copy in line_copies(kind, direction, hop):
                copy.start()

    def line_wait(kind, direction, hop):
        for copy in line_copies(kind, direction, hop):
            copy.wait_recv()

    def line_drain(kind):
        for direction in range(2):
            for hop in range(1, group_size):

                @pl.when(has(direction, hop - 1) & has(1 - direction, 1))
                def _():
                    for copy in line_copies(kind, direction, hop):
                        copy.wait_send()

    slots = [(0, 0)] + [(direction, hop) for hop in range(1, group_size) for direction in range(2)]

    def node_copy(slot, part, level, mask):
        direction, hop = slots[slot]
        origin = beside(direction, hop) if hop else my_group
        view = full.at[place_of(mask, origin), cuts[part]]
        source = shard.at[:, cuts[part]] if hop == 0 and mask == 0 else view
        node = 2**level - 1 + masks_of(orders[part][:level]).index(mask)
        return remote(
            source, view, tree_send.at[slot, part, node], tree_recv.at[slot, part, node],
            (flipped(orders[part][level]), my_group),
        )

    def stage(slot, lag):
        direction, hop = slots[slot]
        if lag == 0:
            if hop:
                line_wait(0, direction, hop)
                if hop + 1 < group_size:
                    line_send_now(0, direction, hop + 1)
            for part in range(2):
                for level in range(levels):
                    node_copy(slot, part, level, 0).start()
        else:
            level = lag - 1
            for part in range(2):
                for mask in masks_of(orders[part][:level]):
                    node_copy(slot, part, level, mask).wait_recv()
                    for later in range(level + 1, levels):
                        node_copy(slot, part, later, mask ^ orders[part][level]).start()

    def when_held(slot, work):
        direction, hop = slots[slot]
        if hop == 0:
            work()
        else:
            pl.when(has(direction, hop))(work)

    own = pltpu.make_async_copy(shard, full.at[place_of(0, my_group)], own_sem.at[0])
    own.start()
    spot = pl.ds(pl.multiple_of(my_group * rows, rows), rows)
    own_feed = [
        pltpu.make_async_copy(feed.at[:, cut], part.at[spot], own_sem.at[1 + at])
        for at, (part, cut) in enumerate(zip((pair_first, pair_second, rest), feed_cuts))
    ]
    for copy in own_feed:
        copy.start()
    for direction in range(2):
        line_send_now(0, direction, 1)
    def feed_hop(hop):
        for direction in range(2):

            @pl.when(has(direction, hop))
            def _():
                line_wait(1, direction, hop)
                if hop + 1 < group_size:
                    line_send_now(1, direction, hop + 1)

    def at_lag(slot, lag):
        when_held(slot, functools.partial(stage, slot, lag))

    at_lag(0, 0)
    for hop in range(1, group_size):
        at_lag(2 * hop - 1, 0)
        at_lag(2 * hop, 0)
        if hop == group_size - 2:
            for direction in range(2):
                line_send_now(1, direction, 1)
        for slot in [0] if hop == 1 else [2 * hop - 3, 2 * hop - 2]:
            at_lag(slot, 1)
    for slot in range(max(2 * group_size - 3, 0), len(slots)):
        at_lag(slot, 1)
    hop_now = 1
    for lag in range(2, levels):
        for slot in range(len(slots)):
            if slot % 3 == 0 and hop_now < group_size:
                feed_hop(hop_now)
                hop_now = hop_now + 1
            at_lag(slot, lag)
    for hop in range(hop_now, group_size):
        feed_hop(hop)
    line_drain(1)
    for copy in own_feed:
        copy.wait()
    half = rest.shape[0]
    first_width = pair_first.shape[1]
    swaps = [
        remote(
            rest.at[:, cut], part.at[pl.ds(half, half)], core_send.at[at], core_recv.at[at],
            (flipped(1), my_group),
        )
        for at, (part, cut) in enumerate(
            (
                (pair_first, pl.ds(0, first_width)),
                (pair_second, pl.ds(first_width, pair_second.shape[1])),
            )
        )
    ]
    for copy in swaps:
        copy.start()
    for slot in range(len(slots)):
        when_held(slot, functools.partial(stage, slot, levels))
    for copy in swaps:
        copy.wait()
    own.wait()
    line_drain(0)

    def drain(slot):
        for part in range(2):
            for level in range(levels):
                for mask in masks_of(orders[part][:level]):
                    node_copy(slot, part, level, mask).wait_send()

    for slot in range(len(slots)):
        when_held(slot, functools.partial(drain, slot))


def gather_call(shard, feed, cuts, feed_cuts, orders, collective_id):
    group_size, seq_size = lax.axis_size("grp"), lax.axis_size("seq")
    rows, width = shard.shape
    bits = [1] + chip_bits()
    nodes = 2 ** len(bits) - 1
    slots = 2 * group_size - 1
    first_width, second_width = feed_cuts[0].size, feed_cuts[1].size
    any_space = pl.BlockSpec(memory_space=pl.ANY)
    dma = pltpu.SemaphoreType.DMA
    return pl.pallas_call(
        functools.partial(gather_kernel, group_size, bits, orders, cuts, feed_cuts),
        in_specs=[any_space] * 2,
        out_specs=[any_space] * 4,
        out_shape=[
            jax.ShapeDtypeStruct((rows * group_size * seq_size, width), LOW),
            jax.ShapeDtypeStruct((2 * rows * group_size, first_width), LOW),
            jax.ShapeDtypeStruct((2 * rows * group_size, second_width), LOW),
            jax.ShapeDtypeStruct((rows * group_size, first_width + second_width), LOW),
        ],
        scratch_shapes=[
            dma((4,)),
            dma((2, group_size - 1, 1)), dma((2, group_size - 1, 1)),
            dma((slots, 2, nodes)), dma((slots, 2, nodes)),
            dma((2, group_size - 1, 3)), dma((2, group_size - 1, 3)),
            dma((2,)), dma((2,)),
        ],
        cost_estimate=estimate(1.5e11, 1e8),
        compiler_params=pltpu.CompilerParams(collective_id=collective_id, has_side_effects=True),
    )(shard, feed)


def reduce_kernel(waited, group_size, all_orders, groups, *refs):
    refs = refs[waited:]
    sets = len(groups)
    inputs, refs = refs[: 4 * sets + 1], refs[4 * sets + 1 :]
    totals, everywhere, refs = refs[:sets], refs[sets], refs[sets + 1 :]
    buffers, refs = refs[: 5 * sets], refs[5 * sets :]
    vector_out, vector_in = refs[:2]
    send_sem, recv_sem, core_send, core_recv, line_send, line_recv, v_send, v_recv = refs[2:]
    my_seq, my_group = lax.axis_index("seq"), lax.axis_index("grp")
    peers = [lax.rem(my_group + step, group_size) for step in range(1, group_size)]
    most = max(len(orders[0]) for orders in all_orders)
    bits = [1] + max(all_orders, key=lambda orders: len(orders[0]))[1]
    units = [(place, group) for place in range(sets) for group in range(groups[place])]
    half = inputs[0].shape[0] // 2 ** len(all_orders[0][0])
    rows = half // group_size

    def partner(bit):
        return my_seq + bit - 2 * bit * lax.rem(my_seq // bit, 2)

    def greet(device):
        pl.semaphore_signal(
            barrier, inc=1, device_id=device, device_id_type=pl.DeviceIdType.MESH
        )

    barrier = pltpu.get_barrier_semaphore()
    for bit in bits:
        greet((partner(bit), my_group))
    for peer in peers:
        greet((my_seq, peer))
    pl.semaphore_wait(barrier, len(bits) + len(peers))

    def remote(source, target, send, recv, device):
        return pltpu.make_async_remote_copy(
            src_ref=source, dst_ref=target, send_sem=send, recv_sem=recv,
            device_id=device, device_id_type=pl.DeviceIdType.MESH,
        )

    def orders_of(unit):
        return all_orders[units[unit][0]]

    def held(unit, level):
        return inputs[4 * units[unit][0]].shape[0] // 2**level

    def begins(unit, level):
        return sum(held(unit, before) for before in range(level))

    def parts_of(unit):
        place, group = units[unit]
        given, own = inputs[4 * place : 4 * place + 4], buffers[5 * place : 5 * place + 5]
        return given, (own[:2], own[2], own[3], own[4]), group

    def chip_copy(unit, part, level):
        given, (arrived, _, _, _), group = parts_of(unit)
        width = arrived[part].shape[-1]
        count = held(unit, level)
        order = orders_of(unit)[part]
        if level == 0:
            source = given[part].at[:, pl.ds(group * width, width)]
        else:
            source = arrived[part].at[group, pl.ds(begins(unit, level - 1) + count, count)]
        return remote(
            source,
            arrived[part].at[group, pl.ds(begins(unit, level), count)],
            send_sem.at[unit, part, level],
            recv_sem.at[unit, part, level],
            (partner(order[len(order) - 1 - level]), my_group),
        )

    def core_copy(unit):
        _, (_, chip_total, core_in, _), group = parts_of(unit)
        return remote(
            chip_total.at[group, pl.ds(half, half)],
            core_in.at[group],
            core_send.at[unit],
            core_recv.at[unit],
            (partner(1), my_group),
        )

    def block_at(group):
        return pl.ds(group * rows, rows)

    def line_copy(unit, side, sender, target):
        _, (_, chip_total, core_in, line_in), group = parts_of(unit)
        source = (chip_total, core_in)[side].at[group, block_at(target)]
        receiver = sender + 1 if target > sender else sender - 1
        spot = group_size if target == receiver < sender else target
        return remote(
            source,
            line_in.at[group, spot, side],
            line_send.at[unit, spot, side],
            line_recv.at[unit, spot, side],
            (my_seq, receiver),
        )

    def line_step(unit, place, hop, up):
        _, (_, chip_total, core_in, line_in), group = parts_of(unit)
        targets = range(place + 1, group_size) if up else range(place)
        for target in targets:
            for side, source in enumerate((chip_total, core_in)):
                if hop:
                    line_copy(unit, side, place - 1 if up else place + 1, target).wait_recv()
                    value = source[group, target * rows : (target + 1) * rows].astype(F32)
                    value = value + line_in[group, target, side].astype(F32)
                    source[group, target * rows : (target + 1) * rows] = value.astype(LOW)
                line_copy(unit, side, place, target).start()

    def line_hop(unit, hop):
        for up, place in ((True, hop), (False, group_size - 1 - hop)):

            @pl.when(my_group == place)
            def _():
                line_step(unit, place, hop, up)

    def line_end(unit, place):
        _, (_, chip_total, core_in, line_in), group = parts_of(unit)
        total = totals[units[unit][0]]
        both = chip_total.shape[-1]
        for side, source in enumerate((chip_total, core_in)):
            value = source[group, place * rows : (place + 1) * rows].astype(F32)
            if place > 0:
                line_copy(unit, side, place - 1, place).wait_recv()
                value = value + line_in[group, place, side].astype(F32)
            if place + 1 < group_size:
                line_copy(unit, side, place + 1, place).wait_recv()
                value = value + line_in[group, group_size, side].astype(F32)
            spot = (group * 2 + side) * both
            total[:, spot : spot + both] = value

    def line_drain(unit, place):
        for target in range(group_size):
            if target != place:
                for side in range(2):
                    line_copy(unit, side, place, target).wait_send()

    def stage(unit, lag):
        given, (arrived, chip_total, core_in, line_in), group = parts_of(unit)
        levels = len(orders_of(unit)[0])
        widths = [buffer.shape[-1] for buffer in arrived]
        if lag == 0:
            for part in range(2):
                chip_copy(unit, part, 0).start()
        elif lag <= levels:
            level = lag - 1
            for part in range(2):
                chip_copy(unit, part, level).wait_recv()
                count, width = held(unit, level), widths[part]

                def added(low, high):
                    base = begins(unit, level)
                    value = arrived[part][group, base + low : base + high].astype(F32)
                    if level == 0:
                        kept = given[2 + part][low:high, group * width : (group + 1) * width]
                    else:
                        before = begins(unit, level - 1)
                        kept = arrived[part][group, before + low : before + high]
                    return value + kept.astype(F32)

                if lag < levels:
                    middle = count // 2
                    base = begins(unit, level)
                    arrived[part][group, base + middle : base + count] = added(
                        middle, count
                    ).astype(LOW)
                    chip_copy(unit, part, level + 1).start()
                    arrived[part][group, base : base + middle] = added(0, middle).astype(LOW)
                else:
                    at = part * widths[0]
                    chip_total[group, :, at : at + width] = added(0, count).astype(LOW)
            if lag == levels:
                core_copy(unit).start()
        elif lag == levels + 1:
            core_copy(unit).wait_recv()
            if group_size > 1:
                line_hop(unit, 0)
        else:
            line_hop(unit, lag - levels - 1)

    def vector_copies(step):
        if step < len(bits):
            return [
                remote(
                    vector_out.at[step], vector_in.at[step], v_send.at[step], v_recv.at[step],
                    (partner(bits[step]), my_group),
                )
            ]
        return [
            remote(
                vector_out.at[step], vector_in.at[step + at], v_send.at[step + at],
                v_recv.at[step + at], (my_seq, peer),
            )
            for at, peer in enumerate(peers)
        ]

    def vector_step(step):
        if step:
            for copy in vector_copies(step - 1):
                copy.wait_recv()
        if step == 0:
            vector_out[0] = inputs[-1][...]
        elif step <= len(bits):
            vector_out[step] = vector_out[step - 1] + vector_in[step - 1]
        else:
            value = vector_out[len(bits)]
            for at in range(len(peers)):
                value = value + vector_in[len(bits) + at]
            everywhere[...] = value
        if step <= len(bits):
            for copy in vector_copies(step):
                copy.start()

    last_step = len(units) + most + group_size - 1
    ahead = AHEAD
    for unit in range(min(ahead, len(units))):
        stage(unit, 0)
    for step in range(last_step):
        if step + ahead < len(units):
            stage(step + ahead, 0)
        for lag in range(1, most + group_size):
            unit = step - lag
            if 0 <= unit < len(units) and lag < len(orders_of(unit)[0]) + max(group_size, 2):
                stage(unit, lag)
        if step <= len(bits) + 1:
            vector_step(step)
    for step in range(last_step, len(bits) + 2):
        vector_step(step)
    for place in range(group_size):

        @pl.when(my_group == place)
        def _():
            for unit in range(len(units)):
                line_end(unit, place)
    for step in range(len(bits) + 1):
        for copy in vector_copies(step):
            copy.wait_send()
    for unit in range(len(units)):
        for part in range(2):
            for level in range(len(orders_of(unit)[0])):
                chip_copy(unit, part, level).wait_send()
        core_copy(unit).wait_send()
    for place in range(group_size):

        @pl.when(my_group == place)
        def _():
            for unit in range(len(units)):
                line_drain(unit, place)


def reduce_call(sets, vector, collective_id, after=()):
    group_size = lax.axis_size("grp")
    groups = [group for _, _, group, _ in sets]
    all_orders = [orders for _, _, _, orders in sets]
    half = sets[0][0][0].shape[0] // 2 ** len(all_orders[0][0])
    rows = half // group_size
    units = sum(groups)
    most = max(len(orders[0]) for orders in all_orders)
    bits = most + 1
    in_vmem = pl.BlockSpec(memory_space=pltpu.VMEM)
    in_any = pl.BlockSpec(memory_space=pl.ANY)
    dma = pltpu.SemaphoreType.DMA
    scratch, operands, results = [], [], []
    for lowers, uppers, group, orders in sets:
        depth = lowers[0].shape[0]
        held_all = sum(depth // 2**level for level in range(len(orders[0])))
        widths = [lower.shape[1] // group for lower in lowers]
        both = sum(widths)
        operands += [*lowers, *uppers]
        scratch += [pltpu.VMEM((group, held_all, width), LOW) for width in widths]
        scratch += [
            pltpu.VMEM((group, 2 * half, both), LOW),
            pltpu.VMEM((group, half, both), LOW),
            pltpu.VMEM((group, group_size + 1, 2, rows, both), LOW),
        ]
        results.append(jax.ShapeDtypeStruct((rows, group * 2 * both), F32))
    return pl.pallas_call(
        functools.partial(reduce_kernel, len(after), group_size, all_orders, groups),
        in_specs=[in_any] * len(after) + [in_any, in_any, in_vmem, in_vmem] * len(sets) + [in_vmem],
        out_specs=[in_vmem] * (len(sets) + 1),
        out_shape=results + [jax.ShapeDtypeStruct(vector.shape, F32)],
        scratch_shapes=scratch
        + [
            pltpu.VMEM((bits + 1,) + vector.shape, F32),
            pltpu.VMEM((bits + group_size,) + vector.shape, F32),
            dma((units, 2, most)), dma((units, 2, most)),
            dma((units,)), dma((units,)),
            dma((units, group_size + 1, 2)), dma((units, group_size + 1, 2)),
            dma((bits + group_size,)), dma((bits + group_size,)),
        ],
        cost_estimate=estimate(1, 1),
        compiler_params=pltpu.CompilerParams(
            collective_id=collective_id, has_side_effects=True, vmem_limit_bytes=VMEM_LIMIT
        ),
    )(*after, *operands, vector)


def local(
    tokens,
    cotangent,
    lengths,
    pad_mask,
    mixer_gain,
    query_weight,
    key_weight,
    value_weight,
    conv_query,
    conv_key,
    conv_value,
    beta_weight,
    beta_bias,
    head_gain,
    out_weight,
    feed_gain,
    gate_weight,
    up_weight,
    down_weight,
):
    row_count, model_width = tokens.shape
    head_count = beta_bias.shape[0]
    head_width = head_gain.shape[0]
    tap_count = conv_query.shape[1]
    hidden_units = gate_weight.shape[1]
    my_core = lax.rem(lax.axis_index("seq"), 2)
    chip = chip_bits()
    chip_orders = (list(reversed(chip)), list(chip))
    plain_orders = [order + [1] for order in chip_orders]
    plain_masks = [masks_of(order) for order in plain_orders]
    pair_masks = [masks_of([1] + order) for order in chip_orders]

    def along_groups(shard):
        return lax.all_gather(shard, "grp", axis=0, tiled=True)

    small_shard = jnp.concatenate(
        [mixer_gain[:, None], feed_gain[:, None], conv_query, conv_key, conv_value, beta_weight],
        axis=1,
    )
    small_width = small_shard.shape[1]
    padded_small = jnp.pad(small_shard, ((0, 0), (0, -small_width % 128)))
    plain_shard = jnp.concatenate(
        [query_weight, key_weight, value_weight, out_weight, padded_small], axis=1
    )
    plain_cut = 2 * model_width
    plain_cuts = (pl.ds(0, plain_cut), pl.ds(plain_cut, plain_shard.shape[1] - plain_cut))
    unit_width = hidden_units // 2
    tile = tile_of(unit_width, 256)
    tiles = unit_width // tile
    early_tiles = -(-tiles // 2)
    rest = tiles - early_tiles
    counts = [-(-early_tiles // 2), early_tiles // 2, -(-rest // 2), rest // 2]
    edges = [sum(counts[:place]) * tile for place in range(5)]
    spans = list(zip(edges[:-1], edges[1:]))
    feed_shards = (gate_weight, up_weight, down_weight)

    def units_of(core, start, stop):
        return [
            lax.dynamic_slice_in_dim(shard, core * unit_width + start, stop - start, 1)
            for shard in feed_shards
        ]

    feed_shard = jnp.concatenate(
        [
            part
            for core in (my_core, 1 - my_core)
            for start, stop in spans[:2]
            for part in units_of(core, start, stop)
        ],
        axis=1,
    )
    widths = [3 * (stop - start) for start, stop in spans]
    feed_cuts = (
        pl.ds(0, widths[0]),
        pl.ds(widths[0], widths[1]),
        pl.ds(widths[0] + widths[1], widths[0] + widths[1]),
    )
    tokens_before = jnp.concatenate(
        [
            jnp.zeros((HALO - (tap_count - 1), model_width), tokens.dtype),
            passed_along(tokens[row_count - (tap_count - 1) :], ("seq", "grp"), 1),
        ],
        axis=0,
    )
    full, pair_first, pair_second, _ = gather_call(
        plain_shard, feed_shard, plain_cuts, feed_cuts, plain_orders, 2
    )
    w_qkv, w_out = full[:, : 3 * model_width], full[:, 3 * model_width : 4 * model_width]
    small = columns(full, 4 * model_width, 128)
    gain_mixer, gain_feed = small[:, 0], small[:, 1]
    c_query = small[:, 2 : 2 + tap_count]
    c_key = small[:, 2 + tap_count : 2 + 2 * tap_count]
    c_value = small[:, 2 + 2 * tap_count : 2 + 3 * tap_count]
    w_beta = small[:, 2 + 3 * tap_count : small_width]

    feed_blocks = [
        along_groups(
            tied(
                jnp.concatenate(
                    [part for start, stop in spans[2:] for part in units_of(core, start, stop)],
                    axis=1,
                ),
                full,
            )
        )
        for core in (1 - my_core, my_core)
    ]
    theirs_block = swapped(feed_blocks[0], 1)
    feed_pieces = [
        spread_views(pair_first, chip_orders[0], True),
        spread_views(pair_second, chip_orders[1], True),
    ]
    out_half = model_width // 2
    qkv_half = 3 * model_width // 2

    anchor = lax.axis_index(("seq", "grp")) * row_count
    places = anchor + jnp.arange(row_count, dtype=jnp.int32)
    starts = jnp.cumsum(lengths) - lengths
    row_start = jnp.max(jnp.where(starts[None, :] <= places[:, None], starts[None, :], 0), axis=1)
    valid = [
        (places - offset >= row_start).astype(jnp.float32) for offset in range(1, tap_count)
    ]
    live_rows = pad_mask.astype(jnp.float32)
    inputs32 = tokens.astype(jnp.float32)
    normed_a, norm_a_back = jax.vjp(rms_scale, inputs32, gain_mixer.astype(jnp.float32))
    normed_low = normed_a.astype(jnp.bfloat16)
    normed_before = rms_scale(tokens_before.astype(F32), gain_mixer.astype(F32)).astype(LOW)
    extended = jnp.dot(
        jnp.concatenate([normed_before, normed_low], axis=0), w_qkv, preferred_element_type=F32
    ).astype(LOW)
    logit_part = jnp.dot(normed_low, w_beta, preferred_element_type=jnp.float32)
    sigmoid_val = jax.nn.sigmoid(logit_part + beta_bias)
    beta_rows = sigmoid_val * live_rows[:, None]
    taps = jnp.pad(
        jnp.transpose(jnp.concatenate([c_query, c_key, c_value], axis=0).astype(jnp.float32)),
        ((0, 8 - tap_count), (0, 0)),
    )
    flags = jnp.stack(
        [
            (row_start < anchor).astype(jnp.float32),
            (row_start == row_start[-1]).astype(jnp.float32),
            live_rows,
        ]
        + valid,
        axis=1,
    )
    inverse, wy, scores, reach, local_out, pairs = span_call(
        row_start,
        flags,
        beta_rows,
        extended,
        taps,
        tap_count,
        head_count,
        after=(feed_pieces[0][1][0], feed_pieces[1][1][0]),
    )
    ready = (pairs, feed_pieces[0][-1][0], feed_pieces[1][-1][0])
    edge = 0
    for place, width in enumerate(widths[2:]):
        paired = join_columns(feed_blocks[1], theirs_block, edge, width, ready)
        feed_pieces.append(spread_views(paired, chip_orders[place], False))
        edge = edge + width
    start_states = scan_call(pairs, False, 0)
    mixed, head_low = mixed_call(
        reach,
        local_out,
        start_states,
        head_gain,
        flags,
        after=tuple(feed_pieces[place][at][0] for place in (2, 3) for at in (1, 2)),
    )
    hidden_one = inputs32 + jnp.dot(head_low, w_out, preferred_element_type=F32)
    normed_f, norm_f_back = jax.vjp(rms_scale, hidden_one, gain_feed.astype(jnp.float32))
    feed_low = normed_f.astype(jnp.bfloat16)
    depth = model_width // len(feed_pieces[0])
    second_places = [pair_masks[1][::2].index(mask) for mask in pair_masks[0][::2]]
    first_places = [pair_masks[0][::2].index(mask) for mask in pair_masks[1][::2]]
    chip_count = len(feed_pieces[0])
    half_places = [
        [list(range(chip_count // 2)), list(range(chip_count // 2, chip_count))],
        [first_places[: chip_count // 2], first_places[chip_count // 2 :]],
    ]
    rows = (feed_low, swapped(feed_low, 1), cotangent, swapped(cotangent, 1))
    chip_masks = [mask // 2 for mask in pair_masks[0][::2]]
    before = None
    feed_grads, lower_halves = [], []

    def feed_lower(chunk, after):
        return [
            outer_call(sources, feed_grads[2 * chunk + part], half_places[part][1], after=after)
            for part in range(2)
        ]

    def feed_sent(chunk, lowers):
        return [swapped(lower, chip_orders[part][-1]) for part, lower in enumerate(lowers)]

    for chunk in range(2):
        grads_first, grads_second, *results = feed_call(
            rows,
            [
                feed_pieces[2 * chunk],
                [feed_pieces[2 * chunk + 1][place] for place in second_places],
            ],
            before,
            chip_masks,
            tile,
            after=lower_halves,
        )
        if chunk == 0:
            rows, before = results[:2], results[2:]
            sources = rows
        feed_grads += [grads_first, grads_second]
        if chunk == 0:
            lower_halves = feed_lower(0, ())
            sent = feed_sent(0, lower_halves)
    out_own, out_other, d_own, d_other = results
    d_feed = d_own + swapped(d_other, 1)
    block_out = (hidden_one + (out_own + swapped(out_other, 1))).astype(jnp.bfloat16)
    grad_out = cotangent.astype(jnp.float32)
    d_hidden_part, d_gain_feed = norm_f_back(d_feed)
    d_hidden = grad_out + d_hidden_part
    d_attn = d_hidden.astype(jnp.bfloat16)
    d_head = contract_rows(
        d_attn, full, 3 * model_width, after=lower_halves
    )

    def feed_upper(place, arrived, after):
        return outer_call(
            sources, feed_grads[place], half_places[place % 2][0], None, (arrived,), (0,), after
        )

    def chip_sum(total, part, after):
        for bit in reversed(chip_orders[part][:-1]):
            total = halved_sum(total, bit, after)
        return total

    def both_owners(totals):
        half = totals[0].shape[0] // 2
        mine = [total[:half] for total in totals]
        theirs = [swapped(total[half:], 1) for total in totals]
        return jnp.concatenate(mine + theirs, axis=1)

    def both_halves(grads):
        width = grads.shape[1] // 2
        mine = lax.dynamic_slice_in_dim(grads, my_core * width, width, 1)
        theirs = lax.dynamic_slice_in_dim(grads, (1 - my_core) * width, width, 1)
        return jnp.concatenate([mine, swapped(theirs, 1)], axis=0)

    d_mixed, d_head_gain, back_pairs = pull_call(
        reach, mixed, d_head, head_gain, flags, pairs
    )
    end_states = scan_call(back_pairs, True, 1)
    upper_first = [feed_upper(place, sent[place], (end_states,)) for place in range(2)]
    both_attn = both_halves(d_attn)
    plain_sources = [
        relative(jnp.concatenate([rows, swapped(rows, 1)], axis=0), pair_masks[0])
        for rows in (normed_low, head_low)
    ]
    d_rows, d_tail, d_before, d_taps, d_betas = back_call(
        row_start,
        flags,
        beta_rows,
        extended,
        taps,
        tap_count,
        inverse,
        wy,
        scores,
        start_states,
        end_states,
        d_mixed,
        after=upper_first,
    )
    d_logit32 = d_betas * live_rows[:, None] * sigmoid_val * (1.0 - sigmoid_val)
    d_logit = d_logit32.astype(jnp.bfloat16)
    lower_second = feed_lower(1, (d_betas,))
    sent_second = feed_sent(1, lower_second)
    chip_first = [
        chip_sum(total, part, lower_second) for part, total in enumerate(upper_first)
    ]
    early_rows = both_owners(chip_first)
    from_next = passed_along(
        d_before[:, 9 - tap_count :].astype(jnp.bfloat16), ("seq", "grp"), -1
    ).astype(jnp.float32)
    fixed = d_tail.at[:, 9 - tap_count :].add(from_next).astype(LOW)
    d_pre = jnp.concatenate(
        [
            jnp.concatenate([d_rows[kind, : row_count - 8], fixed[kind]], axis=0)
            for kind in range(3)
        ],
        axis=1,
    )
    d_kernel = jnp.concatenate(
        [jnp.transpose(d_taps[kind, :tap_count]) for kind in range(3)], axis=0
    )
    both_pre = both_halves(d_pre)
    fine = model_width // 4

    def plain_grads(part):
        kinds = [
            both_pre[:, (3 * part + kind) * fine : (3 * part + kind + 1) * fine]
            for kind in range(3)
        ]
        return jnp.stack(kinds + [both_attn[:, part * fine : (part + 1) * fine]])

    plain_slopes = [plain_grads(part) for part in range(2)]
    plain_lower = [
        outer_call(plain_sources, plain_slopes[part], half_places[part][1], after=chip_first)
        for part in range(2)
    ]
    plain_upper = [
        outer_call(plain_sources, plain_slopes[part], half_places[part][0], after=plain_lower)
        for part in range(2)
    ]
    d_normed = contract(d_logit, w_beta) + contract_rows(
        d_pre, full, 0, after=(*plain_upper, early_rows)
    )
    upper_second = [
        feed_upper(2 + part, sent_second[part], (d_normed,)) for part in range(2)
    ]
    feed_early = over_groups(early_rows)
    d_input_part, d_gain_mixer = norm_a_back(d_normed)
    input_grad = (d_hidden + d_input_part).astype(jnp.bfloat16)
    small_grads = jnp.concatenate(
        [
            lax.dot_general(
                normed_low, d_logit, (((0,), (0,)), ((), ())), preferred_element_type=F32
            ),
            d_kernel[:model_width],
            d_kernel[model_width : 2 * model_width],
            d_kernel[2 * model_width :],
            d_gain_mixer[:, None],
            d_gain_feed[:, None],
        ],
        axis=1,
    )
    small_both = jnp.pad(
        jnp.where(my_core == 0, small_grads + swapped(small_grads, 1), 0.0).astype(LOW),
        ((0, 0), (0, 128 - small_grads.shape[1])),
    )
    block_rows = model_width // lax.axis_size("seq")
    small_blocks = [
        lax.dynamic_slice_in_dim(
            small_both, (lax.axis_index("seq") ^ mask) * block_rows, block_rows, 0
        )
        for mask in pair_masks[0]
    ]
    half_blocks = len(small_blocks) // 2
    small_upper = jnp.concatenate(small_blocks[:half_blocks], axis=0)
    small_lower = jnp.concatenate(small_blocks[half_blocks:], axis=0)
    vector = jnp.concatenate([d_head_gain[0], jnp.sum(d_logit32, axis=0)])
    padded = jnp.zeros((8, 256), F32).at[0, : vector.shape[0]].set(vector)
    rest_orders = [order[:-1] for order in chip_orders]
    rest_half = upper_second[0].shape[0] // 2
    feed_late, plain_sum, small_sum, everywhere = reduce_call(
        [
            (
                [total[rest_half:] for total in upper_second],
                [total[:rest_half] for total in upper_second],
                6,
                rest_orders,
            ),
            (plain_lower, plain_upper, 16, chip_orders),
            ((small_lower, small_lower), (small_upper, small_upper), 1, chip_orders),
        ],
        padded,
        3,
    )
    replicated = everywhere[0, : vector.shape[0]]

    def in_order(mine, other):
        return jnp.concatenate(
            [jnp.where(my_core == 0, mine, other), jnp.where(my_core == 0, other, mine)], axis=1
        )

    fine = fine // 4
    groups = [plain_sum[:, at * fine : (at + 1) * fine] for at in range(64)]
    qkv_grad, out_grad = [
        in_order(
            *[
                jnp.concatenate(
                    [
                        groups[4 * group + 2 * owner + part]
                        for part in range(2)
                        for group in range(*span)
                    ],
                    axis=1,
                )
                for owner in range(2)
            ]
        )
        for span in ((0, 12), (12, 16))
    ]
    feed_sums = []
    for kind in range(3):
        halves = []
        for owner in range(2):
            at = owner * feed_early.shape[1] // 2
            for start, stop in spans[:2]:
                width = stop - start
                halves.append(feed_early[:, at + kind * width : at + (kind + 1) * width])
                at = at + 3 * width
            late = [(stop - start) // 2 for start, stop in spans[2:]]
            for part in range(2):
                for group in (2 * kind, 2 * kind + 1):
                    at = (2 * group + owner) * sum(late) + part * late[0]
                    halves.append(feed_late[:, at : at + late[part]])
        feed_sums.append(
            in_order(jnp.concatenate(halves[:6], axis=1), jnp.concatenate(halves[6:], axis=1))
        )
    gate_grad, up_grad, down_grad = feed_sums
    sharded = jnp.where(my_core == 0, small_sum[:, :128], small_sum[:, 256:384])
    taps_at = head_count + 3 * tap_count
    return (
        block_out,
        input_grad,
        sharded[:, taps_at],
        qkv_grad[:, :model_width],
        qkv_grad[:, model_width : 2 * model_width],
        qkv_grad[:, 2 * model_width :],
        sharded[:, head_count : head_count + tap_count],
        sharded[:, head_count + tap_count : head_count + 2 * tap_count],
        sharded[:, head_count + 2 * tap_count : taps_at],
        sharded[:, :head_count],
        replicated[head_width:],
        replicated[:head_width],
        out_grad,
        sharded[:, taps_at + 1],
        gate_grad,
        up_grad,
        down_grad,
    )


def solution(mesh):
    placed = (
        P(("seq", "grp"), None),
        P(("seq", "grp"), None),
        P(),
        P(("seq", "grp")),
        P(("seq", "grp")),
        P(("seq", "grp"), None),
        P(("seq", "grp"), None),
        P(("seq", "grp"), None),
        P(("seq", "grp"), None),
        P(("seq", "grp"), None),
        P(("seq", "grp"), None),
        P(("seq", "grp"), None),
        P(),
        P(),
        P(("seq", "grp"), None),
        P(("seq", "grp")),
        P(("seq", "grp"), None),
        P(("seq", "grp"), None),
        P(("seq", "grp"), None),
    )
    return jax.shard_map(
        local,
        mesh=mesh,
        in_specs=placed,
        out_specs=(
            P(("seq", "grp"), None),
            P(("seq", "grp"), None),
            P(("seq", "grp")),
            P(("seq", "grp"), None),
            P(("seq", "grp"), None),
            P(("seq", "grp"), None),
            P(("seq", "grp"), None),
            P(("seq", "grp"), None),
            P(("seq", "grp"), None),
            P(("seq", "grp"), None),
            P(),
            P(),
            P(("seq", "grp"), None),
            P(("seq", "grp")),
            P(("seq", "grp"), None),
            P(("seq", "grp"), None),
            P(("seq", "grp"), None),
        ),
        check_vma=False,
    )
```

```python
import functools

import jax
import jax.numpy as jnp
from jax import lax
from jax.experimental import pallas as pl
from jax.experimental.pallas import tpu as pltpu
from jax.sharding import PartitionSpec as P

F32 = jnp.float32
LOW = jnp.bfloat16
EPSILON = 1e-06
VMEM_LIMIT = 56 * 1024 * 1024
SPAN_HEADS = 4
BACK_HEADS = 2
HALO = 16
AHEAD = 1


def passed_along(value, axis, steps):
    count = lax.axis_size(axis)
    first, last = (max(0, -steps), min(count, count - steps))
    return lax.ppermute(value, axis, [(source, source + steps) for source in range(first, last)])


def rms_scale(values, gain):
    return values * lax.rsqrt(jnp.mean(values * values, axis=-1, keepdims=True) + EPSILON) * gain


def contract(left, right):
    return lax.dot_general(
        left, right, (((1,), (1,)), ((), ())), preferred_element_type=jnp.float32
    )


def launch(kernel, after, in_specs, operands, **options):
    count = len(after)

    def body(*refs):
        kernel(*refs[count:])

    return pl.pallas_call(
        body,
        in_specs=[pl.BlockSpec(memory_space=pl.ANY)] * count + list(in_specs),
        compiler_params=pltpu.CompilerParams(vmem_limit_bytes=VMEM_LIMIT),
        **options,
    )(*after, *operands)


def estimate(flops, moved, steps=0):
    return pl.CostEstimate(flops=1, bytes_accessed=1, transcendentals=0)


def split_low(value):
    upper = value.astype(LOW)
    return (upper, (value - upper.astype(F32)).astype(LOW))


def dot_one(left, right, dims=((1,), (0,))):
    return lax.dot_general(
        left.astype(LOW), right.astype(LOW), (dims, ((), ())), preferred_element_type=F32
    )


def dot_three(left, right, dims=((1,), (0,))):
    left_high, left_rest = split_low(left)
    right_high, right_rest = split_low(right)
    both = functools.partial(
        lax.dot_general, dimension_numbers=(dims, ((), ())), preferred_element_type=F32
    )
    return both(left_high, right_high) + (both(left_high, right_rest) + both(left_rest, right_high))


ROWS_ROWS = ((1,), (1,))
FIRST_FIRST = ((0,), (0,))


def inverse_unit_lower(lowers, size):
    row = lax.broadcasted_iota(jnp.int32, (size, size), 0)
    column = lax.broadcasted_iota(jnp.int32, (size, size), 1)
    eye = jnp.where(row == column, 1.0, 0.0).astype(F32)
    inverses = [eye for _ in lowers]
    span = 1
    while span < size:
        joined = (row // (2 * span) == column // (2 * span)) & (row // span != column // span)
        parts = [jnp.where(joined, lower, 0.0) for lower in lowers]
        if span > 1:
            parts = [dot_three(part, inverse) for part, inverse in zip(parts, inverses)]
            parts = [dot_three(inverse, part) for part, inverse in zip(parts, inverses)]
        inverses = [inverse - part for part, inverse in zip(parts, inverses)]
        span = span * 2
    return inverses


def unit(active):
    scale = lax.rsqrt(jnp.sum(active * active, axis=1, keepdims=True) + EPSILON)
    return (active * scale, scale)


def unit_back(grad, normal, scale):
    return scale * (grad - normal * jnp.sum(grad * normal, axis=1, keepdims=True))


def pick_lane(block, index):
    lane = lax.broadcasted_iota(jnp.int32, block.shape, 1)
    return jnp.sum(jnp.where(lane == index, block, 0.0), axis=1, keepdims=True)


def convolved(rows, taps, flags, tap_count):
    extended = rows[HALO - 8 :].astype(F32)
    total = extended[8:] * taps[tap_count - 1 : tap_count]
    for offset in range(1, tap_count):
        moved = pltpu.roll(extended, offset, 0)[8:] * flags[:, 2 + offset : 3 + offset]
        total = total + moved * taps[tap_count - 1 - offset : tap_count - offset]
    return (total, extended)


def convolved_back(d_total, extended, taps, flags, tap_count):
    rows = extended.shape[0]
    before = jnp.zeros((8, d_total.shape[1]), F32)
    d_rows = jnp.concatenate([before, d_total * taps[tap_count - 1 : tap_count]], axis=0)
    d_taps = [jnp.sum(d_total * extended[8:], axis=0, keepdims=True)]
    for offset in range(1, tap_count):
        kept = d_total * flags[:, 2 + offset : 3 + offset]
        moved = pltpu.roll(extended, offset, 0)[8:]
        d_taps = [jnp.sum(kept * moved, axis=0, keepdims=True)] + d_taps
        scaled = jnp.concatenate(
            [before, kept * taps[tap_count - 1 - offset : tap_count - offset]], axis=0
        )
        d_rows = d_rows + pltpu.roll(scaled, rows - offset, 0)
    d_taps = d_taps + [jnp.zeros((8 - tap_count, d_total.shape[1]), F32)]
    return (d_rows[8:], d_rows[:8], jnp.concatenate(d_taps, axis=0))


def silu_of(total):
    gate = 1.0 / (1.0 + jnp.exp(-total))
    return (total * gate, gate)


def span_kernel(
    many, tap_count, starts_col, starts_row, flags, betas, rows_q, rows_k, rows_v,
    taps_q, taps_k, taps_v,
    inverse_out, wy_out, scores_out, reach_out, local_out, pair_out,
):
    count = flags.shape[0]
    width = rows_q.shape[1] // many
    queries, keys, values = [
        silu_of(convolved(rows[...], taps[...], flags, tap_count)[0])[0]
        for rows, taps in ((rows_q, taps_q), (rows_k, taps_k), (rows_v, taps_v))
    ]
    row = lax.broadcasted_iota(jnp.int32, (count, count), 0)
    column = lax.broadcasted_iota(jnp.int32, (count, count), 1)
    same_doc = starts_col[...] == starts_row[...]
    first = flags[:, 0:1]
    last_part = flags[:, 1:2]
    eye = jnp.where(
        lax.broadcasted_iota(jnp.int32, (width, width), 0)
        == lax.broadcasted_iota(jnp.int32, (width, width), 1),
        1.0,
        0.0,
    )
    spots = [slice(at * width, (at + 1) * width) for at in range(many)]
    beta = [pick_lane(betas[...], pl.program_id(0) * many + at) for at in range(many)]
    query = [unit(queries[:, spot])[0] for spot in spots]
    key = [unit(keys[:, spot])[0] for spot in spots]
    products = [
        dot_three(jnp.concatenate([k, q], axis=0), k, ROWS_ROWS) for q, k in zip(query, key)
    ]
    lower = [
        jnp.where(same_doc & (row > column), b * p[:count], 0.0) for b, p in zip(beta, products)
    ]
    scores = [jnp.where(same_doc & (row >= column), p[count:], 0.0) for p in products]
    inverse = inverse_unit_lower(lower, count)
    for at, spot in enumerate(spots):
        scaled = jnp.concatenate(
            [key[at] * (beta[at] * first), values[:, spot] * beta[at]], axis=1
        )
        wy = dot_three(inverse[at], scaled)
        applied = dot_three(scores[at], wy)
        inverse_out[at] = inverse[at]
        wy_out[at] = wy
        scores_out[at] = scores[at]
        reach_out[:, spot] = first * query[at] - applied[:, :width]
        local_out[:, spot] = applied[:, width:]
        pair = dot_three(key[at] * last_part, wy, FIRST_FIRST)
        change = (flags[count - 1 : count, 0:1] - 1.0) * eye - pair[:, :width]
        pair_out[at] = jnp.concatenate([change, pair[:, width:]], axis=1).astype(LOW)


def rows_specs(count, width, head_count):
    steps = head_count
    return [
        pl.BlockSpec((count, width), lambda step, part=part: (0, part * steps + step))
        for part in range(3)
    ]


def span_call(starts, flags, betas, extended, taps, tap_count, head_count, after=()):
    many = SPAN_HEADS
    count, width = flags.shape[0], extended.shape[1] // (3 * head_count)
    rows = pl.BlockSpec((count, many * width), lambda step: (0, step))
    whole = lambda shape: pl.BlockSpec(shape, lambda step: (0, 0))
    square = pl.BlockSpec((many, count, count), lambda step: (step, 0, 0))
    return launch(
        functools.partial(span_kernel, many, tap_count),
        after,
        grid=(head_count // many,),
        in_specs=[
            whole((count, 1)), whole((1, count)), whole(flags.shape), whole(betas.shape),
        ]
        + rows_specs(extended.shape[0], many * width, head_count // many)
        + rows_specs(8, many * width, head_count // many),
        out_specs=[
            square,
            pl.BlockSpec((many, count, 2 * width), lambda step: (step, 0, 0)),
            square, rows, rows,
            pl.BlockSpec((many, width, 2 * width), lambda step: (step, 0, 0)),
        ],
        out_shape=[
            jax.ShapeDtypeStruct((head_count, count, count), F32),
            jax.ShapeDtypeStruct((head_count, count, 2 * width), F32),
            jax.ShapeDtypeStruct((head_count, count, count), F32),
            jax.ShapeDtypeStruct((count, head_count * width), F32),
            jax.ShapeDtypeStruct((count, head_count * width), F32),
            jax.ShapeDtypeStruct((head_count, width, 2 * width), LOW),
        ],
        cost_estimate=estimate(1, 1),
        operands=(
            starts[:, None], starts[None, :], flags, betas, extended, extended, extended,
            taps, taps, taps,
        ),
    )


def mixed_kernel(reach, local, state, gain, flags, mixed_out, head_out):
    mixed = local[...] + dot_three(reach[...], state[0].astype(F32))
    mixed_out[...] = mixed
    scale = lax.rsqrt(jnp.mean(mixed * mixed, axis=1, keepdims=True) + EPSILON)
    head_out[...] = (mixed * scale * gain[...] * flags[:, 2:3]).astype(LOW)


def mixed_call(reach, local, states, gain, flags, after=()):
    head_count, width = states.shape[0], states.shape[1]
    count = reach.shape[0]
    rows = pl.BlockSpec((count, width), lambda head: (0, head))
    return launch(
        mixed_kernel,
        after,
        grid=(head_count,),
        in_specs=[
            rows, rows,
            pl.BlockSpec((1, width, width), lambda head: (head, 0, 0)),
            pl.BlockSpec((1, width), lambda head: (0, 0)),
            pl.BlockSpec(flags.shape, lambda head: (0, 0)),
        ],
        out_specs=[rows, rows],
        out_shape=[
            jax.ShapeDtypeStruct(reach.shape, F32),
            jax.ShapeDtypeStruct(reach.shape, LOW),
        ],
        cost_estimate=estimate(6 * count * width * width * head_count, 14 * reach.shape[0] * reach.shape[1]),
        operands=(reach, local, states, gain[None], flags,),
    )


def pull_kernel(reach, mixed_in, grads, gain, flags, change, d_mixed_out, gain_out, pair_out):
    mixed, d_head, live = mixed_in[...], grads[...], flags[:, 2:3]
    width = mixed.shape[1]
    scale = lax.rsqrt(jnp.mean(mixed * mixed, axis=1, keepdims=True) + EPSILON)
    lifted = d_head * gain[...]
    inner = jnp.mean(lifted * mixed, axis=1, keepdims=True)
    d_mixed = live * (scale * lifted - mixed * (scale * scale * scale * inner))
    d_mixed_out[...] = d_mixed
    part = jnp.sum(d_head * mixed * (scale * live), axis=0, keepdims=True)

    @pl.when(pl.program_id(0) == 0)
    def _():
        gain_out[...] = jnp.zeros_like(gain_out)

    gain_out[...] += part
    pulled = dot_three(reach[...], d_mixed, FIRST_FIRST)
    turned = jnp.transpose(change[0, :, :width].astype(F32))
    pair_out[0] = jnp.concatenate([turned, pulled], axis=1).astype(LOW)


def pull_call(reach, mixed, grads, gain, flags, pairs, after=()):
    head_count, width = pairs.shape[0], pairs.shape[1]
    count = reach.shape[0]
    rows = pl.BlockSpec((count, width), lambda head: (0, head))
    pair = pl.BlockSpec((1, width, 2 * width), lambda head: (head, 0, 0))
    return launch(
        pull_kernel,
        after,
        grid=(head_count,),
        in_specs=[
            rows, rows, rows,
            pl.BlockSpec((1, width), lambda head: (0, 0)),
            pl.BlockSpec(flags.shape, lambda head: (0, 0)),
            pair,
        ],
        out_specs=[rows, pl.BlockSpec((1, width), lambda head: (0, 0)), pair],
        out_shape=[
            jax.ShapeDtypeStruct(reach.shape, F32),
            jax.ShapeDtypeStruct((1, width), F32),
            jax.ShapeDtypeStruct(pairs.shape, LOW),
        ],
        cost_estimate=estimate(6 * count * width * width * head_count, 20 * reach.shape[0] * reach.shape[1]),
        operands=(reach, mixed, grads, gain[None], flags, pairs,),
    )


def back_kernel(
    many, tap_count, starts_col, starts_row, flags, betas, rows_q, rows_k, rows_v,
    taps_q, taps_k, taps_v, inverse_in, wy_in, scores_in, state_in, end_in, grads,
    d_rows_out, d_tail_out, d_before_out, d_taps_out, d_beta_out,
):
    count = flags.shape[0]
    width = rows_q.shape[1] // many
    all_rows, all_taps = (rows_q, rows_k, rows_v), (taps_q, taps_k, taps_v)
    row = lax.broadcasted_iota(jnp.int32, (count, count), 0)
    column = lax.broadcasted_iota(jnp.int32, (count, count), 1)
    same_doc = starts_col[...] == starts_row[...]
    first = flags[:, 0:1]
    last_part = flags[:, 1:2]
    lane = lax.broadcasted_iota(jnp.int32, d_beta_out.shape, 1)
    d_betas = jnp.zeros(d_beta_out.shape, F32)
    for at in range(many):
        spot = slice(at * width, (at + 1) * width)
        head = pl.program_id(0) * many + at
        beta = pick_lane(betas[...], head)
        summed = [
            convolved(rows[:, spot], taps[:, spot], flags, tap_count)
            for rows, taps in zip(all_rows, all_taps)
        ]
        active = [silu_of(total) for total, _ in summed]
        query, query_scale = unit(active[0][0])
        key, key_scale = unit(active[1][0])
        value, grad = active[2][0], grads[:, spot]
        inverse, wy, scores = inverse_in[at], wy_in[at], scores_in[at]
        state, end = state_in[at].astype(F32), end_in[at].astype(F32)
        fresh = wy[:, width:] - dot_three(wy[:, :width], state)
        d_fresh = dot_three(scores, grad, FIRST_FIRST) + dot_three(key * last_part, end)
        pulled = dot_three(inverse, d_fresh, FIRST_FIRST)
        both = jnp.concatenate([grad, pulled], axis=0)
        through_state = dot_three(both, state, ROWS_ROWS)
        through_fresh = dot_three(both, fresh, ROWS_ROWS)
        d_scores = jnp.where(same_doc & (row >= column), through_fresh[:count], 0.0)
        d_lower = jnp.where(same_doc & (row > column), -through_fresh[count:], 0.0)
        by_keys = dot_three(jnp.concatenate([d_scores, d_lower], axis=0), key)
        d_query = first * through_state[:count] + by_keys[:count]
        recalled = -through_state[count:]
        row_part = by_keys[count:]
        d_key = (
            dot_three(d_scores, query, FIRST_FIRST)
            + dot_three(d_lower, beta * key, FIRST_FIRST)
            + last_part * dot_three(fresh, end, ROWS_ROWS)
            + (beta * first) * recalled
            + beta * row_part
        )
        d_active = (
            unit_back(d_query, query, query_scale),
            unit_back(d_key, key, key_scale),
            beta * pulled,
        )
        for kind in range(3):
            total, gate = summed[kind][0], active[kind][1]
            d_total = d_active[kind] * gate * (1.0 + total * (1.0 - gate))
            d_rows, d_before, d_taps = convolved_back(
                d_total, summed[kind][1], all_taps[kind][:, spot], flags, tap_count
            )
            d_rows_out[kind, :, spot] = d_rows.astype(LOW)
            d_tail_out[kind, :, spot] = d_rows[count - 8 :]
            d_before_out[kind, :, spot] = d_before
            d_taps_out[kind, :, spot] = d_taps
        d_beta = jnp.sum(
            (row_part + first * recalled) * key + pulled * value, axis=1, keepdims=True
        )
        d_betas = d_betas + jnp.where(lane == head, d_beta, 0.0)

    @pl.when(pl.program_id(0) == 0)
    def _():
        d_beta_out[...] = d_betas

    @pl.when(pl.program_id(0) > 0)
    def _():
        d_beta_out[...] += d_betas


def back_call(
    starts, flags, betas, extended, taps, tap_count, inverse, wy, scores, states, ends, grads,
    after=(),
):
    many = BACK_HEADS
    head_count, width = states.shape[0], states.shape[1]
    count = flags.shape[0]
    steps = head_count // many
    kinds = lambda height: pl.BlockSpec((3, height, many * width), lambda step: (0, 0, step))
    rows = pl.BlockSpec((count, many * width), lambda step: (0, step))
    whole = lambda shape: pl.BlockSpec(shape, lambda step: (0, 0))
    per_head = lambda shape: pl.BlockSpec((many,) + shape, lambda step: (step, 0, 0))
    return launch(
        functools.partial(back_kernel, many, tap_count),
        after,
        grid=(head_count // many,),
        in_specs=[
            whole((count, 1)), whole((1, count)), whole(flags.shape), whole(betas.shape),
            *rows_specs(extended.shape[0], many * width, steps),
            *rows_specs(8, many * width, steps),
            per_head((count, count)), per_head((count, 2 * width)), per_head((count, count)),
            per_head((width, width)), per_head((width, width)),
            rows,
        ],
        out_specs=[kinds(count), kinds(8), kinds(8), kinds(8), whole(betas.shape)],
        out_shape=[
            jax.ShapeDtypeStruct((3,) + grads.shape, LOW),
            jax.ShapeDtypeStruct((3, 8, grads.shape[1]), F32),
            jax.ShapeDtypeStruct((3, 8, grads.shape[1]), F32),
            jax.ShapeDtypeStruct((3, 8, grads.shape[1]), F32),
            jax.ShapeDtypeStruct(betas.shape, F32),
        ],
        cost_estimate=estimate(36 * head_count * count**3, 40 * grads.shape[0] * grads.shape[1]),
        operands=(
            starts[:, None], starts[None, :], flags, betas, extended, extended, extended,
            taps, taps, taps, inverse, wy, scores, states, ends, grads,
        ),
    )


def apply_pair(change, pair):
    upper, rest = split_low(pair)
    product = functools.partial(jnp.dot, preferred_element_type=F32)
    return pair + (product(change, upper) + product(change, rest))


def scan_kernel(
    waited, backwards, group_size, seq_size, *refs,
):
    scan_steps(backwards, group_size, seq_size, *refs[waited:])


def scan_steps(
    backwards, group_size, seq_size, pairs, states_out,
    got, total_sent, total_got, state_sent, arrived, send_sem, recv_sem,
):
    head_count, width = pairs.shape[0], pairs.shape[1]
    share = head_count // group_size
    my_seq, my_group = lax.axis_index("seq"), lax.axis_index("grp")
    peers = [lax.rem(my_group + step, group_size) for step in range(1, group_size)]
    bits = []
    while 2 ** len(bits) < seq_size:
        bits.append(2 ** len(bits))
    upper_half = [lax.rem(my_seq // bit, 2) for bit in bits]
    partners = [my_seq + bit - 2 * bit * half for bit, half in zip(bits, upper_half)]
    barrier = pltpu.get_barrier_semaphore()
    for peer in peers:
        pl.semaphore_signal(
            barrier, inc=1, device_id=(my_seq, peer), device_id_type=pl.DeviceIdType.MESH
        )
    for partner in partners:
        pl.semaphore_signal(
            barrier, inc=1, device_id=(partner, my_group), device_id_type=pl.DeviceIdType.MESH
        )
    pl.semaphore_wait(barrier, len(peers) + len(partners))

    def send(source, target, place, device):
        copy = pltpu.make_async_remote_copy(
            src_ref=source,
            dst_ref=target,
            send_sem=send_sem.at[place],
            recv_sem=recv_sem.at[place],
            device_id=device,
            device_id_type=pl.DeviceIdType.MESH,
        )
        copy.start()
        return copy

    mine = pl.ds(my_group * share, share)
    copies = [
        send(pairs.at[pl.ds(peer * share, share)], got.at[my_group], place, (my_seq, peer))
        for place, peer in enumerate(peers)
    ]
    got[my_group] = pairs[mine]
    for copy in copies:
        copy.wait()
    members = list(range(group_size))
    if backwards:
        members = members[::-1]
    eye = jnp.where(
        lax.broadcasted_iota(jnp.int32, (width, width), 0)
        == lax.broadcasted_iota(jnp.int32, (width, width), 1),
        1.0,
        0.0,
    )
    nothing = jnp.zeros((width, width), F32)
    start = jnp.concatenate([eye, nothing], axis=1)

    def added(pair):
        return jnp.concatenate([nothing, pair[:, width:].astype(F32)], axis=1)

    totals = []
    for head in range(share):
        total = start + got[members[0], head].astype(F32)
        for member in members[1:]:
            pair = got[member, head]
            total = apply_pair(pair[:, :width], total) + added(pair)
        totals.append(total)
    before = [start for _ in range(share)]
    for level, partner in enumerate(partners):
        for head in range(share):
            total_sent[level, head] = (totals[head] - start).astype(LOW)
        copy = send(
            total_sent.at[level],
            total_got.at[level],
            group_size - 1 + level,
            (partner, my_group),
        )
        copy.wait()
        later = upper_half[level] == (0 if backwards else 1)
        for head in range(share):
            theirs = total_got[level, head].astype(F32) + start
            first_pair = jnp.where(later, theirs, totals[head])
            second_pair = jnp.where(later, totals[head], theirs)
            moved = dot_three(
                jnp.concatenate([second_pair[:, :width], before[head][:, :width]], axis=0),
                first_pair,
            )
            totals[head] = moved[:width] + added(second_pair)
            before[head] = jnp.where(later, moved[width:] + added(before[head]), before[head])
    for head in range(share):
        state = before[head][:, width:]
        for member in members:
            state_sent[member, head] = state.astype(LOW)
            if member != members[-1]:
                pair = got[member, head]
                state = apply_pair(pair[:, :width], state) + pair[:, width:].astype(F32)
    place_now = group_size - 1 + len(bits)
    copies = [
        send(state_sent.at[peer], arrived.at[mine], place_now + place, (my_seq, peer))
        for place, peer in enumerate(peers)
    ]
    arrived[mine] = state_sent[my_group]
    for copy in copies:
        copy.wait()
    states_out[...] = arrived[...]


def scan_call(pairs, backwards, collective_id, after=()):
    head_count, width = pairs.shape[0], pairs.shape[1]
    group_size, seq_size = lax.axis_size("grp"), lax.axis_size("seq")
    share = head_count // group_size
    levels = (seq_size - 1).bit_length()
    sems = 2 * (group_size - 1) + levels
    return pl.pallas_call(
        functools.partial(scan_kernel, len(after), backwards, group_size, seq_size),
        in_specs=[pl.BlockSpec(memory_space=pl.ANY)] * len(after)
        + [pl.BlockSpec(memory_space=pltpu.VMEM)],
        out_specs=pl.BlockSpec(memory_space=pltpu.VMEM),
        out_shape=jax.ShapeDtypeStruct((head_count, width, width), LOW),
        cost_estimate=estimate(400 * share * width**3 * levels, 64 * pairs.size),
        scratch_shapes=[
            pltpu.VMEM((group_size, share, width, 2 * width), LOW),
            pltpu.VMEM((levels, share, width, 2 * width), LOW),
            pltpu.VMEM((levels, share, width, 2 * width), LOW),
            pltpu.VMEM((group_size, share, width, width), LOW),
            pltpu.VMEM((head_count, width, width), LOW),
            pltpu.SemaphoreType.DMA((sems,)),
            pltpu.SemaphoreType.DMA((sems,)),
        ],
        compiler_params=pltpu.CompilerParams(
            collective_id=collective_id, has_side_effects=True, vmem_limit_bytes=VMEM_LIMIT
        ),
    )(*after, pairs)


def swapped(value, bit):
    count = lax.axis_size("seq")
    return lax.ppermute(value, "seq", [(place, place ^ bit) for place in range(count)])


def chip_bits():
    count = lax.axis_size("seq")
    bits = []
    bit = 2
    while bit < count:
        bits.append(bit)
        bit = bit * 2
    return bits


def masks_of(order):
    masks = [0]
    for bit in order:
        masks = masks + [mask ^ bit for mask in masks]
    return masks


def tied(value, *others):
    return lax.optimization_barrier((value,) + others)[0]


def relative(values, masks):
    count = lax.axis_size("seq")
    width = values.shape[1] // count
    mine = lax.axis_index("seq")
    return jnp.concatenate(
        [lax.dynamic_slice_in_dim(values, (mine ^ mask) * width, width, 1) for mask in masks],
        axis=1,
    )


def spread_views(block, order, joined):
    views = [(block, 0)]
    for bit in order:
        if joined:
            if len(views) > 1:
                rows = block.shape[0]
                held = jnp.concatenate(
                    [array[at * rows : (at + 1) * rows] for array, at in views], axis=0
                )
            else:
                held = block
            arrived = swapped(held, bit)
            views = views + [(arrived, at) for at in range(len(views))]
        else:
            views = views + [(swapped(array, bit), at) for array, at in views]
    return views


def add_kernel(kept, arrived, total):
    total[...] = (kept[...].astype(F32) + arrived[...].astype(F32)).astype(LOW)


def halved_sum(kept, lower, bit, after=()):
    half, width = kept.shape
    arrived = swapped(lower, bit)
    tile = wide_tile(width)
    spot = pl.BlockSpec((half, tile), lambda step: (0, step))
    return launch(
        add_kernel,
        after,
        grid=(width // tile,),
        in_specs=[spot, spot],
        out_specs=spot,
        out_shape=jax.ShapeDtypeStruct((half, width), LOW),
        cost_estimate=estimate(1, 1),
        operands=(kept, arrived),
    )


def over_groups(rows):
    return lax.psum_scatter(rows, "grp", scatter_dimension=0, tiled=True).astype(F32)


def wide_tile(width, start=0):
    for parts in (1, 2, 3, 4, 6, 9):
        tile = width // parts
        if width % parts == 0 and tile % 128 == 0 and tile <= 1024 and start % tile == 0:
            return tile
    return 128


def tile_of(width, largest):
    tile = largest
    while width % tile:
        tile = tile // 2
    return tile


def copy_kernel(source, target):
    target[...] = source[...]


def columns(block, start, width):
    rows = block.shape[0]
    return launch(
        copy_kernel,
        (),
        grid=(1,),
        in_specs=[pl.BlockSpec((rows, width), lambda step: (0, start // width))],
        out_specs=pl.BlockSpec((rows, width), lambda step: (0, 0)),
        out_shape=jax.ShapeDtypeStruct((rows, width), block.dtype),
        cost_estimate=estimate(1, 1),
        operands=(block,),
    )


def join_kernel(first, second, target):
    rows = first.shape[0]
    target[:rows] = first[...]
    target[rows:] = second[...]


def join_columns(first, second, start, width, after=()):
    tile = wide_tile(width, start)
    rows = first.shape[0]
    return launch(
        join_kernel,
        after,
        grid=(width // tile,),
        in_specs=[pl.BlockSpec((rows, tile), lambda step: (0, start // tile + step))] * 2,
        out_specs=pl.BlockSpec((2 * rows, tile), lambda step: (0, step)),
        out_shape=jax.ShapeDtypeStruct((2 * rows, width), first.dtype),
        cost_estimate=estimate(0, 4 * rows * width),
        operands=(first, second),
    )


def contract_kernel(grads, weights, total):
    @pl.when(pl.program_id(0) == 0)
    def _():
        total[...] = jnp.zeros_like(total)

    total[...] += lax.dot_general(
        grads[...], weights[...], (((1,), (1,)), ((), ())), preferred_element_type=F32
    )


def contract_rows(grads, weights, start, after=()):
    tokens, width = grads.shape
    tile = tile_of(width, 1024)
    depth = weights.shape[0]
    first = start // tile
    return launch(
        contract_kernel,
        after,
        grid=(width // tile,),
        in_specs=[
            pl.BlockSpec((tokens, tile), lambda step: (0, step)),
            pl.BlockSpec((depth, tile), lambda step: (0, first + step)),
        ],
        out_specs=pl.BlockSpec((tokens, depth), lambda step: (0, 0)),
        out_shape=jax.ShapeDtypeStruct((tokens, depth), F32),
        cost_estimate=estimate(2 * tokens * depth * width, 2 * depth * width),
        operands=(grads, weights),
    )


def chip_spots(orders, depth):
    chip = lax.axis_index("seq") // 2
    spots = []
    for mask in orders:
        place = chip
        bit = 1
        while bit <= mask:
            if mask & bit:
                place = place + bit - 2 * bit * lax.rem(chip // bit, 2)
            bit = bit * 2
        spots.append(pl.ds(pl.multiple_of(place * depth, depth), depth))
    return spots


def fill_by_core(pairs):
    def store(turn):
        for put, block in pairs:
            half = block.shape[1] // 2
            if turn:
                wide = block.astype(F32) if half % 128 else block
                wide = jnp.concatenate([wide[:, half:], wide[:, :half]], axis=1)
                put(wide.astype(block.dtype))
            else:
                put(block)

    core = lax.rem(lax.axis_index("seq"), 2)
    pl.when(core == 0)(functools.partial(store, False))
    pl.when(core == 1)(functools.partial(store, True))


def putter(target, rows, columns_now):
    def put(value):
        target[rows, columns_now] = value

    return put


def feed_kernel(count, cuts, masks, stage, *refs):
    if stage == 0:
        given, refs = refs[:4], refs[4:]
    else:
        (feed, slopes), refs = refs[:2], refs[2:]
    weights, refs = refs[: 6 * count], refs[6 * count :]
    if stage == 0:
        grads_first, grads_second, feed, slopes, out_total, d_total = refs
    else:
        out_before, d_before, grads_first, grads_second, out_own, out_other, d_own, d_other = refs[:8]
        out_total, d_total = refs[8:]
    step = pl.program_id(0)
    tokens, model = feed.shape
    depth = model // count
    spans = [slice(place * depth, (place + 1) * depth) for place in range(count)]

    @pl.when(step == 0)
    def _():
        if stage == 0:
            spots = chip_spots(masks, depth)
            half = tokens // 2
            first_rows, second_rows = slice(0, half), slice(half, tokens)
            for target, (own, other) in ((feed, given[:2]), (slopes, given[2:])):
                for span, spot in zip(spans, spots):
                    fill_by_core(
                        [
                            (putter(target, first_rows, span), own[:, spot]),
                            (putter(target, second_rows, span), other[:, spot]),
                        ]
                    )
            out_total[...] = jnp.zeros_like(out_total)
            d_total[...] = jnp.zeros_like(d_total)
        else:
            out_total[...] = out_before[...]
            d_total[...] = d_before[...]

    back = functools.partial(
        lax.dot_general, dimension_numbers=(((1,), (1,)), ((), ())), preferred_element_type=F32
    )

    def tile_step(pieces, grads_out):
        gate_part, up_part, down_part = [
            jnp.concatenate(
                [piece[...] for piece in pieces[kind * count : (kind + 1) * count]], axis=0
            )
            for kind in range(3)
        ]
        gate = jnp.dot(feed[...], gate_part, preferred_element_type=F32)
        upper = jnp.dot(feed[...], up_part, preferred_element_type=F32)
        d_inner = jnp.dot(slopes[...], down_part, preferred_element_type=F32)
        gate_sig = 1.0 / (1.0 + jnp.exp(-gate))
        gate_act = gate * gate_sig
        inner = (gate_act * upper).astype(LOW)
        d_gate = (d_inner * upper * gate_sig * (1.0 + gate * (1.0 - gate_sig))).astype(LOW)
        d_upper = (d_inner * gate_act).astype(LOW)
        grads_out[0] = d_gate
        grads_out[1] = d_upper
        grads_out[2] = inner
        out_total[...] += back(inner, down_part)
        d_total[...] += back(d_gate, gate_part) + back(d_upper, up_part)

    @pl.when(step < cuts[0])
    def _():
        tile_step(weights[: 3 * count], grads_first)

    @pl.when(step >= cuts[0])
    def _():
        tile_step(weights[3 * count :], grads_second)

    if stage:

        @pl.when(step == cuts[0] + cuts[1] - 1)
        def _():
            spots = chip_spots(masks, depth)
            half = tokens // 2
            for source, own, other in ((out_total, out_own, out_other), (d_total, d_own, d_other)):
                for span, spot in zip(spans, spots):
                    fill_by_core(
                        [
                            (putter(own, slice(None), spot), source[:half, span]),
                            (putter(other, slice(None), spot), source[half:, span]),
                        ]
                    )


def feed_call(rows, piece_lists, before, masks, tile, after=()):
    tokens, depth = (2 * rows[0].shape[0] if before is None else rows[0].shape[0]), rows[0].shape[1]
    cuts = [pieces[0][0].shape[1] // (3 * tile) for pieces in piece_lists]
    block_rows = depth // len(piece_lists[0])
    count = len(piece_lists[0])
    first = lambda step: jnp.minimum(step, cuts[0] - 1)
    second = lambda step: jnp.maximum(step - cuts[0], 0)
    whole = pl.BlockSpec((tokens, depth), lambda step: (0, 0))
    single = pl.BlockSpec((tokens // 2, depth), lambda step: (0, 0))
    weights = [
        pl.BlockSpec(
            (block_rows, tile),
            lambda step, at=at, kind=kind, where=where, cut=cut: (at, kind * cut + where(step)),
        )
        for pieces, where, cut in zip(piece_lists, (first, second), cuts)
        for kind in range(3)
        for _, at in pieces
    ]
    both = jax.ShapeDtypeStruct((tokens, depth), F32)
    one = jax.ShapeDtypeStruct((tokens // 2, depth), F32)
    kept = jax.ShapeDtypeStruct((tokens, depth), LOW)
    return launch(
        functools.partial(feed_kernel, count, cuts, masks, 0 if before is None else 1),
        after,
        grid=(cuts[0] + cuts[1],),
        in_specs=([single] * 4 if before is None else [whole] * 2)
        + weights
        + ([] if before is None else [whole] * 2),
        out_specs=[
            pl.BlockSpec((3, tokens, tile), lambda step: (0, 0, first(step))),
            pl.BlockSpec((3, tokens, tile), lambda step: (0, 0, second(step))),
        ]
        + ([whole] * 4 if before is None else [single] * 4),
        out_shape=[
            jax.ShapeDtypeStruct((3, tokens, cuts[0] * tile), LOW),
            jax.ShapeDtypeStruct((3, tokens, cuts[1] * tile), LOW),
        ]
        + ([kept, kept, both, both] if before is None else [one] * 4),
        scratch_shapes=[]
        if before is None
        else [pltpu.VMEM((tokens, depth), F32), pltpu.VMEM((tokens, depth), F32)],
        cost_estimate=estimate(1, 1),
        operands=(
            *rows,
            *([array for array, _ in piece_lists[0]] * 3),
            *([array for array, _ in piece_lists[1]] * 3),
            *(before if before is not None else ()),
        ),
    )


def outer_kernel(count, kinds, starts, first_kind, outs, *refs):
    sources = (refs[:count], refs[count : 2 * count])
    grads, arrived, results = refs[2 * count], refs[2 * count + 1 : -outs], refs[-outs:]
    kind = pl.program_id(0) + first_kind
    depth = outs * results[0].shape[0] // count
    each = count // outs

    def fill(source, added):
        for place in range(count):
            rows = slice(place * depth, (place + 1) * depth)
            total = lax.dot_general(
                source[place][...], grads[0], (((0,), (0,)), ((), ())),
                preferred_element_type=F32,
            )
            if added is not None:
                total = total + added[rows].astype(F32)
            inside = place % each
            results[place // each][inside * depth : (inside + 1) * depth] = total.astype(LOW)

    for which in range(2):
        wanted = (kind == kinds - 1) if which else (kind < kinds - 1)
        if not arrived:
            pl.when(wanted)(functools.partial(fill, sources[which], None))
        for place, added in enumerate(arrived):
            inside = kind >= starts[place]
            if place + 1 < len(arrived):
                inside = inside & (kind < starts[place + 1])
            pl.when(wanted & inside)(functools.partial(fill, sources[which], added))


def outer_call(sources, grads, places, span=None, arrived=(), starts=(0,), after=(), outs=1):
    tokens, model = sources[0].shape
    kinds, _, width = grads.shape
    blocks = 2 * len(places)
    depth = model // blocks
    half = model // 2
    first_kind, stop = span or (0, kinds)
    last = stop - first_kind

    def own(place):
        return pl.BlockSpec((tokens, depth), lambda kind: (0, place))

    def added(array, start):
        most = array.shape[1] // width - 1
        return pl.BlockSpec(
            (half, width), lambda kind: (0, jnp.clip(kind + first_kind - start, 0, most))
        )

    results = launch(
        functools.partial(outer_kernel, len(places), kinds, starts, first_kind, outs),
        after,
        grid=(last,),
        in_specs=[own(place) for place in places] * 2
        + [pl.BlockSpec((1, tokens, width), lambda kind: (first_kind + kind, 0, 0))]
        + [added(array, start) for array, start in zip(arrived, starts)],
        out_specs=[pl.BlockSpec((half // outs, width), lambda kind: (0, kind))] * outs,
        out_shape=[jax.ShapeDtypeStruct((half // outs, last * width), LOW)] * outs,
        cost_estimate=estimate(1, 1),
        operands=(
            *([sources[0]] * len(places)), *([sources[1]] * len(places)), grads, *arrived,
        ),
    )
    return results[0] if outs == 1 else tuple(results)


def gather_kernel(
    group_size, bits, orders, cuts, feed_cuts, shard, feed, full, pair_first, pair_second, rest,
    own_sem, line_send, line_recv, tree_send, tree_recv, feed_send, feed_recv, core_send, core_recv,
):
    my_seq, my_group = lax.axis_index("seq"), lax.axis_index("grp")
    rows = shard.shape[0]
    levels = len(orders[0])

    def flipped(mask):
        place = my_seq
        for bit in bits:
            if mask & bit:
                place = place + bit - 2 * bit * lax.rem(my_seq // bit, 2)
        return place

    def remote(source, target, send_sem, recv_sem, device):
        return pltpu.make_async_remote_copy(
            src_ref=source, dst_ref=target, send_sem=send_sem, recv_sem=recv_sem,
            device_id=device, device_id_type=pl.DeviceIdType.MESH,
        )

    def greet(device):
        pl.semaphore_signal(
            barrier, inc=1, device_id=device, device_id_type=pl.DeviceIdType.MESH
        )

    def has(direction, steps):
        return my_group >= steps if direction == 0 else my_group + steps < group_size

    def beside(direction, steps):
        return my_group - steps if direction == 0 else my_group + steps

    barrier = pltpu.get_barrier_semaphore()
    for bit in bits:
        greet((flipped(bit), my_group))
    for direction in range(2):

        @pl.when(has(direction, 1))
        def _():
            greet((my_seq, beside(direction, 1)))

    pl.semaphore_wait(
        barrier,
        len(bits) + jnp.minimum(my_group, 1) + jnp.minimum(group_size - 1 - my_group, 1),
    )

    def place_of(mask, group):
        return pl.ds(pl.multiple_of((flipped(mask) * group_size + group) * rows, rows), rows)

    def line_copies(kind, direction, hop):
        origin = beside(direction, hop - 1)
        device = (my_seq, beside(1 - direction, 1))
        if kind == 0:
            views = [(shard if hop == 1 else full.at[place_of(0, origin)], full.at[place_of(0, origin)])]
            sems = (line_send, line_recv)
        else:
            spot = pl.ds(pl.multiple_of(origin * rows, rows), rows)
            parts = (pair_first, pair_second, rest)
            views = [
                (
                    feed.at[:, cut] if hop == 1 else part.at[spot],
                    part.at[spot],
                )
                for part, cut in zip(parts, feed_cuts)
            ]
            sems = (feed_send, feed_recv)
        return [
            remote(source, target, sems[0].at[direction, hop - 1, at], sems[1].at[direction, hop - 1, at], device)
            for at, (source, target) in enumerate(views)
        ]

    def line_send_now(kind, direction, hop):
        @pl.when(has(1 - direction, 1))
        def _():
            for copy in line_copies(kind, direction, hop):
                copy.start()

    def line_wait(kind, direction, hop):
        for copy in line_copies(kind, direction, hop):
            copy.wait_recv()

    def line_drain(kind):
        for direction in range(2):
            for hop in range(1, group_size):

                @pl.when(has(direction, hop - 1) & has(1 - direction, 1))
                def _():
                    for copy in line_copies(kind, direction, hop):
                        copy.wait_send()

    slots = [(0, 0)] + [(direction, hop) for hop in range(1, group_size) for direction in range(2)]

    def node_copy(slot, part, level, mask):
        direction, hop = slots[slot]
        origin = beside(direction, hop) if hop else my_group
        view = full.at[place_of(mask, origin), cuts[part]]
        source = shard.at[:, cuts[part]] if hop == 0 and mask == 0 else view
        node = 2**level - 1 + masks_of(orders[part][:level]).index(mask)
        return remote(
            source, view, tree_send.at[slot, part, node], tree_recv.at[slot, part, node],
            (flipped(orders[part][level]), my_group),
        )

    def stage(slot, lag):
        direction, hop = slots[slot]
        if lag == 0:
            if hop:
                line_wait(0, direction, hop)
                if hop + 1 < group_size:
                    line_send_now(0, direction, hop + 1)
            for part in range(2):
                for level in range(levels):
                    node_copy(slot, part, level, 0).start()
        else:
            level = lag - 1
            for part in range(2):
                for mask in masks_of(orders[part][:level]):
                    node_copy(slot, part, level, mask).wait_recv()
                    for later in range(level + 1, levels):
                        node_copy(slot, part, later, mask ^ orders[part][level]).start()

    def when_held(slot, work):
        direction, hop = slots[slot]
        if hop == 0:
            work()
        else:
            pl.when(has(direction, hop))(work)

    own = pltpu.make_async_copy(shard, full.at[place_of(0, my_group)], own_sem.at[0])
    own.start()
    spot = pl.ds(pl.multiple_of(my_group * rows, rows), rows)
    own_feed = [
        pltpu.make_async_copy(feed.at[:, cut], part.at[spot], own_sem.at[1 + at])
        for at, (part, cut) in enumerate(zip((pair_first, pair_second, rest), feed_cuts))
    ]
    for copy in own_feed:
        copy.start()
    for direction in range(2):
        line_send_now(0, direction, 1)
    def feed_hop(hop):
        for direction in range(2):

            @pl.when(has(direction, hop))
            def _():
                line_wait(1, direction, hop)
                if hop + 1 < group_size:
                    line_send_now(1, direction, hop + 1)

    def at_lag(slot, lag):
        when_held(slot, functools.partial(stage, slot, lag))

    at_lag(0, 0)
    for hop in range(1, group_size):
        at_lag(2 * hop - 1, 0)
        at_lag(2 * hop, 0)
        if hop == group_size - 2:
            for direction in range(2):
                line_send_now(1, direction, 1)
        for slot in [0] if hop == 1 else [2 * hop - 3, 2 * hop - 2]:
            at_lag(slot, 1)
    for slot in range(max(2 * group_size - 3, 0), len(slots)):
        at_lag(slot, 1)
    hop_now = 1
    for lag in range(2, levels):
        for slot in range(len(slots)):
            if slot % 3 == 0 and hop_now < group_size:
                feed_hop(hop_now)
                hop_now = hop_now + 1
            at_lag(slot, lag)
    for hop in range(hop_now, group_size):
        feed_hop(hop)
    line_drain(1)
    for copy in own_feed:
        copy.wait()
    half = rest.shape[0]
    first_width = pair_first.shape[1]
    swaps = [
        remote(
            rest.at[:, cut], part.at[pl.ds(half, half)], core_send.at[at], core_recv.at[at],
            (flipped(1), my_group),
        )
        for at, (part, cut) in enumerate(
            (
                (pair_first, pl.ds(0, first_width)),
                (pair_second, pl.ds(first_width, pair_second.shape[1])),
            )
        )
    ]
    for copy in swaps:
        copy.start()
    for slot in range(len(slots)):
        when_held(slot, functools.partial(stage, slot, levels))
    for copy in swaps:
        copy.wait()
    own.wait()
    line_drain(0)

    def drain(slot):
        for part in range(2):
            for level in range(levels):
                for mask in masks_of(orders[part][:level]):
                    node_copy(slot, part, level, mask).wait_send()

    for slot in range(len(slots)):
        when_held(slot, functools.partial(drain, slot))


def gather_call(shard, feed, cuts, feed_cuts, orders, collective_id):
    group_size, seq_size = lax.axis_size("grp"), lax.axis_size("seq")
    rows, width = shard.shape
    bits = [1] + chip_bits()
    nodes = 2 ** len(bits) - 1
    slots = 2 * group_size - 1
    first_width, second_width = feed_cuts[0].size, feed_cuts[1].size
    any_space = pl.BlockSpec(memory_space=pl.ANY)
    dma = pltpu.SemaphoreType.DMA
    return pl.pallas_call(
        functools.partial(gather_kernel, group_size, bits, orders, cuts, feed_cuts),
        in_specs=[any_space] * 2,
        out_specs=[any_space] * 4,
        out_shape=[
            jax.ShapeDtypeStruct((rows * group_size * seq_size, width), LOW),
            jax.ShapeDtypeStruct((2 * rows * group_size, first_width), LOW),
            jax.ShapeDtypeStruct((2 * rows * group_size, second_width), LOW),
            jax.ShapeDtypeStruct((rows * group_size, first_width + second_width), LOW),
        ],
        scratch_shapes=[
            dma((4,)),
            dma((2, group_size - 1, 1)), dma((2, group_size - 1, 1)),
            dma((slots, 2, nodes)), dma((slots, 2, nodes)),
            dma((2, group_size - 1, 3)), dma((2, group_size - 1, 3)),
            dma((2,)), dma((2,)),
        ],
        cost_estimate=estimate(1.5e11, 1e8),
        compiler_params=pltpu.CompilerParams(collective_id=collective_id, has_side_effects=True),
    )(shard, feed)


def reduce_kernel(waited, group_size, all_orders, groups, *refs):
    refs = refs[waited:]
    sets = len(groups)
    inputs, refs = refs[: 4 * sets + 1], refs[4 * sets + 1 :]
    totals, everywhere, refs = refs[:sets], refs[sets], refs[sets + 1 :]
    buffers, refs = refs[: 5 * sets], refs[5 * sets :]
    vector_out, vector_in = refs[:2]
    send_sem, recv_sem, core_send, core_recv, line_send, line_recv, v_send, v_recv = refs[2:]
    my_seq, my_group = lax.axis_index("seq"), lax.axis_index("grp")
    peers = [lax.rem(my_group + step, group_size) for step in range(1, group_size)]
    most = max(len(orders[0]) for orders in all_orders)
    bits = [1] + max(all_orders, key=lambda orders: len(orders[0]))[1]
    units = [(place, group) for place in range(sets) for group in range(groups[place])]
    half = inputs[0].shape[0] // 2 ** len(all_orders[0][0])
    rows = half // group_size

    def partner(bit):
        return my_seq + bit - 2 * bit * lax.rem(my_seq // bit, 2)

    def greet(device):
        pl.semaphore_signal(
            barrier, inc=1, device_id=device, device_id_type=pl.DeviceIdType.MESH
        )

    barrier = pltpu.get_barrier_semaphore()
    for bit in bits:
        greet((partner(bit), my_group))
    for peer in peers:
        greet((my_seq, peer))
    pl.semaphore_wait(barrier, len(bits) + len(peers))

    def remote(source, target, send, recv, device):
        return pltpu.make_async_remote_copy(
            src_ref=source, dst_ref=target, send_sem=send, recv_sem=recv,
            device_id=device, device_id_type=pl.DeviceIdType.MESH,
        )

    def orders_of(unit):
        return all_orders[units[unit][0]]

    def held(unit, level):
        return inputs[4 * units[unit][0]].shape[0] // 2**level

    def begins(unit, level):
        return sum(held(unit, before) for before in range(level))

    def parts_of(unit):
        place, group = units[unit]
        given, own = inputs[4 * place : 4 * place + 4], buffers[5 * place : 5 * place + 5]
        return given, (own[:2], own[2], own[3], own[4]), group

    def chip_copy(unit, part, level):
        given, (arrived, _, _, _), group = parts_of(unit)
        width = arrived[part].shape[-1]
        count = held(unit, level)
        order = orders_of(unit)[part]
        if level == 0:
            source = given[part].at[:, pl.ds(group * width, width)]
        else:
            source = arrived[part].at[group, pl.ds(begins(unit, level - 1) + count, count)]
        return remote(
            source,
            arrived[part].at[group, pl.ds(begins(unit, level), count)],
            send_sem.at[unit, part, level],
            recv_sem.at[unit, part, level],
            (partner(order[len(order) - 1 - level]), my_group),
        )

    def core_copy(unit):
        _, (_, chip_total, core_in, _), group = parts_of(unit)
        return remote(
            chip_total.at[group, pl.ds(half, half)],
            core_in.at[group],
            core_send.at[unit],
            core_recv.at[unit],
            (partner(1), my_group),
        )

    def block_at(group):
        return pl.ds(group * rows, rows)

    def line_copy(unit, side, sender, target):
        _, (_, chip_total, core_in, line_in), group = parts_of(unit)
        source = (chip_total, core_in)[side].at[group, block_at(target)]
        receiver = sender + 1 if target > sender else sender - 1
        spot = group_size if target == receiver < sender else target
        return remote(
            source,
            line_in.at[group, spot, side],
            line_send.at[unit, spot, side],
            line_recv.at[unit, spot, side],
            (my_seq, receiver),
        )

    def line_step(unit, place, hop, up):
        _, (_, chip_total, core_in, line_in), group = parts_of(unit)
        targets = range(place + 1, group_size) if up else range(place)
        for target in targets:
            for side, source in enumerate((chip_total, core_in)):
                if hop:
                    line_copy(unit, side, place - 1 if up else place + 1, target).wait_recv()
                    value = source[group, target * rows : (target + 1) * rows].astype(F32)
                    value = value + line_in[group, target, side].astype(F32)
                    source[group, target * rows : (target + 1) * rows] = value.astype(LOW)
                line_copy(unit, side, place, target).start()

    def line_hop(unit, hop):
        for up, place in ((True, hop), (False, group_size - 1 - hop)):

            @pl.when(my_group == place)
            def _():
                line_step(unit, place, hop, up)

    def line_end(unit, place):
        _, (_, chip_total, core_in, line_in), group = parts_of(unit)
        total = totals[units[unit][0]]
        both = chip_total.shape[-1]
        for side, source in enumerate((chip_total, core_in)):
            value = source[group, place * rows : (place + 1) * rows].astype(F32)
            if place > 0:
                line_copy(unit, side, place - 1, place).wait_recv()
                value = value + line_in[group, place, side].astype(F32)
            if place + 1 < group_size:
                line_copy(unit, side, place + 1, place).wait_recv()
                value = value + line_in[group, group_size, side].astype(F32)
            spot = (group * 2 + side) * both
            total[:, spot : spot + both] = value

    def line_drain(unit, place):
        for target in range(group_size):
            if target != place:
                for side in range(2):
                    line_copy(unit, side, place, target).wait_send()

    def stage(unit, lag):
        given, (arrived, chip_total, core_in, line_in), group = parts_of(unit)
        levels = len(orders_of(unit)[0])
        widths = [buffer.shape[-1] for buffer in arrived]
        if lag == 0:
            for part in range(2):
                chip_copy(unit, part, 0).start()
        elif lag <= levels:
            level = lag - 1
            for part in range(2):
                chip_copy(unit, part, level).wait_recv()
                count, width = held(unit, level), widths[part]

                def added(low, high):
                    base = begins(unit, level)
                    value = arrived[part][group, base + low : base + high].astype(F32)
                    if level == 0:
                        kept = given[2 + part][low:high, group * width : (group + 1) * width]
                    else:
                        before = begins(unit, level - 1)
                        kept = arrived[part][group, before + low : before + high]
                    return value + kept.astype(F32)

                if lag < levels:
                    middle = count // 2
                    base = begins(unit, level)
                    arrived[part][group, base + middle : base + count] = added(
                        middle, count
                    ).astype(LOW)
                    chip_copy(unit, part, level + 1).start()
                    arrived[part][group, base : base + middle] = added(0, middle).astype(LOW)
                else:
                    at = part * widths[0]
                    chip_total[group, :, at : at + width] = added(0, count).astype(LOW)
            if lag == levels:
                core_copy(unit).start()
        elif lag == levels + 1:
            core_copy(unit).wait_recv()
            if group_size > 1:
                line_hop(unit, 0)
        else:
            line_hop(unit, lag - levels - 1)

    def vector_copies(step):
        if step < len(bits):
            return [
                remote(
                    vector_out.at[step], vector_in.at[step], v_send.at[step], v_recv.at[step],
                    (partner(bits[step]), my_group),
                )
            ]
        return [
            remote(
                vector_out.at[step], vector_in.at[step + at], v_send.at[step + at],
                v_recv.at[step + at], (my_seq, peer),
            )
            for at, peer in enumerate(peers)
        ]

    def vector_step(step):
        if step:
            for copy in vector_copies(step - 1):
                copy.wait_recv()
        if step == 0:
            vector_out[0] = inputs[-1][...]
        elif step <= len(bits):
            vector_out[step] = vector_out[step - 1] + vector_in[step - 1]
        else:
            value = vector_out[len(bits)]
            for at in range(len(peers)):
                value = value + vector_in[len(bits) + at]
            everywhere[...] = value
        if step <= len(bits):
            for copy in vector_copies(step):
                copy.start()

    last_step = len(units) + most + group_size - 1
    ahead = AHEAD
    for unit in range(min(ahead, len(units))):
        stage(unit, 0)
    for step in range(last_step):
        if step + ahead < len(units):
            stage(step + ahead, 0)
        for lag in range(1, most + group_size):
            unit = step - lag
            if 0 <= unit < len(units) and lag < len(orders_of(unit)[0]) + max(group_size, 2):
                stage(unit, lag)
        if step <= len(bits) + 1:
            vector_step(step)
    for step in range(last_step, len(bits) + 2):
        vector_step(step)
    for place in range(group_size):

        @pl.when(my_group == place)
        def _():
            for unit in range(len(units)):
                line_end(unit, place)
    for step in range(len(bits) + 1):
        for copy in vector_copies(step):
            copy.wait_send()
    for unit in range(len(units)):
        for part in range(2):
            for level in range(len(orders_of(unit)[0])):
                chip_copy(unit, part, level).wait_send()
        core_copy(unit).wait_send()
    for place in range(group_size):

        @pl.when(my_group == place)
        def _():
            for unit in range(len(units)):
                line_drain(unit, place)


def reduce_call(sets, vector, collective_id, after=()):
    group_size = lax.axis_size("grp")
    groups = [group for _, _, group, _ in sets]
    all_orders = [orders for _, _, _, orders in sets]
    half = sets[0][0][0].shape[0] // 2 ** len(all_orders[0][0])
    rows = half // group_size
    units = sum(groups)
    most = max(len(orders[0]) for orders in all_orders)
    bits = most + 1
    in_vmem = pl.BlockSpec(memory_space=pltpu.VMEM)
    in_any = pl.BlockSpec(memory_space=pl.ANY)
    dma = pltpu.SemaphoreType.DMA
    scratch, operands, results = [], [], []
    for lowers, uppers, group, orders in sets:
        depth = lowers[0].shape[0]
        held_all = sum(depth // 2**level for level in range(len(orders[0])))
        widths = [lower.shape[1] // group for lower in lowers]
        both = sum(widths)
        operands += [*lowers, *uppers]
        scratch += [pltpu.VMEM((group, held_all, width), LOW) for width in widths]
        scratch += [
            pltpu.VMEM((group, 2 * half, both), LOW),
            pltpu.VMEM((group, half, both), LOW),
            pltpu.VMEM((group, group_size + 1, 2, rows, both), LOW),
        ]
        results.append(jax.ShapeDtypeStruct((rows, group * 2 * both), F32))
    return pl.pallas_call(
        functools.partial(reduce_kernel, len(after), group_size, all_orders, groups),
        in_specs=[in_any] * len(after) + [in_any, in_any, in_vmem, in_vmem] * len(sets) + [in_vmem],
        out_specs=[in_vmem] * (len(sets) + 1),
        out_shape=results + [jax.ShapeDtypeStruct(vector.shape, F32)],
        scratch_shapes=scratch
        + [
            pltpu.VMEM((bits + 1,) + vector.shape, F32),
            pltpu.VMEM((bits + group_size,) + vector.shape, F32),
            dma((units, 2, most)), dma((units, 2, most)),
            dma((units,)), dma((units,)),
            dma((units, group_size + 1, 2)), dma((units, group_size + 1, 2)),
            dma((bits + group_size,)), dma((bits + group_size,)),
        ],
        cost_estimate=estimate(1, 1),
        compiler_params=pltpu.CompilerParams(
            collective_id=collective_id, has_side_effects=True, vmem_limit_bytes=VMEM_LIMIT
        ),
    )(*after, *operands, vector)


def local(
    tokens,
    cotangent,
    lengths,
    pad_mask,
    mixer_gain,
    query_weight,
    key_weight,
    value_weight,
    conv_query,
    conv_key,
    conv_value,
    beta_weight,
    beta_bias,
    head_gain,
    out_weight,
    feed_gain,
    gate_weight,
    up_weight,
    down_weight,
):
    row_count, model_width = tokens.shape
    head_count = beta_bias.shape[0]
    head_width = head_gain.shape[0]
    tap_count = conv_query.shape[1]
    hidden_units = gate_weight.shape[1]
    my_core = lax.rem(lax.axis_index("seq"), 2)
    chip = chip_bits()
    chip_orders = (list(reversed(chip)), list(chip))
    plain_orders = [order + [1] for order in chip_orders]
    plain_masks = [masks_of(order) for order in plain_orders]
    pair_masks = [masks_of([1] + order) for order in chip_orders]

    def along_groups(shard):
        return lax.all_gather(shard, "grp", axis=0, tiled=True)

    small_shard = jnp.concatenate(
        [mixer_gain[:, None], feed_gain[:, None], conv_query, conv_key, conv_value, beta_weight],
        axis=1,
    )
    small_width = small_shard.shape[1]
    padded_small = jnp.pad(small_shard, ((0, 0), (0, -small_width % 128)))
    plain_shard = jnp.concatenate(
        [query_weight, key_weight, value_weight, out_weight, padded_small], axis=1
    )
    plain_cut = 2 * model_width
    plain_cuts = (pl.ds(0, plain_cut), pl.ds(plain_cut, plain_shard.shape[1] - plain_cut))
    unit_width = hidden_units // 2
    tile = tile_of(unit_width, 256)
    tiles = unit_width // tile
    early_tiles = -(-tiles // 2)
    rest = tiles - early_tiles
    counts = [-(-early_tiles // 2), early_tiles // 2, -(-rest // 2), rest // 2]
    edges = [sum(counts[:place]) * tile for place in range(5)]
    spans = list(zip(edges[:-1], edges[1:]))
    feed_shards = (gate_weight, up_weight, down_weight)

    def units_of(core, start, stop):
        return [
            lax.dynamic_slice_in_dim(shard, core * unit_width + start, stop - start, 1)
            for shard in feed_shards
        ]

    feed_shard = jnp.concatenate(
        [
            part
            for core in (my_core, 1 - my_core)
            for start, stop in spans[:2]
            for part in units_of(core, start, stop)
        ],
        axis=1,
    )
    widths = [3 * (stop - start) for start, stop in spans]
    feed_cuts = (
        pl.ds(0, widths[0]),
        pl.ds(widths[0], widths[1]),
        pl.ds(widths[0] + widths[1], widths[0] + widths[1]),
    )
    tokens_before = jnp.concatenate(
        [
            jnp.zeros((HALO - (tap_count - 1), model_width), tokens.dtype),
            passed_along(tokens[row_count - (tap_count - 1) :], ("seq", "grp"), 1),
        ],
        axis=0,
    )
    full, pair_first, pair_second, _ = gather_call(
        plain_shard, feed_shard, plain_cuts, feed_cuts, plain_orders, 2
    )
    w_qkv, w_out = full[:, : 3 * model_width], full[:, 3 * model_width : 4 * model_width]
    small = columns(full, 4 * model_width, 128)
    gain_mixer, gain_feed = small[:, 0], small[:, 1]
    c_query = small[:, 2 : 2 + tap_count]
    c_key = small[:, 2 + tap_count : 2 + 2 * tap_count]
    c_value = small[:, 2 + 2 * tap_count : 2 + 3 * tap_count]
    w_beta = small[:, 2 + 3 * tap_count : small_width]

    feed_blocks = [
        along_groups(
            tied(
                jnp.concatenate(
                    [part for start, stop in spans[2:] for part in units_of(core, start, stop)],
                    axis=1,
                ),
                full,
            )
        )
        for core in (1 - my_core, my_core)
    ]
    theirs_block = swapped(feed_blocks[0], 1)
    feed_pieces = [
        spread_views(pair_first, chip_orders[0], True),
        spread_views(pair_second, chip_orders[1], True),
    ]
    out_half = model_width // 2
    qkv_half = 3 * model_width // 2

    anchor = lax.axis_index(("seq", "grp")) * row_count
    places = anchor + jnp.arange(row_count, dtype=jnp.int32)
    starts = jnp.cumsum(lengths) - lengths
    row_start = jnp.max(jnp.where(starts[None, :] <= places[:, None], starts[None, :], 0), axis=1)
    valid = [
        (places - offset >= row_start).astype(jnp.float32) for offset in range(1, tap_count)
    ]
    live_rows = pad_mask.astype(jnp.float32)
    inputs32 = tokens.astype(jnp.float32)
    normed_a, norm_a_back = jax.vjp(rms_scale, inputs32, gain_mixer.astype(jnp.float32))
    normed_low = normed_a.astype(jnp.bfloat16)
    normed_before = rms_scale(tokens_before.astype(F32), gain_mixer.astype(F32)).astype(LOW)
    extended = jnp.dot(
        jnp.concatenate([normed_before, normed_low], axis=0), w_qkv, preferred_element_type=F32
    ).astype(LOW)
    logit_part = jnp.dot(normed_low, w_beta, preferred_element_type=jnp.float32)
    sigmoid_val = jax.nn.sigmoid(logit_part + beta_bias)
    beta_rows = sigmoid_val * live_rows[:, None]
    taps = jnp.pad(
        jnp.transpose(jnp.concatenate([c_query, c_key, c_value], axis=0).astype(jnp.float32)),
        ((0, 8 - tap_count), (0, 0)),
    )
    flags = jnp.stack(
        [
            (row_start < anchor).astype(jnp.float32),
            (row_start == row_start[-1]).astype(jnp.float32),
            live_rows,
        ]
        + valid,
        axis=1,
    )
    inverse, wy, scores, reach, local_out, pairs = span_call(
        row_start,
        flags,
        beta_rows,
        extended,
        taps,
        tap_count,
        head_count,
        after=(feed_pieces[0][1][0], feed_pieces[1][1][0]),
    )
    ready = (pairs, feed_pieces[0][-1][0], feed_pieces[1][-1][0])
    edge = 0
    for place, width in enumerate(widths[2:]):
        paired = join_columns(feed_blocks[1], theirs_block, edge, width, ready)
        feed_pieces.append(spread_views(paired, chip_orders[place], False))
        edge = edge + width
    start_states = scan_call(pairs, False, 0)
    mixed, head_low = mixed_call(
        reach,
        local_out,
        start_states,
        head_gain,
        flags,
        after=tuple(feed_pieces[place][at][0] for place in (2, 3) for at in (1, 2)),
    )
    hidden_one = inputs32 + jnp.dot(head_low, w_out, preferred_element_type=F32)
    normed_f, norm_f_back = jax.vjp(rms_scale, hidden_one, gain_feed.astype(jnp.float32))
    feed_low = normed_f.astype(jnp.bfloat16)
    depth = model_width // len(feed_pieces[0])
    second_places = [pair_masks[1][::2].index(mask) for mask in pair_masks[0][::2]]
    first_places = [pair_masks[0][::2].index(mask) for mask in pair_masks[1][::2]]
    chip_count = len(feed_pieces[0])
    half_places = [
        [list(range(chip_count // 2)), list(range(chip_count // 2, chip_count))],
        [first_places[: chip_count // 2], first_places[chip_count // 2 :]],
    ]
    rows = (feed_low, swapped(feed_low, 1), cotangent, swapped(cotangent, 1))
    chip_masks = [mask // 2 for mask in pair_masks[0][::2]]
    before = None
    feed_grads, lower_halves = [], []

    def feed_lower(chunk, after):
        lowers = []
        for part in range(2):
            grads = feed_grads[2 * chunk + part]
            lowers.append(
                outer_call(sources, grads, half_places[part][1], after=(*after, *lowers))
            )
        return lowers

    def feed_sent(chunk, lowers):
        return [swapped(lower, chip_orders[part][-1]) for part, lower in enumerate(lowers)]

    for chunk in range(2):
        grads_first, grads_second, *results = feed_call(
            rows,
            [
                feed_pieces[2 * chunk],
                [feed_pieces[2 * chunk + 1][place] for place in second_places],
            ],
            before,
            chip_masks,
            tile,
            after=lower_halves,
        )
        if chunk == 0:
            rows, before = results[:2], results[2:]
            sources = rows
        feed_grads += [grads_first, grads_second]
        if chunk == 0:
            lower_halves = feed_lower(0, ())
            sent = feed_sent(0, lower_halves)
    out_own, out_other, d_own, d_other = results
    d_feed = d_own + swapped(d_other, 1)
    block_out = (hidden_one + (out_own + swapped(out_other, 1))).astype(jnp.bfloat16)
    grad_out = cotangent.astype(jnp.float32)
    d_hidden_part, d_gain_feed = norm_f_back(d_feed)
    d_hidden = grad_out + d_hidden_part
    d_attn = d_hidden.astype(jnp.bfloat16)
    d_head = contract_rows(
        d_attn, full, 3 * model_width, after=lower_halves
    )

    def feed_upper(place, arrived, after):
        return outer_call(
            sources,
            feed_grads[place],
            half_places[place % 2][0],
            None,
            (arrived,),
            (0,),
            after,
            2,
        )

    def chip_sum(halves, part, after):
        bits = list(reversed(chip_orders[part][:-1]))
        for place, bit in enumerate(bits):
            total = halved_sum(*halves, bit, after)
            middle = total.shape[0] // 2
            if place + 1 < len(bits):
                halves = (total[:middle], total[middle:])
        return total

    def both_owners(totals):
        half = totals[0].shape[0] // 2
        mine = [total[:half] for total in totals]
        theirs = [swapped(total[half:], 1) for total in totals]
        return jnp.concatenate(mine + theirs, axis=1)

    def both_halves(grads):
        width = grads.shape[1] // 2
        mine = lax.dynamic_slice_in_dim(grads, my_core * width, width, 1)
        theirs = lax.dynamic_slice_in_dim(grads, (1 - my_core) * width, width, 1)
        return jnp.concatenate([mine, swapped(theirs, 1)], axis=0)

    d_mixed, d_head_gain, back_pairs = pull_call(
        reach, mixed, d_head, head_gain, flags, pairs
    )
    end_states = scan_call(back_pairs, True, 1)
    upper_first = [feed_upper(place, sent[place], (end_states,)) for place in range(2)]
    both_attn = both_halves(d_attn)
    plain_sources = [
        relative(jnp.concatenate([rows, swapped(rows, 1)], axis=0), pair_masks[0])
        for rows in (normed_low, head_low)
    ]
    d_rows, d_tail, d_before, d_taps, d_betas = back_call(
        row_start,
        flags,
        beta_rows,
        extended,
        taps,
        tap_count,
        inverse,
        wy,
        scores,
        start_states,
        end_states,
        d_mixed,
        after=[half for halves in upper_first for half in halves],
    )
    d_logit32 = d_betas * live_rows[:, None] * sigmoid_val * (1.0 - sigmoid_val)
    d_logit = d_logit32.astype(jnp.bfloat16)
    lower_second = feed_lower(1, (d_betas,))
    sent_second = feed_sent(1, lower_second)
    chip_first = [
        chip_sum(total, part, lower_second) for part, total in enumerate(upper_first)
    ]
    early_rows = both_owners(chip_first)
    from_next = passed_along(
        d_before[:, 9 - tap_count :].astype(jnp.bfloat16), ("seq", "grp"), -1
    ).astype(jnp.float32)
    fixed = d_tail.at[:, 9 - tap_count :].add(from_next).astype(LOW)
    d_pre = jnp.concatenate(
        [
            jnp.concatenate([d_rows[kind, : row_count - 8], fixed[kind]], axis=0)
            for kind in range(3)
        ],
        axis=1,
    )
    d_kernel = jnp.concatenate(
        [jnp.transpose(d_taps[kind, :tap_count]) for kind in range(3)], axis=0
    )
    both_pre = both_halves(d_pre)
    fine = model_width // 4

    def plain_grads(part):
        kinds = [
            both_pre[:, (3 * part + kind) * fine : (3 * part + kind + 1) * fine]
            for kind in range(3)
        ]
        return jnp.stack(kinds + [both_attn[:, part * fine : (part + 1) * fine]])

    plain_slopes = [plain_grads(part) for part in range(2)]
    plain_lower = [
        outer_call(plain_sources, plain_slopes[part], half_places[part][1], after=chip_first)
        for part in range(2)
    ]
    plain_upper = [
        outer_call(plain_sources, plain_slopes[part], half_places[part][0], after=plain_lower)
        for part in range(2)
    ]
    d_normed = contract(d_logit, w_beta) + contract_rows(
        d_pre, full, 0, after=(*plain_upper, early_rows)
    )
    upper_second = [
        feed_upper(2 + part, sent_second[part], (d_normed,)) for part in range(2)
    ]
    feed_early = over_groups(early_rows)
    d_input_part, d_gain_mixer = norm_a_back(d_normed)
    input_grad = (d_hidden + d_input_part).astype(jnp.bfloat16)
    small_grads = jnp.concatenate(
        [
            lax.dot_general(
                normed_low, d_logit, (((0,), (0,)), ((), ())), preferred_element_type=F32
            ),
            d_kernel[:model_width],
            d_kernel[model_width : 2 * model_width],
            d_kernel[2 * model_width :],
            d_gain_mixer[:, None],
            d_gain_feed[:, None],
        ],
        axis=1,
    )
    small_both = jnp.pad(
        jnp.where(my_core == 0, small_grads + swapped(small_grads, 1), 0.0).astype(LOW),
        ((0, 0), (0, 128 - small_grads.shape[1])),
    )
    block_rows = model_width // lax.axis_size("seq")
    small_blocks = [
        lax.dynamic_slice_in_dim(
            small_both, (lax.axis_index("seq") ^ mask) * block_rows, block_rows, 0
        )
        for mask in pair_masks[0]
    ]
    half_blocks = len(small_blocks) // 2
    small_upper = jnp.concatenate(small_blocks[:half_blocks], axis=0)
    small_lower = jnp.concatenate(small_blocks[half_blocks:], axis=0)
    vector = jnp.concatenate([d_head_gain[0], jnp.sum(d_logit32, axis=0)])
    padded = jnp.zeros((8, 256), F32).at[0, : vector.shape[0]].set(vector)
    rest_orders = [order[:-1] for order in chip_orders]
    small_sum, feed_late, plain_sum, everywhere = reduce_call(
        [
            ((small_lower, small_lower), (small_upper, small_upper), 1, chip_orders),
            (
                [lower for _, lower in upper_second],
                [upper for upper, _ in upper_second],
                6,
                rest_orders,
            ),
            (plain_lower, plain_upper, 16, chip_orders),
        ],
        padded,
        3,
    )
    replicated = everywhere[0, : vector.shape[0]]

    def in_order(mine, other):
        return jnp.concatenate(
            [jnp.where(my_core == 0, mine, other), jnp.where(my_core == 0, other, mine)], axis=1
        )

    fine = fine // 4
    groups = [plain_sum[:, at * fine : (at + 1) * fine] for at in range(64)]
    qkv_grad, out_grad = [
        in_order(
            *[
                jnp.concatenate(
                    [
                        groups[4 * group + 2 * owner + part]
                        for part in range(2)
                        for group in range(*span)
                    ],
                    axis=1,
                )
                for owner in range(2)
            ]
        )
        for span in ((0, 12), (12, 16))
    ]
    feed_sums = []
    for kind in range(3):
        halves = []
        for owner in range(2):
            at = owner * feed_early.shape[1] // 2
            for start, stop in spans[:2]:
                width = stop - start
                halves.append(feed_early[:, at + kind * width : at + (kind + 1) * width])
                at = at + 3 * width
            late = [(stop - start) // 2 for start, stop in spans[2:]]
            for part in range(2):
                for group in (2 * kind, 2 * kind + 1):
                    at = (2 * group + owner) * sum(late) + part * late[0]
                    halves.append(feed_late[:, at : at + late[part]])
        feed_sums.append(
            in_order(jnp.concatenate(halves[:6], axis=1), jnp.concatenate(halves[6:], axis=1))
        )
    gate_grad, up_grad, down_grad = feed_sums
    sharded = jnp.where(my_core == 0, small_sum[:, :128], small_sum[:, 256:384])
    taps_at = head_count + 3 * tap_count
    return (
        block_out,
        input_grad,
        sharded[:, taps_at],
        qkv_grad[:, :model_width],
        qkv_grad[:, model_width : 2 * model_width],
        qkv_grad[:, 2 * model_width :],
        sharded[:, head_count : head_count + tap_count],
        sharded[:, head_count + tap_count : head_count + 2 * tap_count],
        sharded[:, head_count + 2 * tap_count : taps_at],
        sharded[:, :head_count],
        replicated[head_width:],
        replicated[:head_width],
        out_grad,
        sharded[:, taps_at + 1],
        gate_grad,
        up_grad,
        down_grad,
    )


def solution(mesh):
    placed = (
        P(("seq", "grp"), None),
        P(("seq", "grp"), None),
        P(),
        P(("seq", "grp")),
        P(("seq", "grp")),
        P(("seq", "grp"), None),
        P(("seq", "grp"), None),
        P(("seq", "grp"), None),
        P(("seq", "grp"), None),
        P(("seq", "grp"), None),
        P(("seq", "grp"), None),
        P(("seq", "grp"), None),
        P(),
        P(),
        P(("seq", "grp"), None),
        P(("seq", "grp")),
        P(("seq", "grp"), None),
        P(("seq", "grp"), None),
        P(("seq", "grp"), None),
    )
    return jax.shard_map(
        local,
        mesh=mesh,
        in_specs=placed,
        out_specs=(
            P(("seq", "grp"), None),
            P(("seq", "grp"), None),
            P(("seq", "grp")),
            P(("seq", "grp"), None),
            P(("seq", "grp"), None),
            P(("seq", "grp"), None),
            P(("seq", "grp"), None),
            P(("seq", "grp"), None),
            P(("seq", "grp"), None),
            P(("seq", "grp"), None),
            P(),
            P(),
            P(("seq", "grp"), None),
            P(("seq", "grp")),
            P(("seq", "grp"), None),
            P(("seq", "grp"), None),
            P(("seq", "grp"), None),
        ),
        check_vma=False,
    )
```
